32 devices in a mesh: grp: 8 (over z, x), exp: 4 (over y, core).
Axes of the slice: x: 2, y: 2, z: 4, core: 2. Of those that a mesh axis runs over, the one named last changes fastest.
Arguments:
- layer_input: bfloat16 [4096, 2048], P(('grp', 'exp')), may hold values from -6 to 6
- out_grad: bfloat16 [4096, 2048], P(('grp', 'exp')), may hold values from -6 to 6
- doc_lengths: int32 [8, 2], P('grp'), may hold values from 64 to 448, as said below
- block_order: int32 [8, 8], P('grp'), may hold values from 0 to 7, as said below
- attn_route: int32 [4096, 2], P('grp'), may hold values from 0 to 3, all different within a row; in each aligned block of 128 rows (0 to 127, 128 to 255, ...) at most 96 rows name the same one
- ffn_route: int32 [4096, 2], P('grp'), may hold values from 0 to 3, all different within a row; in each aligned block of 128 rows (0 to 127, 128 to 255, ...) at most 96 rows name the same one
- norm_gains: float32 [2048, 2], P(('grp', 'exp')), may hold values from 0.5 to 1.5
- kv_master: float32 [2048, 4096], P(('grp', 'exp')), may hold values from -0.125 to 0.125
- router_master: float32 [2048, 8], P(('grp', 'exp')), may hold values from -0.09375 to 0.09375
- query_master: float32 [4, 2048, 2048], P('exp', 'grp'), may hold values from -0.125 to 0.125
- output_master: float32 [4, 2048, 2048], P('exp', 'grp'), may hold values from -1 to 1
- gate_up_master: float32 [4, 5632, 2, 2048], P('exp', 'grp'), may hold values from -0.125 to 0.125
- down_master: float32 [4, 5632, 2048], P('exp', 'grp'), may hold values from -0.109375 to 0.109375
Outputs:
- layer_output: bfloat16 [4096, 2048], P(('grp', 'exp'))
- input_grad: float32 [4096, 2048], P(('grp', 'exp'))
- gain_grad: float32 [2048, 2], P(('grp', 'exp'))
- kv_grad: float32 [2048, 4096], P(('grp', 'exp'))
- router_grad: float32 [2048, 8], P(('grp', 'exp'))
- query_grad: float32 [4, 2048, 2048], P('exp', 'grp')
- output_grad: float32 [4, 2048, 2048], P('exp', 'grp')
- gate_up_grad: float32 [4, 5632, 2, 2048], P('exp', 'grp')
- down_grad: float32 [4, 5632, 2048], P('exp', 'grp')
The draws below stay inside these ranges and needn't reach their ends.
Inputs may be any that keep to these rules, and one draw needn't show every extreme that they name: `doc_lengths`: each row: the lengths of the group's two documents in stream order, summing to 512. In every draw some group has one document of exactly 64 tokens and one of 448. `block_order`: each row names every block once; the two dealt blocks of one device are b and 7 - b. `attn_route`: A row names two different experts. Among the 128 rows of one device no expert is named by more than 96 rows, a bound that some block reaches. `ffn_route`: A row names two different experts. Among the 128 rows of one device no expert is named by more than 96 rows, a bound that some block reaches.
All inputs are finite; a program needn't handle non-finite values.
Results may differ from the reference program's by a relative error of at most 0.02.
Values may be sent and summed in bfloat16 or wider, within the bound.
A program may use at most 384 MiB of HBM per device.

```python
import math
import jax
import jax.numpy as jnp
import numpy as np
from jax import lax

D = 2048
HEADS = 16
HD = 128
FF = 5632
E = 4
TOK_DEV = 128
BLOCK = 64
TOK_GRP = 512
TOKENS = 4096
NBLK = 8
CAP = 96
N_GRP = 8


def shuffled(single):
    return jax.random.permutation(single, NBLK // 2)


def draw_block_order(key, part):
    key = jax.random.fold_in(key, 7)
    keys = jax.random.split(key, N_GRP)
    picks = jax.vmap(shuffled)(keys).astype(jnp.int32)
    paired = jnp.stack([picks, NBLK - 1 - picks], axis=2)
    return paired.reshape(N_GRP, NBLK).astype(jnp.int32)


def draw_doc_lengths(key, part):
    key = jax.random.fold_in(key, 11)
    key_len, key_group, key_side = jax.random.split(key, 3)
    shortest = TOK_GRP // 8
    longest = TOK_GRP - shortest
    first = jax.random.randint(key_len, (N_GRP,), shortest, longest + 1).astype(jnp.int32)
    chosen_group = jax.random.randint(key_group, (), 0, N_GRP).astype(jnp.int32)
    side = jax.random.randint(key_side, (), 0, 2).astype(jnp.int32)
    forced = shortest + side * (longest - shortest)
    first = jnp.where(jnp.arange(N_GRP, dtype=jnp.int32) == chosen_group, forced, first).astype(jnp.int32)
    return jnp.stack([first, TOK_GRP - first], axis=1).astype(jnp.int32)


def steps_of(key, extent, cuts, low, largest):
    factor_of, own = 1.0, jax.random.fold_in(key, 6)
    for axis_at, parts in cuts:
        steps = jnp.exp(jax.random.uniform(jax.random.fold_in(own, axis_at), (parts,), jnp.float32, low / len(cuts), largest / len(cuts)))
        factor_of = factor_of * jnp.repeat(steps, extent[axis_at] // parts).reshape([-1 if axis == axis_at else 1 for axis in range(len(extent))])
    return factor_of


def routed_block(own_key, own, number, rows, count, top, reach, lean):
    order = jax.random.permutation(own_key, count)
    heavy_load, common = shares(count, rows * top, reach, lean, True), shares(count, rows * top, reach, lean, False)
    places = jnp.arange(count)

    def named(sizes, offset_by):
        used = int((sizes > 0).sum())
        fixed = max(1, used // 4)
        shifted = fixed + (places - fixed + offset_by * (used - fixed)) % max(1, count - fixed)
        return jnp.zeros((count,), jnp.int32).at[order[jnp.where(places < fixed, places, shifted)]].set(jnp.asarray(sizes, jnp.int32))

    sizes = jnp.where(number % 4 == 0, named(heavy_load, number // 4), named(common, number - number // 4 - 1))
    mixed = jax.random.permutation(jax.random.fold_in(own, 3), count)
    donor, sink = mixed[0:count // 2 * 2:2], mixed[1:count // 2 * 2:2]
    margin = jnp.minimum(sizes[donor] - 1, reach - sizes[sink]) // 2
    margin = jnp.where((donor == order[0]) | (sink == order[0]) | (sizes[sink] == 0), 0, jnp.maximum(margin, 0))
    shifted = jax.random.randint(jax.random.fold_in(own, 4), (count // 2,), 0, 1 << 20) % (margin + 1)
    sizes = sizes.at[donor].add(-shifted).at[sink].add(shifted)
    labels = jnp.searchsorted(jnp.cumsum(sizes), jnp.arange(rows * top), side="right").astype(jnp.int32)
    listing = labels.reshape(top, rows).T
    listing = listing[jax.random.permutation(jax.random.fold_in(own, 1), rows)]
    offset_by = jax.random.randint(jax.random.fold_in(own, 2), (rows, 1), 0, top)
    return jnp.take_along_axis(listing, (jnp.arange(top)[None, :] + offset_by) % top, axis=1)


def shares(count, total, most, slope, full):
    portions = [(1 << 20) // math.isqrt(grade ** slope) + 1 for grade in range(1, count + 1)]
    largest = most if full else min(most, max(-(-total // count), total * portions[0] // sum(portions)))
    least = 1 if total - largest >= count - 1 else 0
    counts, spare = [largest] + [least] * (count - 1), total - largest - least * (count - 1)
    while spare > 0:
        free = [i for i in range(1, count) if counts[i] < largest] or [i for i in range(1, count) if counts[i] < most]
        pool, left = sum([portions[i] for i in free]), spare
        for i in free:
            extra = min(most - counts[i], max(1, left * portions[i] // pool), spare)
            counts[i] = counts[i] + extra
            spare = spare - extra
    return np.array(counts)


def gaussian(rng, shape, scale, limit, cuts=(), kind=jnp.bfloat16):
    drawn = jax.random.normal(rng, shape, jnp.float32) * scale
    if len(cuts) > 0:
        drawn = steps_of(rng, shape, cuts, -0.22, 0.18) * drawn
    return jnp.clip(drawn, min=-limit, max=limit).astype(kind)


def setup_inputs(seed: int = 0) -> dict:
    seeds = jax.random.split(jax.random.key(seed), 14)
    layer_input = gaussian(seeds[0], (TOKENS, D), 1.0, 6.0, ((0, 32),))
    out_grad = gaussian(seeds[1], (TOKENS, D), 1.0, 6.0, ((0, 32),))
    doc_lengths = draw_doc_lengths(jax.random.fold_in(seeds[13], 71), 0)
    block_order = draw_block_order(jax.random.fold_in(seeds[13], 71), 0)
    attn_route_keys = jax.random.split(jax.random.fold_in(seeds[4], 1), TOKENS // TOK_DEV)
    attn_route_turns = jax.random.permutation(jax.random.fold_in(seeds[4], 3), TOKENS // TOK_DEV)
    attn_route = jax.vmap(lambda own, number: routed_block(jax.random.fold_in(seeds[4], 2), own, number, TOK_DEV, E, 2, CAP, 2))(attn_route_keys, attn_route_turns).reshape((TOKENS, 2))
    ffn_route_keys = jax.random.split(jax.random.fold_in(seeds[5], 1), TOKENS // TOK_DEV)
    ffn_route_turns = jax.random.permutation(jax.random.fold_in(seeds[5], 3), TOKENS // TOK_DEV)
    ffn_route = jax.vmap(lambda own, number: routed_block(jax.random.fold_in(seeds[5], 2), own, number, TOK_DEV, E, 2, CAP, 2))(ffn_route_keys, ffn_route_turns).reshape((TOKENS, 2))
    norm_gains = jnp.clip(1.0 + 0.1 * jax.random.normal(seeds[6], (D, 2), jnp.float32), 0.5, 1.5)
    kv_master = gaussian(seeds[7], (D, 2 * D), D ** -0.5, 0.125, ((0, 32),), jnp.float32)
    router_master = gaussian(seeds[8], (D, 2 * E), (2 * D) ** -0.5, 0.09375, ((0, 32),), jnp.float32)
    query_master = gaussian(seeds[9], (E, D, D), D ** -0.5, 0.125, ((0, 4), (1, 8)), jnp.float32)
    output_master = gaussian(seeds[10], (E, D, D), (D // 64) ** -0.5, 1.0, ((0, 4), (1, 8)), jnp.float32)
    gate_up_master = gaussian(seeds[11], (E, FF, 2, D), D ** -0.5, 0.125, ((0, 4), (1, 8)), jnp.float32)
    down_master = gaussian(seeds[12], (E, FF, D), (FF // 2) ** -0.5, 0.109375, ((0, 4), (1, 8)), jnp.float32)
    return {"layer_input": layer_input, "out_grad": out_grad, "doc_lengths": doc_lengths, "block_order": block_order, "attn_route": attn_route, "ffn_route": ffn_route, "norm_gains": norm_gains, "kv_master": kv_master, "router_master": router_master, "query_master": query_master, "output_master": output_master, "gate_up_master": gate_up_master, "down_master": down_master}


epsilon = 1e-05
negative = -1e+30
highest = lax.Precision.HIGHEST

@jax.custom_vjp
def low(v):
    return lax.optimization_barrier(v.astype(jnp.bfloat16)).astype(jnp.float32)

@jax.custom_vjp
def low_back(v):
    return v

def low_keep(v):
    return (low(v), None)

def low_pass(kept, grad):
    return (grad,)

def back_keep(v):
    return (v, None)

def back_low(kept, grad):
    return (low(grad),)
low.defvjp(low_keep, low_pass)
low_back.defvjp(back_keep, back_low)

def product(left, right):
    return jnp.dot(left, right, precision=highest, preferred_element_type=jnp.float32)

def rotate(values, positions, sign):
    count = values.shape[0]
    half = HD // 2
    split = values.reshape(count, HEADS, HD)
    freq = jnp.exp(jnp.arange(half, dtype=jnp.float32) * (-2.0 * math.log(10000.0) / HD))
    angle = positions.astype(jnp.float32)[:, None] * freq[None, :]
    cosine = jnp.cos(angle)[:, None, :]
    sine = sign * jnp.sin(angle)[:, None, :]
    first = split[:, :, :half]
    second = split[:, :, half:]
    turned = jnp.concatenate([first * cosine - second * sine, second * cosine + first * sine], axis=2)
    return turned.reshape(count, HEADS * HD)

def layout(lengths, order):
    places = jnp.arange(TOK_GRP, dtype=jnp.int32)
    anchor = order[places // BLOCK] * BLOCK + places % BLOCK
    first = lengths[0]
    doc = (anchor >= first).astype(jnp.int32)
    return (anchor, doc, anchor - doc * first)

def rms(values):
    return values * lax.rsqrt(lax.optimization_barrier(jnp.mean(values * values, axis=1, keepdims=True)) + epsilon)

def gating(logits, picks):
    chosen = (picks[:, :, None] == jnp.arange(E, dtype=jnp.int32)[None, None, :]).astype(jnp.float32)
    picked = lax.optimization_barrier(jnp.sum(chosen * logits[:, None, :], axis=2))
    return (jax.nn.softmax(picked, axis=1), chosen)

def attention(query, keys, values, allowed):
    count = query.shape[0]
    query_heads = query.reshape(count, HEADS, HD)
    key_heads = keys.reshape(count, HEADS, HD)
    value_heads = values.reshape(count, HEADS, HD)
    scores = jnp.einsum('qhd,khd->hqk', query_heads, key_heads, precision=highest) * (1.0 / math.sqrt(HD))
    scores = low_back(scores)
    scores = jnp.where(allowed[None], scores, negative)
    weights = low(jax.nn.softmax(scores, axis=2))
    attended = jnp.einsum('hqk,khd->qhd', weights, value_heads, precision=highest)
    return attended.reshape(count, HEADS * HD)

def group_forward(inputs, lengths, order, attn_pick, ffn_pick, weights):
    gains, kv_weight, route_weight, query_weight, output_weight, gate_up, down = weights
    anchor, doc, place = layout(lengths, order)
    hidden_one = low(rms(inputs) * gains[:, 0])
    projected = low_back(product(hidden_one, kv_weight))
    keys = low(rotate(projected[:, :D], place, 1.0))
    values = low(projected[:, D:])
    attn_gates, attn_chosen = gating(product(hidden_one, route_weight[:, :E]), attn_pick)
    sent_zero = low_back(hidden_one)
    sent_one = low_back(hidden_one)
    allowed = (doc[:, None] == doc[None, :]) & (anchor[None, :] <= anchor[:, None])

    def attn_expert(total, item):
        index, query_w, output_w = item
        pick = lax.dynamic_index_in_dim(attn_chosen, index, 2, keepdims=False)
        routed = pick[:, 0:1] * sent_zero + pick[:, 1:2] * sent_one
        query = low(rotate(low_back(product(routed, query_w)), place, 1.0))
        attended = low(low_back(attention(query, keys, values, allowed)))
        mapped = low(low_back(product(attended, output_w)))
        weight = lax.optimization_barrier(jnp.sum(pick * attn_gates, axis=1, keepdims=True))
        return (total + weight * mapped, None)
    attn_total, _ = lax.scan(attn_expert, jnp.zeros_like(inputs), (jnp.arange(E, dtype=jnp.int32), query_weight, output_weight))
    middle = inputs + attn_total
    hidden_two = low(rms(middle) * gains[:, 1])
    ffn_gates, ffn_chosen = gating(product(hidden_two, route_weight[:, E:]), ffn_pick)
    second_zero = low_back(hidden_two)
    second_one = low_back(hidden_two)

    def ffn_expert(total, item):
        index, pair_w, down_w = item
        pick = lax.dynamic_index_in_dim(ffn_chosen, index, 2, keepdims=False)
        routed = pick[:, 0:1] * second_zero + pick[:, 1:2] * second_one
        gate = low_back(product(routed, pair_w[:, 0, :].T))
        up = low_back(product(routed, pair_w[:, 1, :].T))
        act = low(jax.nn.silu(gate) * up)
        produced = low(low_back(product(act, down_w)))
        weight = lax.optimization_barrier(jnp.sum(pick * ffn_gates, axis=1, keepdims=True))
        return (total + weight * produced, None)
    ffn_total, _ = lax.scan(ffn_expert, jnp.zeros_like(inputs), (jnp.arange(E, dtype=jnp.int32), gate_up, down))
    return middle + ffn_total

def reference(layer_input, out_grad, doc_lengths, block_order, attn_route, ffn_route, norm_gains, kv_master, router_master, query_master, output_master, gate_up_master, down_master):
    group_items = (doc_lengths, block_order, attn_route.reshape(N_GRP, TOK_GRP, 2), ffn_route.reshape(N_GRP, TOK_GRP, 2))

    def forward(inputs, gain_full, kv_full, router_full, query_full, output_full, pair_full, down_full):
        weights = (low(gain_full), low(kv_full), low(router_full), low(query_full), low(output_full), low(pair_full), low(down_full))

        def grouped(rows_in, lengths, order, attn_pick, ffn_pick):
            return group_forward(rows_in, lengths, order, attn_pick, ffn_pick, weights)
        saved_group = jax.checkpoint(grouped)

        def step(carry, items):
            return (carry, saved_group(*items))
        _, outputs = lax.scan(step, (), (inputs.reshape(N_GRP, TOK_GRP, D),) + group_items)
        return outputs.reshape(TOKENS, D)
    result, pull = jax.vjp(forward, layer_input.astype(jnp.float32), norm_gains, kv_master, router_master, query_master, output_master, gate_up_master, down_master)
    grads = pull(out_grad.astype(jnp.float32))
    return (result.astype(jnp.bfloat16), grads[0], grads[1], grads[2], grads[3], grads[4], grads[5], grads[6], grads[7])
```

```python
import functools
import math

import jax
import jax.numpy as jnp
from jax import lax
from jax.experimental import pallas as pl
from jax.experimental.pallas import tpu as pltpu
from jax.sharding import PartitionSpec as P

HEADS = 16
LANES = 128
MESH = pl.DeviceIdType.MESH
MB = 1024 * 1024

epsilon = 1e-05
negative = -1e30
highest = lax.Precision.HIGHEST
f32 = jnp.float32
bf16 = jnp.bfloat16


def nn(a, b):
    return jnp.dot(a, b, preferred_element_type=f32)


def nt(a, b):
    return lax.dot_general(a, b, (((1,), (1,)), ((), ())), preferred_element_type=f32)


def tn(a, b):
    return lax.dot_general(a, b, (((0,), (0,)), ((), ())), preferred_element_type=f32)


def loop(count, step):
    def run(i, carry):
        step(i)
        return carry

    lax.fori_loop(0, count, run, 0)


def rows_at(i, size):
    return pl.ds(pl.multiple_of(i * size, size), size)


def turn(v, cos, sin):
    return v * cos + pltpu.roll(v, LANES // 2, 1) * sin


def gate_columns(logits, r0, r1, me):
    lane = lax.broadcasted_iota(jnp.int32, logits.shape, 1)
    l0 = jnp.sum(jnp.where(lane == r0, logits, 0.0), axis=1, keepdims=True)
    l1 = jnp.sum(jnp.where(lane == r1, logits, 0.0), axis=1, keepdims=True)
    top = jnp.maximum(l0, l1)
    e0, e1 = jnp.exp(l0 - top), jnp.exp(l1 - top)
    g0, g1 = e0 / (e0 + e1), e1 / (e0 + e1)
    weight = jnp.where(r0 == me, g0, 0.0) + jnp.where(r1 == me, g1, 0.0)
    sign = jnp.where(r0 == me, 1.0, 0.0) - jnp.where(r1 == me, 1.0, 0.0)
    return jnp.where(
        lane == 0,
        weight,
        jnp.where(lane == 1, sign, jnp.where(lane == 2, g0, jnp.where(lane == 3, g1, 0.0))),
    )


def attn_forward_kernel(
    cw, scale, me, tokens, gain, w_all, ow, cos, sin, meta, krow, qkv, att, aux, part, h1, inv
):
    count, width = h1.shape
    heads = cw // LANES
    step_rows = 256

    def normalise(i):
        at = rows_at(i, 64)
        v = tokens[at, :].astype(f32)
        inverse = lax.rsqrt(jnp.mean(v * v, axis=1, keepdims=True) + epsilon)
        inv[at, :] = jnp.broadcast_to(inverse, (64, LANES))
        h1[at, :] = (v * inverse * gain[...]).astype(bf16)

    loop(count // 64, normalise)

    def project(i):
        at = rows_at(i, step_rows)
        y = nn(h1[at, :], w_all[...])
        c, s = cos[at, :], sin[at, :]
        for h in range(2 * heads):
            qkv[at, h * LANES : (h + 1) * LANES] = turn(
                y[:, h * LANES : (h + 1) * LANES], c, s
            ).astype(bf16)
        qkv[at, 2 * cw : 3 * cw] = y[:, 2 * cw : 3 * cw].astype(bf16)
        found = gate_columns(y[:, 3 * cw : 3 * cw + LANES], meta[at, 2:3], meta[at, 3:4], me[0])
        lane = lax.broadcasted_iota(jnp.int32, found.shape, 1)
        aux[at, :] = jnp.where(lane == 4, inv[at, :], found)

    loop(count // step_rows, project)

    for h in range(heads):

        def attend(i, h=h):
            at = rows_at(i, LANES)
            q = qkv[at, h * LANES : (h + 1) * LANES]
            k = qkv[:, cw + h * LANES : cw + (h + 1) * LANES]
            v = qkv[:, 2 * cw + h * LANES : 2 * cw + (h + 1) * LANES]
            ak = krow[0, 0:1, :]
            allowed = (ak <= meta[at, 0:1]) & (ak >= meta[at, 1:2])
            scores = jnp.where(allowed, nt(q, k) * scale, negative)
            top = jnp.max(scores, axis=1, keepdims=True)
            raised = jnp.exp(scores - top)
            total = jnp.sum(raised, axis=1, keepdims=True)
            probs = (raised * (1.0 / total)).astype(bf16)
            att[at, h * LANES : (h + 1) * LANES] = nn(probs, v).astype(bf16)
            old = aux[at, :]
            lane = lax.broadcasted_iota(jnp.int32, old.shape, 1)
            aux[at, :] = jnp.where(lane == 8 + h, top + jnp.log(total), old)

        loop(count // LANES, attend)

    def output(i):
        at = rows_at(i, step_rows)
        scaled = (aux[at, 0:1] * att[at, :].astype(f32)).astype(bf16)
        part[at, :] = nn(scaled, ow[...]).astype(bf16)

    loop(count // step_rows, output)


def attn_backward_kernel(
    cw, scale, dmid, tokens, gain, qkv, att, aux, cos, sin, meta, krow, w_all, ow,
    dh1, dw, do, h1, datt, watt, dqkv, dk_sum, dv_sum,
):
    count, width = h1.shape
    heads = cw // LANES
    step_rows = 256

    @pl.when(pl.program_id(0) == 0)
    def _():
        dw[...] = jnp.zeros_like(dw)
        do[...] = jnp.zeros_like(do)

    def normalise(i):
        at = rows_at(i, 64)
        h1[at, :] = (tokens[at, :].astype(f32) * aux[at, 4:5] * gain[...]).astype(bf16)

    loop(count // 64, normalise)

    def incoming(i):
        at = rows_at(i, step_rows)
        raw = nt(dmid[at, :], ow[...])
        a = att[at, :].astype(f32)
        weight, sign = aux[at, 0:1], aux[at, 1:2]
        share = sign * jnp.sum(raw * a, axis=1, keepdims=True)
        dh1[at, width:] = jnp.broadcast_to(share, (step_rows, LANES)).astype(bf16)
        datt[at, :] = (weight * raw).astype(bf16)
        watt[at, :] = (weight * a).astype(bf16)

    loop(count // step_rows, incoming)

    def out_weight(i):
        at = rows_at(i, 512)
        do[:, at] += tn(watt[...], dmid[:, at])

    loop(width // 512, out_weight)

    for h in range(heads):
        hs = slice(h * LANES, (h + 1) * LANES)
        ks = slice(cw + h * LANES, cw + (h + 1) * LANES)
        vs = slice(2 * cw + h * LANES, 2 * cw + (h + 1) * LANES)
        dk_sum[...] = jnp.zeros_like(dk_sum)
        dv_sum[...] = jnp.zeros_like(dv_sum)

        def back(i, h=h, hs=hs, ks=ks, vs=vs):
            at = rows_at(i, LANES)
            q, k, v = qkv[at, hs], qkv[:, ks], qkv[:, vs]
            ak = krow[0, 0:1, :]
            allowed = (ak <= meta[at, 0:1]) & (ak >= meta[at, 1:2])
            scores = jnp.where(allowed, nt(q, k) * scale, negative)
            probs = jnp.exp(scores - aux[at, 8 + h : 9 + h])
            grad = datt[at, hs]
            dprobs = nt(grad, v)
            inner = jnp.sum(probs * dprobs, axis=1, keepdims=True)
            dscores = (probs * (dprobs - inner)).astype(bf16)
            dqkv[at, hs] = turn(nn(dscores, k) * scale, cos[at, :], -sin[at, :]).astype(bf16)
            dk_sum[...] += tn(dscores, q)
            dv_sum[...] += tn(probs.astype(bf16), grad)

        loop(count // LANES, back)
        dqkv[:, ks] = turn(dk_sum[...] * scale, cos[...], -sin[...]).astype(bf16)
        dqkv[:, vs] = dv_sum[...].astype(bf16)

    def to_hidden(i):
        at = rows_at(i, step_rows)
        dh1[at, :width] = nt(dqkv[at, :], w_all[:, : 3 * cw]).astype(bf16)

    loop(count // step_rows, to_hidden)

    def weights(i):
        at = rows_at(i, 512)
        dw[:, at] += tn(dqkv[...], h1[:, at])

    loop(width // 512, weights)


def whole_block(shape):
    return pl.BlockSpec(shape, lambda i: (0,) * len(shape))


def attn_forward(me, tokens, gain, w_all, ow, cos, sin, meta, krow, groups, scale):
    total = tokens.shape[0]
    cw, width = ow.shape
    count = total // groups
    row = lambda w: pl.BlockSpec((count, w), lambda i: (i, 0))
    shape = lambda w, t: jax.ShapeDtypeStruct((total, w), t)
    return pl.pallas_call(
        functools.partial(attn_forward_kernel, cw, scale),
        grid=(groups,),
        in_specs=[
            pl.BlockSpec(memory_space=pltpu.SMEM), row(width), whole_block(gain.shape),
            whole_block(w_all.shape), whole_block(ow.shape), row(LANES), row(LANES), row(8),
            pl.BlockSpec((1, 8, count), lambda i: (i, 0, 0)),
        ],
        out_specs=[row(3 * cw), row(cw), row(LANES), row(width)],
        out_shape=[shape(3 * cw, bf16), shape(cw, bf16), shape(LANES, f32), shape(width, bf16)],
        scratch_shapes=[pltpu.VMEM((count, width), bf16), pltpu.VMEM((count, LANES), f32)],
        compiler_params=pltpu.CompilerParams(vmem_limit_bytes=60 * MB),
    )(me, tokens, gain, w_all, ow, cos, sin, meta, krow)


def attn_backward(dmid, tokens, gain, qkv, att, aux, cos, sin, meta, krow, w_all, ow, groups, scale):
    total, width = dmid.shape
    cw = ow.shape[0]
    count = total // groups
    row = lambda w: pl.BlockSpec((count, w), lambda i: (i, 0))
    return pl.pallas_call(
        functools.partial(attn_backward_kernel, cw, scale),
        grid=(groups,),
        in_specs=[
            row(width), row(width), whole_block(gain.shape), row(3 * cw), row(cw), row(LANES), row(LANES), row(LANES), row(8),
            pl.BlockSpec((1, 8, count), lambda i: (i, 0, 0)),
            whole_block(w_all.shape), whole_block(ow.shape),
        ],
        out_specs=[row(width + LANES), whole_block((3 * cw, width)), whole_block((cw, width))],
        out_shape=[
            jax.ShapeDtypeStruct((total, width + LANES), bf16),
            jax.ShapeDtypeStruct((3 * cw, width), f32),
            jax.ShapeDtypeStruct((cw, width), f32),
        ],
        scratch_shapes=[
            pltpu.VMEM((count, width), bf16), pltpu.VMEM((count, cw), bf16), pltpu.VMEM((count, cw), bf16), pltpu.VMEM((count, 3 * cw), bf16),
            pltpu.VMEM((count, LANES), f32), pltpu.VMEM((count, LANES), f32),
        ],
        compiler_params=pltpu.CompilerParams(vmem_limit_bytes=60 * MB),
    )(dmid, tokens, gain, qkv, att, aux, cos, sin, meta, krow, w_all, ow)


def pieces(total, size):
    return [(at, min(size, total - at)) for at in range(0, total, size)]


def ffn_kernel(
    cap, me, h2, top, router, meta, posrow, gate_up, down,
    produced, dh2, aux, gate_up_grad, down_grad,
    wg, wu, wd, sg, su, sd, xc, gc, act, dgate, dup, yc, bc, gw, sems,
):
    rows, width = h2.shape
    hidden = wd.shape[0]
    blocks = rows // LANES
    step = pl.program_id(0)

    def masters(back):
        pairs = [(gate_up.at[:, 0, :], sg), (gate_up.at[:, 1, :], su), (down, sd)]
        if back:
            pairs = [(sg, gate_up_grad.at[:, 0, :]), (su, gate_up_grad.at[:, 1, :]), (sd, down_grad)]
        return [pltpu.make_async_copy(a, b, sems.at[i]) for i, (a, b) in enumerate(pairs)]

    @pl.when(step == 0)
    def _():
        copies = masters(False)
        for c in copies:
            c.start()
        for c, a, b in zip(copies, (sg, su, sd), (wg, wu, wd), strict=True):
            c.wait()

            def cast(i, a=a, b=b):
                at = rows_at(i, 32)
                b[at, :] = a[at, :].astype(bf16)
                a[at, :] = jnp.zeros((32, width), f32)

            loop(hidden // 32, cast)

    def gates(i):
        at = rows_at(i, LANES)
        found = gate_columns(nn(h2[at, :], router[...]), meta[at, 0:1], meta[at, 1:2], me[0])
        aux[at, :] = found
        gw[at, :] = (found[:, 0:1] * top[at, :].astype(f32)).astype(bf16)
        slot = lax.broadcasted_iota(jnp.int32, (cap, LANES), 0)
        choose = (slot == posrow[0, pl.ds(i, 1), :]).astype(bf16)
        to = rows_at(i, cap)
        xc[to, :] = nn(choose, h2[at, :]).astype(bf16)
        gc[to, :] = nn(choose, gw[at, :]).astype(bf16)

    loop(blocks, gates)

    for start, size in pieces(hidden, 256):
        fs = slice(start, start + size)
        gate, up, dact = nt(xc[...], wg[fs, :]), nt(xc[...], wu[fs, :]), nt(gc[...], wd[fs, :])
        sigmoid = 1.0 / (1.0 + jnp.exp(-gate))
        silu = gate * sigmoid
        act[:, fs] = (silu * up).astype(bf16)
        dgate[:, fs] = (dact * up * sigmoid * (1.0 + gate * (1.0 - sigmoid))).astype(bf16)
        dup[:, fs] = (dact * silu).astype(bf16)

        def grads(i, fs=fs):
            at = rows_at(i, 512)
            sd[fs, at] += tn(act[:, fs], gc[:, at])
            sg[fs, at] += tn(dgate[:, fs], xc[:, at])
            su[fs, at] += tn(dup[:, fs], xc[:, at])

        loop(width // 512, grads)

    def results(i):
        at = rows_at(i, 512)
        yc[:, at] = nn(act[...], wd[:, at]).astype(bf16)
        bc[:, at] = (nn(dgate[...], wg[:, at]) + nn(dup[...], wu[:, at])).astype(bf16)

    loop(width // 512, results)

    def scatter(i):
        at, of = rows_at(i, LANES), rows_at(i, cap)
        slot = lax.broadcasted_iota(jnp.int32, (cap, LANES), 0)
        choose = (slot == posrow[0, pl.ds(i, 1), :]).astype(bf16)
        found = aux[at, :]
        share = jnp.zeros((LANES, 1), f32)
        for start, size in pieces(width, 512):
            cs = slice(start, start + size)
            y = tn(choose, yc[of, cs])
            share = share + jnp.sum(y * top[at, cs].astype(f32), axis=1, keepdims=True)
            produced[at, cs] = (found[:, 0:1] * y).astype(bf16)
            dh2[at, cs] = tn(choose, bc[of, cs]).astype(bf16)
        dh2[at, width:] = jnp.broadcast_to(found[:, 1:2] * share, (LANES, LANES)).astype(bf16)

    loop(blocks, scatter)

    @pl.when(step == pl.num_programs(0) - 1)
    def _():
        copies = masters(True)
        for c in copies:
            c.start()
        for c in copies:
            c.wait()


def ffn(me, h2, top, router, meta, posrow, gate_up, down, cap):
    total, width = h2.shape
    hidden = down.shape[0]
    tile = posrow.shape[1] * LANES
    few = tile // LANES * cap
    row = lambda w: pl.BlockSpec((tile, w), lambda i: (i, 0))
    hbm = pl.BlockSpec(memory_space=pl.ANY)
    V = pltpu.VMEM
    return pl.pallas_call(
        functools.partial(ffn_kernel, cap),
        grid=(total // tile,),
        in_specs=[
            pl.BlockSpec(memory_space=pltpu.SMEM), row(width), row(width), whole_block(router.shape), row(8),
            pl.BlockSpec((1,) + posrow.shape[1:], lambda i: (i, 0, 0)), hbm, hbm,
        ],
        out_specs=[row(width), row(width + LANES), row(LANES), hbm, hbm],
        out_shape=[
            jax.ShapeDtypeStruct((total, width), bf16),
            jax.ShapeDtypeStruct((total, width + LANES), bf16),
            jax.ShapeDtypeStruct((total, LANES), f32),
            jax.ShapeDtypeStruct(gate_up.shape, f32),
            jax.ShapeDtypeStruct(down.shape, f32),
        ],
        scratch_shapes=[V((hidden, width), bf16)] * 3 + [V((hidden, width), f32)] * 3 + [V((few, width), bf16)] * 2
        + [V((few, hidden), bf16)] * 3 + [V((few, width), bf16)] * 2 + [V((tile, width), bf16), pltpu.SemaphoreType.DMA((3,))],
        compiler_params=pltpu.CompilerParams(vmem_limit_bytes=63 * MB),
    )(me, h2, top, router, meta, posrow, gate_up, down)


def ag_kernel(dims, halves, src, out, local_sem, zs, zr, xs, xr, ys, yr, cs, cr):
    nz, nx, ny = dims
    gi = lax.axis_index("grp"); ei = lax.axis_index("exp")
    z, x = gi // nx, gi % nx
    y, c = ei // 2, ei % 2
    ne = ny * 2
    rows = src.shape[0]
    part = rows // halves
    def dev(z_, x_, y_, c_):
        return (z_ * nx + x_, y_ * 2 + c_)
    def slot(z_, x_, y_, c_):
        return (z_ * nx + x_) * ne + y_ * 2 + c_
    barrier = pltpu.get_barrier_semaphore()
    def sig(d):
        pl.semaphore_signal(barrier, inc=1, device_id=d, device_id_type=MESH)
    sig(dev(z, 1 - x, y, c)); sig(dev(z, x, 1 - y, c)); sig(dev(z, x, y, 1 - c))
    @pl.when(z > 0)
    def _(): sig(dev(z - 1, x, y, c))
    @pl.when(z < nz - 1)
    def _(): sig(dev(z + 1, x, y, c))
    pl.semaphore_wait(barrier, 3 + (z > 0).astype(jnp.int32) + (z < nz - 1).astype(jnp.int32))
    own = pltpu.make_async_copy(src, out.at[slot(z, x, y, c)], local_sem)
    own.start()
    span = 2 * nz - 1
    def piece(sl, h):
        return out.at[sl, pl.ds(h * part, part)]
    def copy(sl, h, is_own, ssem, rsem, d):
        s = src.at[pl.ds(h * part, part)] if is_own else piece(sl, h)
        return pltpu.make_async_remote_copy(src_ref=s, dst_ref=piece(sl, h), send_sem=ssem, recv_sem=rsem, device_id=d, device_id_type=MESH)
    def zcopy(h, delta, direction, arriving):
        zz = z - delta * direction
        k = (h * 2 + (0 if direction > 0 else 1)) * nz
        if arriving:
            return copy(slot(zz, x, y, c), h, False, zs.at[k + delta], zr.at[k + delta], dev(z, x, y, c) if False else dev(z, x, y, 1 - c))
        return copy(slot(zz, x, y, c), h, delta == 0, zs.at[k + delta + 1], zr.at[k + delta + 1], dev(z + direction, x, y, c))
    def valid(delta):
        zz = z + delta
        return (zz >= 0) & (zz < nz)
    def when(cond, f):
        pl.when(cond)(f)
    sends = []
    def order(h):
        return ("x", "y") if h % 2 == 0 else ("y", "x")
    def first(h, delta):
        a = order(h)[0]
        sems = (xs, xr) if a == "x" else (ys, yr)
        k = h * 2 * span + delta + nz - 1
        d = dev(z, 1 - x, y, c) if a == "x" else dev(z, x, 1 - y, c)
        return copy(slot(z + delta, x, y, c), h, delta == 0, sems[0].at[k], sems[1].at[k], d), (
            lambda: copy(slot(z + delta, 1 - x if a == "x" else x, 1 - y if a == "y" else y, c), h, False, sems[0].at[k], sems[1].at[k], d))
    def second(h, delta, rel):
        a0, a = order(h)
        sems = (xs, xr) if a == "x" else (ys, yr)
        k = h * 2 * span + (rel * span) + delta + nz - 1
        d = dev(z, 1 - x, y, c) if a == "x" else dev(z, x, 1 - y, c)
        x0 = (1 - x if rel else x) if a0 == "x" else x
        y0 = (1 - y if rel else y) if a0 == "y" else y
        snd = copy(slot(z + delta, x0, y0, c), h, delta == 0 and rel == 0, sems[0].at[k], sems[1].at[k], d)
        x1 = 1 - x if a == "x" else x0
        y1 = 1 - y if a == "y" else y0
        rcv = copy(slot(z + delta, x1, y1, c), h, False, sems[0].at[k], sems[1].at[k], d)
        return snd, rcv
    def core(h, delta, rx, ry):
        k = h * 4 * span + (rx * 2 + ry) * span + delta + nz - 1
        d = dev(z, x, y, 1 - c)
        xx = 1 - x if rx else x
        yy = 1 - y if ry else y
        return (copy(slot(z + delta, xx, yy, c), h, delta == 0 and not rx and not ry, cs.at[k], cr.at[k], d),
                copy(slot(z + delta, xx, yy, 1 - c), h, False, cs.at[k], cr.at[k], d))
    hs = range(halves)
    def have_z(delta):
        for h in hs:
            if delta <= 0:
                when(z < nz - 1, lambda h=h: zcopy(h, -delta, 1, False).start())
            if delta >= 0:
                when(z > 0, lambda h=h: zcopy(h, delta, -1, False).start())
            first(h, delta)[0].start()
            second(h, delta, 0)[0].start()
            core(h, delta, 0, 0)[0].start()
    have_z(0)
    def get_z(delta):
        def f():
            for h in hs:
                zcopy(h, abs(delta), -1 if delta > 0 else 1, True).wait_recv()
            have_z(delta)
        when(valid(delta), f)
    def get_first(delta):
        def f():
            for h in hs:
                first(h, delta)[1]().wait_recv()
                second(h, delta, 1)[0].start()
                rx = 1 if order(h)[0] == "x" else 0
                core(h, delta, rx, 1 - rx)[0].start()
        when(valid(delta), f)
    def get_second(delta):
        def f():
            for h in hs:
                for rel in range(2):
                    second(h, delta, rel)[1].wait_recv()
                    a0, a = order(h)
                    rx = 1 if a == "x" else (rel if a0 == "x" else 0)
                    ry = 1 if a == "y" else (rel if a0 == "y" else 0)
                    core(h, delta, rx, ry)[0].start()
        when(valid(delta), f)
    for step in range(nz + 2):
        for dist, fn in ((step, get_z), (step - 1, get_first), (step - 2, get_second)):
            if 0 <= dist < nz:
                if dist == 0:
                    if fn is not get_z: fn(0)
                else:
                    fn(-dist); fn(dist)
    own.wait()
    for delta in range(-(nz - 1), nz):
        def f(delta=delta):
            for h in hs:
                for rx in range(2):
                    for ry in range(2):
                        a, b = core(h, delta, rx, ry)
                        b.wait_recv(); a.wait_send()
                first(h, delta)[0].wait_send()
                for rel in range(2):
                    second(h, delta, rel)[0].wait_send()
                if delta <= 0:
                    when(z < nz - 1, lambda h=h: zcopy(h, -delta, 1, False).wait_send())
                if delta >= 0:
                    when(z > 0, lambda h=h: zcopy(h, delta, -1, False).wait_send())
        when(valid(delta), f)

def gather_kernel(v, dims, cid, halves=2):
    nz, nx, ny = dims
    n = nz * nx * ny * 2
    span = 2 * nz - 1
    D = pltpu.SemaphoreType.DMA
    return pl.pallas_call(
        functools.partial(ag_kernel, dims, halves),
        out_shape=jax.ShapeDtypeStruct((n,) + v.shape, v.dtype),
        in_specs=[pl.BlockSpec(memory_space=pl.ANY)],
        out_specs=pl.BlockSpec(memory_space=pl.ANY),
        scratch_shapes=[D] + [D((halves * 2 * (nz + 1),))] * 2 + [D((halves * 2 * span,))] * 4 + [D((halves * 4 * span,))] * 2,
        compiler_params=pltpu.CompilerParams(collective_id=cid, has_side_effects=True),
    )(v)


def rs_kernel(dims, src, out, loc, crv, frv, srv, zrv, lsem, cs, cr, fs, fr, ss, sr, zs, zr):
    nz, nx, ny = dims
    gi = lax.axis_index("grp"); ei = lax.axis_index("exp")
    z, x = gi // nx, gi % nx
    y, c = ei // 2, ei % 2
    ne = ny * 2
    rows, width = out.shape
    part = rows // 2
    span = 2 * nz - 1
    def dev(z_, x_, y_, c_):
        return (z_ * nx + x_, y_ * 2 + c_)
    def slot(z_, x_, y_, c_):
        return (z_ * nx + x_) * ne + y_ * 2 + c_
    barrier = pltpu.get_barrier_semaphore()
    def sig(d):
        pl.semaphore_signal(barrier, inc=1, device_id=d, device_id_type=MESH)
    sig(dev(z, 1 - x, y, c)); sig(dev(z, x, 1 - y, c)); sig(dev(z, x, y, 1 - c))
    @pl.when(z > 0)
    def _(): sig(dev(z - 1, x, y, c))
    @pl.when(z < nz - 1)
    def _(): sig(dev(z + 1, x, y, c))
    pl.semaphore_wait(barrier, 3 + (z > 0).astype(jnp.int32) + (z < nz - 1).astype(jnp.int32))

    def flip(v, r):
        return 1 - v if r else v
    def remote(s, d, a, b, to):
        return pltpu.make_async_remote_copy(src_ref=s, dst_ref=d, send_sem=a, recv_sem=b, device_id=to, device_id_type=MESH)
    deltas = [d for k in range(nz - 1, 0, -1) for d in (k, -k)] + [0]
    def valid(d):
        return (z + d >= 0) & (z + d < nz)
    classes = [(1, 1), (1, 0), (0, 1), (0, 0)]
    def piece(ref, lead, h):
        return ref.at[lead, pl.ds(h * part, part)]
    def load(d, rx, ry):
        i = (z + d) * 4 + rx * 2 + ry
        return pltpu.make_async_copy(src.at[slot(z + d, flip(x, rx), flip(y, ry), c)], loc.at[i], lsem.at[i])
    def core(d, rx, ry, h):
        i = (z + d) * 4 + rx * 2 + ry
        return remote(src.at[slot(z + d, flip(x, rx), flip(y, ry), 1 - c), pl.ds(h * part, part)],
                      piece(crv, i, h), cs.at[i * 2 + h], cr.at[i * 2 + h], dev(z, x, y, 1 - c))
    def first(d, other, h):
        rx, ry = (other, 1) if h == 0 else (1, other)
        i = (z + d) * 4 + rx * 2 + ry
        k = ((z + d) * 2 + other) * 2 + h
        to = dev(z, x, 1 - y, c) if h == 0 else dev(z, 1 - x, y, c)
        return remote(piece(loc, i, h), frv.at[k], fs.at[k], fr.at[k], to)
    def second(d, h):
        rx, ry = (1, 0) if h == 0 else (0, 1)
        i = (z + d) * 4 + rx * 2 + ry
        k = (z + d) * 2 + h
        to = dev(z, 1 - x, y, c) if h == 0 else dev(z, x, 1 - y, c)
        return remote(piece(loc, i, h), srv.at[k], ss.at[k], sr.at[k], to)
    def zcopy(d, h, arriving_from):
        pass
    def zk(way, dist, h):
        return (way * nz + dist) * 2 + h
    def zsend(d, h):
        way = 0 if d > 0 else 1
        i = (z + d) * 4
        k = zk(way, abs(d) - 1, h)
        to = dev(z + (1 if d > 0 else -1), x, y, c)
        return remote(piece(loc, i, h), zrv.at[k], zs.at[k], zr.at[k], to)
    def zwait(way, dist, h):
        k = zk(way, dist, h)
        remote(piece(loc, 0, h), zrv.at[k], zs.at[k], zr.at[k], dev(z, x, y, 1 - c)).wait_recv()
        return zrv.at[k]
    def add(i, h, *others):
        def step(r, _):
            at = pl.ds(pl.multiple_of(r * 16, 16), 16)
            here = pl.ds(pl.multiple_of(h * part + r * 16, 16), 16)
            total = loc[i, here, :].astype(jnp.float32)
            for o in others:
                total = total + o[at, :].astype(jnp.float32)
            loc[i, here, :] = total.astype(loc.dtype)
            return 0
        lax.fori_loop(0, part // 16, step, 0)
    for cl in classes:
        for d in deltas:
            def go(cl=cl, d=d):
                load(d, *cl).start()
                for h in range(2):
                    core(d, *cl, h).start()
            pl.when(valid(d))(go)
    def got_core(d, rx, ry, h, *more):
        i = (z + d) * 4 + rx * 2 + ry
        core(d, rx, ry, h).wait_recv()
        add(i, h, crv.at[i, pl.ds(h * part, part)], *more)
    def each(f):
        for d in deltas:
            pl.when(valid(d))(functools.partial(f, d))
    def c11(d):
        load(d, 1, 1).wait()
        for h in range(2):
            got_core(d, 1, 1, h)
            first(d, 1, h).start()
    each(c11)
    def c_first(d):
        load(d, 0, 1).wait(); load(d, 1, 0).wait()
        got_core(d, 0, 1, 0); first(d, 0, 0).start()
        got_core(d, 1, 0, 1); first(d, 0, 1).start()
    each(c_first)
    def c_second(d):
        first(d, 1, 0).wait_recv()
        got_core(d, 1, 0, 0, frv.at[((z + d) * 2 + 1) * 2 + 0]); second(d, 0).start()
        first(d, 1, 1).wait_recv()
        got_core(d, 0, 1, 1, frv.at[((z + d) * 2 + 1) * 2 + 1]); second(d, 1).start()
    each(c_second)
    def c_last(d):
        load(d, 0, 0).wait()
        for h in range(2):
            first(d, 0, h).wait_recv()
            second(d, h).wait_recv()
            more = [frv.at[((z + d) * 2) * 2 + h], srv.at[(z + d) * 2 + h]]
            got_core(d, 0, 0, h, *more)
            if d != 0:
                way = 0 if d > 0 else 1
                def chained(h=h):
                    add((z + d) * 4, h, zwait(way, abs(d), h))
                pl.when(z > 0 if d > 0 else z < nz - 1)(chained)
                zsend(d, h).start()
    each(c_last)
    for h in range(2):
        def left(h=h): add(z * 4, h, zwait(0, 0, h))
        def right(h=h): add(z * 4, h, zwait(1, 0, h))
        pl.when(z > 0)(left)
        pl.when(z < nz - 1)(right)
    def finish(r, _):
        at = pl.ds(pl.multiple_of(r * 16, 16), 16)
        out[at, :] = loc[z * 4, at, :].astype(out.dtype)
        return 0
    lax.fori_loop(0, rows // 16, finish, 0)
    def drain(d):
        for cl in classes:
            for h in range(2):
                core(d, *cl, h).wait_send()
        for h in range(2):
            first(d, 0, h).wait_send(); first(d, 1, h).wait_send(); second(d, h).wait_send()
            if d != 0:
                zsend(d, h).wait_send()
    each(drain)

def scatter_kernel(p, dims, cid):
    nz, nx, ny = dims
    n, rows, width = p.shape
    D = pltpu.SemaphoreType.DMA
    V = lambda *s: pltpu.VMEM(s, p.dtype)
    return pl.pallas_call(
        functools.partial(rs_kernel, dims),
        out_shape=jax.ShapeDtypeStruct((rows, width), jnp.float32),
        in_specs=[pl.BlockSpec(memory_space=pl.ANY)],
        out_specs=pl.BlockSpec(memory_space=pltpu.VMEM),
        scratch_shapes=[V(nz * 4, rows, width), V(nz * 4, rows, width), V(nz * 4, rows // 2, width), V(nz * 2, rows // 2, width), V(nz * 4, rows // 2, width),
            D((nz * 4,)), D((nz * 8,)), D((nz * 8,)), D((nz * 4,)), D((nz * 4,)), D((nz * 2,)), D((nz * 2,)), D((nz * 4,)), D((nz * 4,))],
        compiler_params=pltpu.CompilerParams(collective_id=cid, has_side_effects=True, vmem_limit_bytes=56 * 1024 * 1024),
    )(p)


def layout(first, order, group_rows, block):
    places = jnp.arange(group_rows, dtype=jnp.int32)
    anchor = jnp.repeat(order, block, axis=1) * block + places % block
    doc = (anchor >= first).astype(jnp.int32)
    return (anchor, anchor - doc * first)


def rotary_tables(place):
    half = LANES // 2
    freq = jnp.exp(jnp.arange(half, dtype=f32) * (-2.0 * math.log(10000.0) / LANES))
    angle = place.astype(f32)[:, None] * freq[None, :]
    cos, sin = jnp.cos(angle), jnp.sin(angle)
    return (jnp.concatenate([cos, cos], axis=1), jnp.concatenate([-sin, sin], axis=1))


def logit_grad(route, gates, difference, experts):
    moved = gates[:, 0:1] * gates[:, 1:2] * difference
    names = jnp.arange(experts, dtype=jnp.int32)[None, :]
    return jnp.where(route[:, 0:1] == names, moved, 0.0) - jnp.where(
        route[:, 1:2] == names, moved, 0.0
    )


def norm_back(grad_hidden, normed, inverse, gain):
    grad_normed = grad_hidden * gain
    gain_grad = jnp.sum(grad_hidden * normed, axis=0)
    mean_term = jnp.mean(grad_normed * normed, axis=1, keepdims=True)
    return (inverse * (grad_normed - normed * mean_term), gain_grad)


def body(
    dims,
    layer_input,
    out_grad,
    doc_lengths,
    block_order,
    attn_route,
    ffn_route,
    norm_gains,
    kv_master,
    router_master,
    query_master,
    output_master,
    gate_up_master,
    down_master,
):
    own_rows, width = layer_input.shape
    members, groups = lax.axis_size("exp"), lax.axis_size("grp")
    member, group = lax.axis_index("exp"), lax.axis_index("grp")
    experts = members
    capacity = 3 * own_rows // experts
    group_rows = own_rows * members
    total = group_rows * groups
    devices = groups * members
    cw = width // groups
    depth = kv_master.shape[0]
    scale = 1.0 / math.sqrt(LANES)
    me = member.reshape(1).astype(jnp.int32)
    both = ("grp", "exp")

    def gather_all(v, cid):
        if dims is None:
            return lax.all_gather(v, both, axis=0, tiled=False)
        return gather_kernel(v, dims, cid)

    def scatter_all(v, cid):
        v = v.reshape(devices, own_rows, v.shape[-1])
        if dims is None:
            return lax.psum_scatter(v, both, scatter_dimension=0, tiled=False).astype(f32)
        return scatter_kernel(v, dims, cid)

    blocks = block_order.shape[1]
    start_row = member * own_rows
    own_attn_route = lax.dynamic_slice_in_dim(attn_route, start_row, own_rows)
    own_ffn_route = lax.dynamic_slice_in_dim(ffn_route, start_row, own_rows)
    tall = lambda v: jnp.pad(v.astype(bf16), ((0, own_rows - v.shape[0]), (0, 0)))
    first_doc = doc_lengths[:, 0]
    small = jnp.concatenate(
        [
            tall(norm_gains),
            tall(router_master),
            own_attn_route.astype(bf16),
            own_ffn_route.astype(bf16),
            tall(jnp.concatenate([first_doc // 16, first_doc % 16, block_order[0]])[:, None]),
        ],
        axis=1,
    )
    at_route = 2 + 2 * experts
    sent = jnp.concatenate([layer_input, jnp.pad(small, ((0, 0), (0, LANES - small.shape[1])))], axis=1)
    tokens = gather_all(sent, 1).reshape(total, width + LANES)
    tops = gather_all(out_grad, 2).reshape(total, width)

    query_low = query_master[0].astype(bf16)
    kv_low = kv_master.astype(bf16).reshape(depth * 2, groups, cw)
    pieces_out = jnp.concatenate(
        [query_low.reshape(query_low.shape[0], groups, cw), kv_low], axis=0
    ).transpose(1, 0, 2)
    pieces_in = lax.all_to_all(pieces_out, "grp", split_axis=0, concat_axis=0, tiled=True)
    query_weight = pieces_in[:, : query_low.shape[0]].reshape(width, cw)
    kv_all = lax.all_gather(pieces_in[:, query_low.shape[0] :], "exp", axis=1, tiled=False)
    kv_weight = kv_all.reshape(width, 2 * cw)
    output_weight = output_master[0].astype(bf16)

    extra = tokens[:, width:]
    tables = extra.reshape(devices, own_rows, LANES)[:, :depth, :at_route].reshape(width, at_route)
    gains = tables[:, :2].astype(f32)
    router = tables[:, 2:]
    router_float = router.astype(f32)
    wide = lambda v: jnp.pad(v, ((0, 0), (0, LANES - v.shape[1])))
    routes = extra[:, at_route : at_route + 4].astype(jnp.int32)
    column = extra.reshape(groups, group_rows, LANES)[:, : blocks + 2, at_route + 4].astype(jnp.int32)
    anchor, place = layout(
        column[:, 0:1] * 16 + column[:, 1:2], column[:, 2:], group_rows, own_rows // 2
    )
    cos, sin = rotary_tables(place.reshape(total))
    zero = jnp.zeros((total, 4), jnp.int32)
    attn_meta = jnp.concatenate(
        [anchor.reshape(total, 1), (anchor - place).reshape(total, 1), routes[:, :2], zero], axis=1
    )
    key_rows = jnp.broadcast_to(anchor[:, None, :], (groups, 8, group_rows))
    gain_one, gain_two = gains[:, 0], gains[:, 1]
    w_all = jnp.concatenate([query_weight, kv_weight, wide(router[:, :experts])], axis=1)

    qkv, att, aux, attn_part = attn_forward(
        me, tokens, gain_one[None], w_all, output_weight, cos, sin, attn_meta, key_rows, groups, scale
    )
    own = (group * members + member) * own_rows
    attn_gates = lax.dynamic_slice(aux, (own, 2), (own_rows, 2))
    inputs = layer_input.astype(f32)
    middle = inputs + scatter_all(attn_part, 3)
    inverse_two = lax.rsqrt(jnp.mean(middle * middle, axis=1, keepdims=True) + epsilon)
    normed_two = middle * inverse_two
    hidden_two = (normed_two * gain_two).astype(bf16)
    h2 = gather_all(hidden_two, 4).reshape(total, width)

    ffn_meta = jnp.concatenate([routes[:, 2:], zero, zero[:, :2]], axis=1)
    named = (routes[:, 2] == member) | (routes[:, 3] == member)
    named = named.reshape(devices, own_rows)
    position = jnp.cumsum(named.astype(jnp.int32), axis=1) - 1
    position = jnp.where(named, position, -1)
    tile_blocks = 4
    produced, dh2, ffn_aux, gate_up_grad, down_grad = ffn(
        me, h2, tops, wide(router[:, experts:]), ffn_meta,
        position.reshape(devices // tile_blocks, tile_blocks, own_rows),
        gate_up_master[0], down_master[0], capacity,
    )
    ffn_gates = lax.dynamic_slice(ffn_aux, (own, 2), (own_rows, 2))
    back = scatter_all(dh2, 5)
    top_grad = out_grad.astype(f32)
    ffn_logit_grad = logit_grad(own_ffn_route, ffn_gates, back[:, width : width + 1], experts)
    hidden_two_grad = back[:, :width] + jnp.einsum(
        "te,de->td", ffn_logit_grad, router_float[:, experts:], precision=highest
    )
    middle_part, gain_two_grad = norm_back(hidden_two_grad, normed_two, inverse_two, gain_two)
    middle_grad = top_grad + middle_part
    dmid = gather_all(middle_grad.astype(bf16), 6).reshape(total, width)

    if dims is None:
        again, dmid = lax.optimization_barrier((layer_input, dmid))
        tokens = gather_all(again, 9).reshape(total, width)
    dh1, dw, do = attn_backward(
        dmid, tokens, gain_one[None], qkv, att, aux, cos, sin, attn_meta, key_rows, w_all, output_weight, groups, scale
    )
    final = middle + scatter_all(produced, 7)
    back = scatter_all(dh1, 8)
    inverse_one = lax.rsqrt(jnp.mean(inputs * inputs, axis=1, keepdims=True) + epsilon)
    normed_one = inputs * inverse_one
    hidden_one = (normed_one * gain_one).astype(bf16)
    attn_logit_grad = logit_grad(own_attn_route, attn_gates, back[:, width : width + 1], experts)
    hidden_one_grad = back[:, :width] + jnp.einsum(
        "te,de->td", attn_logit_grad, router_float[:, :experts], precision=highest
    )
    input_part, gain_one_grad = norm_back(hidden_one_grad, normed_one, inverse_one, gain_one)
    input_grad = middle_grad + input_part
    route_grad = [
        jnp.einsum("td,te->de", a.astype(f32), b, precision=highest)
        for a, b in ((hidden_one, attn_logit_grad), (hidden_two, ffn_logit_grad))
    ]
    sums = jnp.concatenate(
        [gain_one_grad[:, None], gain_two_grad[:, None], route_grad[0], route_grad[1]], axis=1
    )
    sums = lax.psum_scatter(sums, both, scatter_dimension=0, tiled=True)

    kv_part = dw[cw:].reshape(2 * cw, groups, members, depth)
    kv_part = lax.psum_scatter(kv_part.astype(bf16), "exp", scatter_dimension=2, tiled=False)
    query_part = dw[:cw].astype(bf16).reshape(cw, groups, width // groups)
    pieces_out = jnp.concatenate(
        [query_part.transpose(1, 0, 2).reshape(groups, -1), kv_part.transpose(1, 0, 2).reshape(groups, -1)],
        axis=1,
    )
    pieces_in = lax.all_to_all(pieces_out, "grp", split_axis=0, concat_axis=0, tiled=True)
    cut = cw * (width // groups)
    query_grad = pieces_in[:, :cut].reshape(width, width // groups).T.astype(f32)
    kv_grad = (
        pieces_in[:, cut:].reshape(groups, 2, cw, depth).transpose(3, 1, 0, 2).reshape(depth, 2 * width)
    ).astype(f32)
    return (
        final.astype(bf16),
        input_grad,
        sums[:, :2],
        kv_grad,
        sums[:, 2:],
        query_grad[None],
        do[None],
        gate_up_grad[None],
        down_grad[None],
    )


def solution(mesh):
    groups, members = mesh.shape["grp"], mesh.shape["exp"]
    dims = (groups // 2, 2, members // 2) if groups <= 8 and members == 4 else None
    in_specs = (
        P(("grp", "exp"), None),
        P(("grp", "exp"), None),
        P("grp", None),
        P("grp", None),
        P("grp", None),
        P("grp", None),
        P(("grp", "exp"), None),
        P(("grp", "exp"), None),
        P(("grp", "exp"), None),
        P("exp", "grp", None),
        P("exp", "grp", None),
        P("exp", "grp", None, None),
        P("exp", "grp", None),
    )
    out_specs = (
        P(("grp", "exp"), None),
        P(("grp", "exp"), None),
        P(("grp", "exp"), None),
        P(("grp", "exp"), None),
        P(("grp", "exp"), None),
        P("exp", "grp", None),
        P("exp", "grp", None),
        P("exp", "grp", None, None),
        P("exp", "grp", None),
    )
    return jax.shard_map(
        functools.partial(body, dims),
        mesh=mesh,
        in_specs=in_specs,
        out_specs=out_specs,
        check_vma=False,
    )
```

```python
import functools
import math

import jax
import jax.numpy as jnp
from jax import lax
from jax.experimental import pallas as pl
from jax.experimental.pallas import tpu as pltpu
from jax.sharding import PartitionSpec as P

HEADS = 16
LANES = 128
MESH = pl.DeviceIdType.MESH
MB = 1024 * 1024

epsilon = 1e-05
negative = -1e30
highest = lax.Precision.HIGHEST
f32 = jnp.float32
bf16 = jnp.bfloat16


def nn(a, b):
    return jnp.dot(a, b, preferred_element_type=f32)


def nt(a, b):
    return lax.dot_general(a, b, (((1,), (1,)), ((), ())), preferred_element_type=f32)


def tn(a, b):
    return lax.dot_general(a, b, (((0,), (0,)), ((), ())), preferred_element_type=f32)


def loop(count, step):
    def run(i, carry):
        step(i)
        return carry

    lax.fori_loop(0, count, run, 0)


def rows_at(i, size):
    return pl.ds(pl.multiple_of(i * size, size), size)


def kept(v):
    def copy(src, dst):
        dst[...] = src[...]

    return pl.pallas_call(copy, out_shape=jax.ShapeDtypeStruct(v.shape, v.dtype))(v)


def turn(v, cos, sin):
    return v * cos + pltpu.roll(v, LANES // 2, 1) * sin


def gate_columns(logits, r0, r1, me):
    lane = lax.broadcasted_iota(jnp.int32, logits.shape, 1)
    l0 = jnp.sum(jnp.where(lane == r0, logits, 0.0), axis=1, keepdims=True)
    l1 = jnp.sum(jnp.where(lane == r1, logits, 0.0), axis=1, keepdims=True)
    top = jnp.maximum(l0, l1)
    e0, e1 = jnp.exp(l0 - top), jnp.exp(l1 - top)
    g0, g1 = e0 / (e0 + e1), e1 / (e0 + e1)
    weight = jnp.where(r0 == me, g0, 0.0) + jnp.where(r1 == me, g1, 0.0)
    sign = jnp.where(r0 == me, 1.0, 0.0) - jnp.where(r1 == me, 1.0, 0.0)
    return jnp.where(
        lane == 0,
        weight,
        jnp.where(lane == 1, sign, jnp.where(lane == 2, g0, jnp.where(lane == 3, g1, 0.0))),
    )


def attn_forward_kernel(
    cw, scale, me, tokens, gain, w_all, ow, cos, sin, meta, krow, qkv, att, aux, part, h1, inv
):
    count, width = h1.shape
    heads = cw // LANES
    step_rows = 256

    def normalise(i):
        at = rows_at(i, 64)
        v = tokens[at, :].astype(f32)
        inverse = lax.rsqrt(jnp.mean(v * v, axis=1, keepdims=True) + epsilon)
        inv[at, :] = jnp.broadcast_to(inverse, (64, LANES))
        h1[at, :] = (v * inverse * gain[...]).astype(bf16)

    loop(count // 64, normalise)

    def project(i):
        at = rows_at(i, step_rows)
        y = nn(h1[at, :], w_all[...])
        c, s = cos[at, :], sin[at, :]
        for h in range(2 * heads):
            qkv[at, h * LANES : (h + 1) * LANES] = turn(
                y[:, h * LANES : (h + 1) * LANES], c, s
            ).astype(bf16)
        qkv[at, 2 * cw : 3 * cw] = y[:, 2 * cw : 3 * cw].astype(bf16)
        found = gate_columns(y[:, 3 * cw : 3 * cw + LANES], meta[at, 2:3], meta[at, 3:4], me[0])
        lane = lax.broadcasted_iota(jnp.int32, found.shape, 1)
        aux[at, :] = jnp.where(lane == 4, inv[at, :], found)

    loop(count // step_rows, project)

    for h in range(heads):

        def attend(i, h=h):
            at = rows_at(i, LANES)
            q = qkv[at, h * LANES : (h + 1) * LANES]
            k = qkv[:, cw + h * LANES : cw + (h + 1) * LANES]
            v = qkv[:, 2 * cw + h * LANES : 2 * cw + (h + 1) * LANES]
            ak = krow[0, 0:1, :]
            allowed = (ak <= meta[at, 0:1]) & (ak >= meta[at, 1:2])
            scores = jnp.where(allowed, nt(q, k) * scale, negative)
            top = jnp.max(scores, axis=1, keepdims=True)
            raised = jnp.exp(scores - top)
            total = jnp.sum(raised, axis=1, keepdims=True)
            probs = (raised * (1.0 / total)).astype(bf16)
            att[at, h * LANES : (h + 1) * LANES] = nn(probs, v).astype(bf16)
            old = aux[at, :]
            lane = lax.broadcasted_iota(jnp.int32, old.shape, 1)
            aux[at, :] = jnp.where(lane == 8 + h, top + jnp.log(total), old)

        loop(count // LANES, attend)

    def output(i):
        at = rows_at(i, step_rows)
        scaled = (aux[at, 0:1] * att[at, :].astype(f32)).astype(bf16)
        part[at, :] = nn(scaled, ow[...]).astype(bf16)

    loop(count // step_rows, output)


def attn_backward_kernel(
    cw, scale, dmid, tokens, gain, qkv, att, aux, cos, sin, meta, krow, w_all, ow,
    dh1, side, dw, do, h1, datt, watt, dqkv, dk_sum, dv_sum,
):
    count, width = h1.shape
    heads = cw // LANES
    step_rows = 256

    @pl.when(pl.program_id(0) == 0)
    def _():
        dw[...] = jnp.zeros_like(dw)
        do[...] = jnp.zeros_like(do)

    def normalise(i):
        at = rows_at(i, 64)
        h1[at, :] = (tokens[at, :].astype(f32) * aux[at, 4:5] * gain[...]).astype(bf16)

    loop(count // 64, normalise)

    def incoming(i):
        at = rows_at(i, step_rows)
        raw = nt(dmid[at, :], ow[...])
        a = att[at, :].astype(f32)
        weight, sign = aux[at, 0:1], aux[at, 1:2]
        share = sign * jnp.sum(raw * a, axis=1, keepdims=True)
        side[at, :] = jnp.broadcast_to(share, (step_rows, LANES)).astype(bf16)
        datt[at, :] = (weight * raw).astype(bf16)
        watt[at, :] = (weight * a).astype(bf16)

    loop(count // step_rows, incoming)

    def out_weight(i):
        at = rows_at(i, 512)
        do[:, at] += tn(watt[...], dmid[:, at])

    loop(width // 512, out_weight)

    for h in range(heads):
        hs = slice(h * LANES, (h + 1) * LANES)
        ks = slice(cw + h * LANES, cw + (h + 1) * LANES)
        vs = slice(2 * cw + h * LANES, 2 * cw + (h + 1) * LANES)
        dk_sum[...] = jnp.zeros_like(dk_sum)
        dv_sum[...] = jnp.zeros_like(dv_sum)

        def back(i, h=h, hs=hs, ks=ks, vs=vs):
            at = rows_at(i, LANES)
            q, k, v = qkv[at, hs], qkv[:, ks], qkv[:, vs]
            ak = krow[0, 0:1, :]
            allowed = (ak <= meta[at, 0:1]) & (ak >= meta[at, 1:2])
            scores = jnp.where(allowed, nt(q, k) * scale, negative)
            probs = jnp.exp(scores - aux[at, 8 + h : 9 + h])
            grad = datt[at, hs]
            dprobs = nt(grad, v)
            inner = jnp.sum(probs * dprobs, axis=1, keepdims=True)
            dscores = (probs * (dprobs - inner)).astype(bf16)
            dqkv[at, hs] = turn(nn(dscores, k) * scale, cos[at, :], -sin[at, :]).astype(bf16)
            dk_sum[...] += tn(dscores, q)
            dv_sum[...] += tn(probs.astype(bf16), grad)

        loop(count // LANES, back)
        dqkv[:, ks] = turn(dk_sum[...] * scale, cos[...], -sin[...]).astype(bf16)
        dqkv[:, vs] = dv_sum[...].astype(bf16)

    def to_hidden(i):
        at = rows_at(i, step_rows)
        dh1[at, :width] = nt(dqkv[at, :], w_all[:, : 3 * cw]).astype(bf16)

    loop(count // step_rows, to_hidden)

    def weights(i):
        at = rows_at(i, 512)
        dw[:, at] += tn(dqkv[...], h1[:, at])

    loop(width // 512, weights)


def whole_block(shape):
    return pl.BlockSpec(shape, lambda i: (0,) * len(shape))


def once(shape):
    return pl.BlockSpec(shape, lambda i: (0,) * len(shape), pipeline_mode=pl.Buffered(1))


def attn_forward_fused(dims, cw, scale, me, tokens, gain, w_all, ow, cos, sin, meta, krow, qkv, att, aux, out, h1, inv, *refs):
    i = pl.program_id(0)
    place = Place(dims)
    sums = Scatter(dims, place, out, refs)
    pl.when(i == 0)(place.greet)

    @pl.when(i < sums.tiles)
    def _():
        attn_forward_kernel(cw, scale, me, tokens, gain, w_all, ow, cos, sin, meta, krow, qkv, att, aux, sums.tile.at[i % 2], h1, inv)

    pl.when(i == 0)(place.greeted)
    sums.run(i)


def attn_forward(dims, cid, me, tokens, gain, w_all, ow, cos, sin, meta, krow, groups, scale):
    total = tokens.shape[0]
    cw, width = ow.shape
    count = total // groups
    at = (lambda i: tile_group(i, dims)) if dims else (lambda i: i)
    row = lambda w: pl.BlockSpec((count, w), lambda i: (at(i), 0))
    shape = lambda w, t: jax.ShapeDtypeStruct((total, w), t)
    if dims:
        own = count // 4
        kernel = functools.partial(attn_forward_fused, dims, cw, scale)
        last_spec, last_shape = whole_block((own, width)), jax.ShapeDtypeStruct((own, width), f32)
        params, more = dict(collective_id=cid, has_side_effects=True), scatter_scratch(dims, own, width)
    else:
        kernel = functools.partial(attn_forward_kernel, cw, scale)
        last_spec, last_shape, params, more = row(width), shape(width, bf16), {}, []
    return pl.pallas_call(
        kernel,
        grid=(groups + 2 + dims[0] if dims else groups,),
        in_specs=[
            pl.BlockSpec(memory_space=pltpu.SMEM), row(width), whole_block(gain.shape),
            once(w_all.shape), once(ow.shape), row(LANES), row(LANES), row(8),
            pl.BlockSpec((1, 8, count), lambda i: (at(i), 0, 0)),
        ],
        out_specs=[row(3 * cw), row(cw), row(LANES), last_spec],
        out_shape=[shape(3 * cw, bf16), shape(cw, bf16), shape(LANES, f32), last_shape],
        scratch_shapes=[pltpu.VMEM((count, width), bf16), pltpu.VMEM((count, LANES), f32)] + more,
        compiler_params=pltpu.CompilerParams(vmem_limit_bytes=60 * MB, **params),
    )(me, tokens, gain, w_all, ow, cos, sin, meta, krow)


def attn_backward_plain(cw, scale, dmid, tokens, gain, qkv, att, aux, cos, sin, meta, krow, w_all, ow, dw_hbm, do_hbm, dh1, side, dw, do, sems, *more):
    attn_backward_kernel(cw, scale, dmid, tokens, gain, qkv, att, aux, cos, sin, meta, krow, w_all, ow, dh1, side, dw, do, *more)
    pl.when(pl.program_id(0) == pl.num_programs(0) - 1)(lambda: attn_weights_out(dw, do, dw_hbm, do_hbm, sems))


def attn_weights_out(dw, do, dw_hbm, do_hbm, sems):
    copies = [pltpu.make_async_copy(a, b, sems.at[n]) for n, (a, b) in enumerate(((dw, dw_hbm), (do, do_hbm)))]
    for c in copies:
        c.start()
    for c in copies:
        c.wait()


def attn_backward_fused(dims, cw, scale, dmid, tokens, gain, qkv, att, aux, cos, sin, meta, krow, w_all, ow, dw_hbm, do_hbm, out, dw, do, sems, h1, datt, watt, dqkv, dk_sum, dv_sum, *refs):
    i = pl.program_id(0)
    place = Place(dims)
    sums = Scatter(dims, place, out, refs)
    pl.when(i == 0)(place.greet)

    @pl.when(i < sums.tiles)
    def _():
        tile, side = sums.tile.at[i % 2], sums.tile.at[i % 2, :, pl.ds(dmid.shape[1], LANES)]
        attn_backward_kernel(cw, scale, dmid, tokens, gain, qkv, att, aux, cos, sin, meta, krow, w_all, ow, tile, side, dw, do, h1, datt, watt, dqkv, dk_sum, dv_sum)

    pl.when(i == 0)(place.greeted)
    sums.run(i)
    pl.when(i == sums.tiles)(lambda: attn_weights_out(dw, do, dw_hbm, do_hbm, sems))


def attn_backward(dims, cid, dmid, tokens, gain, qkv, att, aux, cos, sin, meta, krow, w_all, ow, groups, scale):
    total, width = dmid.shape
    cw = ow.shape[0]
    count = total // groups
    at = (lambda i: tile_group(i, dims)) if dims else (lambda i: i)
    row = lambda w: pl.BlockSpec((count, w), lambda i: (at(i), 0))
    wide = width + LANES
    hbm = pl.BlockSpec(memory_space=pl.ANY)
    if dims:
        own = count // 4
        kernel = functools.partial(attn_backward_fused, dims, cw, scale)
        last_spec, last_shape = [whole_block((own, wide))], [jax.ShapeDtypeStruct((own, wide), f32)]
        params, more = dict(collective_id=cid, has_side_effects=True), scatter_scratch(dims, own, wide)
    else:
        kernel = functools.partial(attn_backward_plain, cw, scale)
        last_spec = [row(width), row(LANES)]
        last_shape = [jax.ShapeDtypeStruct((total, w), bf16) for w in (width, LANES)]
        params, more = {}, []
    return pl.pallas_call(
        kernel,
        grid=(groups + 2 + dims[0] if dims else groups,),
        in_specs=[
            row(width), row(width), whole_block(gain.shape), row(3 * cw), row(cw), row(LANES), row(LANES), row(LANES), row(8),
            pl.BlockSpec((1, 8, count), lambda i: (at(i), 0, 0)),
            once(w_all.shape), once(ow.shape),
        ],
        out_specs=[hbm, hbm] + last_spec,
        out_shape=[jax.ShapeDtypeStruct((3 * cw, width), f32), jax.ShapeDtypeStruct((cw, width), f32)] + last_shape,
        scratch_shapes=[
            pltpu.VMEM((3 * cw, width), f32), pltpu.VMEM((cw, width), f32), pltpu.SemaphoreType.DMA((2,)),
            pltpu.VMEM((count, width), bf16), pltpu.VMEM((count, cw), bf16), pltpu.VMEM((count, cw), bf16), pltpu.VMEM((count, 3 * cw), bf16),
            pltpu.VMEM((count, LANES), f32), pltpu.VMEM((count, LANES), f32),
        ] + more,
        compiler_params=pltpu.CompilerParams(vmem_limit_bytes=62 * MB, **params),
    )(dmid, tokens, gain, qkv, att, aux, cos, sin, meta, krow, w_all, ow)


def pieces(total, size):
    return [(at, min(size, total - at)) for at in range(0, total, size)]


def chosen(posrow, i, cap):
    slot = lax.broadcasted_iota(jnp.int32, (cap, LANES), 0)
    return (slot == posrow[0, pl.ds(i, 1), :]).astype(bf16)


def compact(cap, h2, top, posrow, weight, xc, gc):
    def block(i):
        at, to = rows_at(i, LANES), rows_at(i, cap)
        choose = chosen(posrow, i, cap)
        w = weight(i, at)
        for start, size in pieces(h2.shape[1], 512):
            cs = slice(start, start + size)
            xc[to, cs] = nn(choose, h2[at, cs]).astype(bf16)
            gated = (w * top[at, cs].astype(f32)).astype(bf16)
            gc[to, cs] = nn(choose, gated).astype(bf16)

    loop(h2.shape[0] // LANES, block)


def stage_rows(hidden):
    return max(r for r in range(16, 177, 16) if hidden % r == 0)


def load_masters(gate_up, down, wg, wu, wd, stage, sems):
    hidden, part = wd.shape[0], stage.shape[1]
    jobs = [
        (src.at[pl.ds(n * part, part)], dst.at[pl.ds(n * part, part)])
        for n in range(hidden // part)
        for src, dst in ((gate_up.at[:, 0, :], wg), (gate_up.at[:, 1, :], wu), (down, wd))
    ]
    copies = [pltpu.make_async_copy(job[0], stage.at[n % 2], sems.at[n % 2]) for n, job in enumerate(jobs)]
    copies[0].start()
    for n, (_, dst) in enumerate(jobs):
        if n + 1 < len(jobs):
            copies[n + 1].start()
        copies[n].wait()

        def cast(r, dst=dst, n=n):
            at = rows_at(r, 16)
            dst[at, :] = stage[n % 2, at, :].astype(bf16)

        loop(part // 16, cast)


def ffn_compute(cap, me, h2, top, router, meta, posrow, produced, dh2, side, aux, act, dgate, dup, wg, wu, wd, xc, gc):
    rows, width = h2.shape
    hidden = wd.shape[0]
    blocks = rows // LANES

    def weight(i, at):
        found = gate_columns(nn(h2[at, :], router[...]), meta[at, 4:5], meta[at, 5:6], me[0])
        aux[at, :] = found
        return found[:, 0:1]

    compact(cap, h2, top, posrow, weight, xc, gc)

    for start, size in pieces(hidden, 256):
        fs = slice(start, start + size)
        gate, up, dact = nt(xc[...], wg[fs, :]), nt(xc[...], wu[fs, :]), nt(gc[...], wd[fs, :])
        sigmoid = 1.0 / (1.0 + jnp.exp(-gate))
        silu = gate * sigmoid
        act[:, fs] = (silu * up).astype(bf16)
        dgate[:, fs] = (dact * up * sigmoid * (1.0 + gate * (1.0 - sigmoid))).astype(bf16)
        dup[:, fs] = (dact * silu).astype(bf16)

    yc, bc = gc, xc

    def results(i):
        at = rows_at(i, 512)
        yc[:, at] = nn(act[...], wd[:, at]).astype(bf16)
        bc[:, at] = (nn(dgate[...], wg[:, at]) + nn(dup[...], wu[:, at])).astype(bf16)

    loop(width // 512, results)

    def scatter(i):
        at, of = rows_at(i, LANES), rows_at(i, cap)
        choose = chosen(posrow, i, cap)
        found = aux[at, :]
        share = jnp.zeros((LANES, 1), f32)
        for start, size in pieces(width, 512):
            cs = slice(start, start + size)
            y = tn(choose, yc[of, cs])
            share = share + jnp.sum(y * top[at, cs].astype(f32), axis=1, keepdims=True)
            produced[at, cs] = (found[:, 0:1] * y).astype(bf16)
            dh2[at, cs] = tn(choose, bc[of, cs]).astype(bf16)
        side[at, :] = jnp.broadcast_to(found[:, 1:2] * share, (LANES, LANES)).astype(bf16)

    loop(blocks, scatter)


def ffn_kernel(cap, me, h2, top, router, meta, posrow, gate_up, down, produced, aux, act, dgate, dup, dh2, side, wg, wu, wd, xc, gc, stage, sems):
    pl.when(pl.program_id(0) == 0)(lambda: load_masters(gate_up, down, wg, wu, wd, stage, sems))
    ffn_compute(cap, me, h2, top, router, meta, posrow, produced, dh2, side, aux, act, dgate, dup, wg, wu, wd, xc, gc)


def ffn_fused_kernel(dims, cap, me, h2, top, router, meta, posrow, gate_up, down, produced, aux, act, dgate, dup, out, wg, wu, wd, xc, gc, stage, sems, *refs):
    i = pl.program_id(0)
    place = Place(dims)
    sums = Scatter(dims, place, out, refs)

    @pl.when(i == 0)
    def _():
        place.greet()
        load_masters(gate_up, down, wg, wu, wd, stage, sems)

    @pl.when(i < sums.tiles)
    def _():
        tile, side = sums.tile.at[i % 2], sums.tile.at[i % 2, :, pl.ds(h2.shape[1], LANES)]
        ffn_compute(cap, me, h2, top, router, meta, posrow, produced, tile, side, aux, act, dgate, dup, wg, wu, wd, xc, gc)

    pl.when(i == 0)(place.greeted)
    sums.run(i)


def ffn(dims, cid, me, h2, top, router, meta, posrow, gate_up, down, cap):
    total, width = h2.shape
    hidden = down.shape[0]
    tile = posrow.shape[1] * LANES
    few = tile // LANES * cap
    tiles = total // tile
    at = (lambda i: tile_group(i, dims)) if dims else (lambda i: i)
    row = lambda w: pl.BlockSpec((tile, w), lambda i: (at(i), 0))
    some = pl.BlockSpec((few, hidden), lambda i: (at(i), 0))
    hbm = pl.BlockSpec(memory_space=pl.ANY)
    V = pltpu.VMEM
    own = total // (dims[0] * dims[1] * dims[2] * 2) if dims else 0
    wide = width + LANES
    if dims:
        kernel = functools.partial(ffn_fused_kernel, dims, cap)
        last_spec, last_shape = [whole_block((own, wide))], [jax.ShapeDtypeStruct((own, wide), f32)]
        params = dict(collective_id=cid, has_side_effects=True)
    else:
        kernel = functools.partial(ffn_kernel, cap)
        last_spec = [row(width), row(LANES)]
        last_shape = [jax.ShapeDtypeStruct((total, w), bf16) for w in (width, LANES)]
        params = {}
    return pl.pallas_call(
        kernel,
        grid=(tiles + 2 + dims[0] if dims else tiles,),
        in_specs=[
            pl.BlockSpec(memory_space=pltpu.SMEM), row(width), row(width), whole_block(router.shape), row(8),
            pl.BlockSpec((1,) + posrow.shape[1:], lambda i: (at(i), 0, 0)), hbm, hbm,
        ],
        out_specs=[row(width), row(LANES), some, some, some] + last_spec,
        out_shape=[
            jax.ShapeDtypeStruct((total, width), bf16),
            jax.ShapeDtypeStruct((total, LANES), f32),
        ] + [jax.ShapeDtypeStruct((tiles * few, hidden), bf16)] * 3 + last_shape,
        scratch_shapes=[V((hidden, width), bf16)] * 3 + [V((few, width), bf16)] * 2
        + [V((2, stage_rows(hidden), width), f32), pltpu.SemaphoreType.DMA((2,))]
        + (scatter_scratch(dims, own, wide) if dims else []),
        compiler_params=pltpu.CompilerParams(vmem_limit_bytes=63 * MB, **params),
    )(me, h2, top, router, meta, posrow, gate_up, down)


def ffn_weights_compute(cap, first, h2, top, aux, posrow, act, dgate, dup, sg, su, sd, xc, gc):
    width = h2.shape[1]
    hidden = sd.shape[0]

    @pl.when(first)
    def _():
        for s in (sg, su, sd):

            def clear(i, s=s):
                s[rows_at(i, 32), :] = jnp.zeros((32, width), f32)

            loop(hidden // 32, clear)

    compact(cap, h2, top, posrow, lambda i, at: aux[at, 0:1], xc, gc)
    for start, size in pieces(hidden, 256):
        fs = slice(start, start + size)

        def grads(i, fs=fs):
            at = rows_at(i, 512)
            sd[fs, at] += tn(act[:, fs], gc[:, at])
            sg[fs, at] += tn(dgate[:, fs], xc[:, at])
            su[fs, at] += tn(dup[:, fs], xc[:, at])

        loop(width // 512, grads)


def ffn_weights_out(gate_up_grad, down_grad, sg, su, sd, sems):
    pairs = [(sg, gate_up_grad.at[:, 0, :]), (su, gate_up_grad.at[:, 1, :]), (sd, down_grad)]
    return [pltpu.make_async_copy(a, b, sems.at[i]) for i, (a, b) in enumerate(pairs)]


def ffn_weights_kernel(cap, h2, top, aux, posrow, act, dgate, dup, gate_up_grad, down_grad, sg, su, sd, xc, gc, sems):
    i = pl.program_id(0)
    ffn_weights_compute(cap, i == 0, h2, top, aux, posrow, act, dgate, dup, sg, su, sd, xc, gc)

    @pl.when(i == pl.num_programs(0) - 1)
    def _():
        copies = ffn_weights_out(gate_up_grad, down_grad, sg, su, sd, sems)
        for c in copies:
            c.start()
        for c in copies:
            c.wait()


def ffn_weights_fused(dims, cap, h2, top, aux, posrow, act, dgate, dup, extra, produced, gate_up_grad, down_grad, out, sg, su, sd, xc, gc, sems, load, *refs):
    i = pl.program_id(0)
    place = Place(dims)
    sums = Scatter(dims, place, out, refs)
    rows, width = h2.shape
    copies = ffn_weights_out(gate_up_grad, down_grad, sg, su, sd, sems)
    pl.when(i == 0)(place.greet)

    @pl.when(i < sums.tiles)
    def _():
        tile = sums.tile.at[i % 2]
        fetch = pltpu.make_async_copy(produced.at[rows_at(tile_group(i, dims), rows)], tile.at[:, pl.ds(0, width)], load)
        fetch.start()
        tile[:, width:] = extra[...]
        ffn_weights_compute(cap, i == 0, h2, top, aux, posrow, act, dgate, dup, sg, su, sd, xc, gc)
        fetch.wait()

    @pl.when(i == sums.tiles)
    def _():
        for c in copies:
            c.start()

    pl.when(i == 0)(place.greeted)
    sums.run(i)

    @pl.when(i == sums.steps - 1)
    def _():
        for c in copies:
            c.wait()


def ffn_weights(dims, cid, h2, top, aux, posrow, act, dgate, dup, extra, produced, cap):
    total, width = h2.shape
    hidden = act.shape[1]
    tile = posrow.shape[1] * LANES
    few = tile // LANES * cap
    tiles = total // tile
    at = (lambda i: tile_group(i, dims)) if dims else (lambda i: i)
    row = lambda w: pl.BlockSpec((tile, w), lambda i: (at(i), 0))
    some = pl.BlockSpec((few, hidden), lambda i: (at(i), 0))
    hbm = pl.BlockSpec(memory_space=pl.ANY)
    V = pltpu.VMEM
    scratch = [V((hidden, width), f32)] * 3 + [V((few, width), bf16)] * 2 + [pltpu.SemaphoreType.DMA((3,))]
    out_specs = [hbm, hbm]
    out_shape = [jax.ShapeDtypeStruct((hidden, 2, width), f32), jax.ShapeDtypeStruct((hidden, width), f32)]
    in_specs = [
        row(width), row(width), row(LANES), pl.BlockSpec((1,) + posrow.shape[1:], lambda i: (at(i), 0, 0)), some, some, some,
    ]
    operands = [h2, top, aux, posrow, act, dgate, dup]
    if dims:
        own = tile // 4
        kernel = functools.partial(ffn_weights_fused, dims, cap)
        wide = width + LANES
        operands, in_specs = operands + [extra, produced], in_specs + [row(LANES), hbm]
        out_specs, out_shape = out_specs + [once((own, wide))], out_shape + [jax.ShapeDtypeStruct((own, wide), f32)]
        scratch = scratch + [pltpu.SemaphoreType.DMA] + scatter_scratch(dims, own, wide)
        params = dict(collective_id=cid, has_side_effects=True)
    else:
        kernel, params = functools.partial(ffn_weights_kernel, cap), {}
    return pl.pallas_call(
        kernel,
        grid=(tiles + 2 + dims[0] if dims else tiles,),
        in_specs=in_specs,
        out_specs=out_specs,
        out_shape=out_shape,
        scratch_shapes=scratch,
        compiler_params=pltpu.CompilerParams(vmem_limit_bytes=63 * MB, **params),
    )(*operands)


def ag_kernel(dims, halves, src, out, local_sem, zs, zr, xs, xr, ys, yr, cs, cr):
    nz, nx, ny = dims
    gi = lax.axis_index("grp"); ei = lax.axis_index("exp")
    z, x = gi // nx, gi % nx
    y, c = ei // 2, ei % 2
    ne = ny * 2
    rows = src.shape[0]
    part = rows // halves
    def dev(z_, x_, y_, c_):
        return (z_ * nx + x_, y_ * 2 + c_)
    def slot(z_, x_, y_, c_):
        return (z_ * nx + x_) * ne + y_ * 2 + c_
    barrier = pltpu.get_barrier_semaphore()
    def sig(d):
        pl.semaphore_signal(barrier, inc=1, device_id=d, device_id_type=MESH)
    sig(dev(z, 1 - x, y, c)); sig(dev(z, x, 1 - y, c)); sig(dev(z, x, y, 1 - c))
    @pl.when(z > 0)
    def _(): sig(dev(z - 1, x, y, c))
    @pl.when(z < nz - 1)
    def _(): sig(dev(z + 1, x, y, c))
    pl.semaphore_wait(barrier, 3 + (z > 0).astype(jnp.int32) + (z < nz - 1).astype(jnp.int32))
    own = pltpu.make_async_copy(src, out.at[slot(z, x, y, c)], local_sem)
    own.start()
    span = 2 * nz - 1
    def piece(sl, h):
        return out.at[sl, pl.ds(h * part, part)]
    def copy(sl, h, is_own, ssem, rsem, d):
        s = src.at[pl.ds(h * part, part)] if is_own else piece(sl, h)
        return pltpu.make_async_remote_copy(src_ref=s, dst_ref=piece(sl, h), send_sem=ssem, recv_sem=rsem, device_id=d, device_id_type=MESH)
    def zcopy(h, delta, direction, arriving):
        zz = z - delta * direction
        k = (h * 2 + (0 if direction > 0 else 1)) * nz
        if arriving:
            return copy(slot(zz, x, y, c), h, False, zs.at[k + delta], zr.at[k + delta], dev(z, x, y, c) if False else dev(z, x, y, 1 - c))
        return copy(slot(zz, x, y, c), h, delta == 0, zs.at[k + delta + 1], zr.at[k + delta + 1], dev(z + direction, x, y, c))
    def valid(delta):
        zz = z + delta
        return (zz >= 0) & (zz < nz)
    def when(cond, f):
        pl.when(cond)(f)
    sends = []
    def order(h):
        return ("x", "y") if h % 2 == 0 else ("y", "x")
    def first(h, delta):
        a = order(h)[0]
        sems = (xs, xr) if a == "x" else (ys, yr)
        k = h * 2 * span + delta + nz - 1
        d = dev(z, 1 - x, y, c) if a == "x" else dev(z, x, 1 - y, c)
        return copy(slot(z + delta, x, y, c), h, delta == 0, sems[0].at[k], sems[1].at[k], d), (
            lambda: copy(slot(z + delta, 1 - x if a == "x" else x, 1 - y if a == "y" else y, c), h, False, sems[0].at[k], sems[1].at[k], d))
    def second(h, delta, rel):
        a0, a = order(h)
        sems = (xs, xr) if a == "x" else (ys, yr)
        k = h * 2 * span + (rel * span) + delta + nz - 1
        d = dev(z, 1 - x, y, c) if a == "x" else dev(z, x, 1 - y, c)
        x0 = (1 - x if rel else x) if a0 == "x" else x
        y0 = (1 - y if rel else y) if a0 == "y" else y
        snd = copy(slot(z + delta, x0, y0, c), h, delta == 0 and rel == 0, sems[0].at[k], sems[1].at[k], d)
        x1 = 1 - x if a == "x" else x0
        y1 = 1 - y if a == "y" else y0
        rcv = copy(slot(z + delta, x1, y1, c), h, False, sems[0].at[k], sems[1].at[k], d)
        return snd, rcv
    def core(h, delta, rx, ry):
        k = h * 4 * span + (rx * 2 + ry) * span + delta + nz - 1
        d = dev(z, x, y, 1 - c)
        xx = 1 - x if rx else x
        yy = 1 - y if ry else y
        return (copy(slot(z + delta, xx, yy, c), h, delta == 0 and not rx and not ry, cs.at[k], cr.at[k], d),
                copy(slot(z + delta, xx, yy, 1 - c), h, False, cs.at[k], cr.at[k], d))
    hs = range(halves)
    def have_z(delta):
        for h in hs:
            if delta <= 0:
                when(z < nz - 1, lambda h=h: zcopy(h, -delta, 1, False).start())
            if delta >= 0:
                when(z > 0, lambda h=h: zcopy(h, delta, -1, False).start())
            first(h, delta)[0].start()
            second(h, delta, 0)[0].start()
            core(h, delta, 0, 0)[0].start()
    have_z(0)
    def get_z(delta):
        def f():
            for h in hs:
                zcopy(h, abs(delta), -1 if delta > 0 else 1, True).wait_recv()
            have_z(delta)
        when(valid(delta), f)
    def get_first(delta):
        def f():
            for h in hs:
                first(h, delta)[1]().wait_recv()
                second(h, delta, 1)[0].start()
                rx = 1 if order(h)[0] == "x" else 0
                core(h, delta, rx, 1 - rx)[0].start()
        when(valid(delta), f)
    def get_second(delta):
        def f():
            for h in hs:
                for rel in range(2):
                    second(h, delta, rel)[1].wait_recv()
                    a0, a = order(h)
                    rx = 1 if a == "x" else (rel if a0 == "x" else 0)
                    ry = 1 if a == "y" else (rel if a0 == "y" else 0)
                    core(h, delta, rx, ry)[0].start()
        when(valid(delta), f)
    for step in range(nz + 2):
        for dist, fn in ((step, get_z), (step - 1, get_first), (step - 2, get_second)):
            if 0 <= dist < nz:
                if dist == 0:
                    if fn is not get_z: fn(0)
                else:
                    fn(-dist); fn(dist)
    own.wait()
    for delta in range(-(nz - 1), nz):
        def f(delta=delta):
            for h in hs:
                for rx in range(2):
                    for ry in range(2):
                        a, b = core(h, delta, rx, ry)
                        b.wait_recv(); a.wait_send()
                first(h, delta)[0].wait_send()
                for rel in range(2):
                    second(h, delta, rel)[0].wait_send()
                if delta <= 0:
                    when(z < nz - 1, lambda h=h: zcopy(h, -delta, 1, False).wait_send())
                if delta >= 0:
                    when(z > 0, lambda h=h: zcopy(h, delta, -1, False).wait_send())
        when(valid(delta), f)

def gather_kernel(v, dims, cid, halves=2):
    nz, nx, ny = dims
    n = nz * nx * ny * 2
    span = 2 * nz - 1
    D = pltpu.SemaphoreType.DMA
    return pl.pallas_call(
        functools.partial(ag_kernel, dims, halves),
        out_shape=jax.ShapeDtypeStruct((n,) + v.shape, v.dtype),
        in_specs=[pl.BlockSpec(memory_space=pl.ANY)],
        out_specs=pl.BlockSpec(memory_space=pl.ANY),
        scratch_shapes=[D] + [D((halves * 2 * (nz + 1),))] * 2 + [D((halves * 2 * span,))] * 4 + [D((halves * 4 * span,))] * 2,
        compiler_params=pltpu.CompilerParams(collective_id=cid, has_side_effects=True),
    )(v)


def target_order(nz):
    low, high, order = 0, nz - 1, []
    while low <= high:
        order += [low] if low == high else [low, high]
        low, high = low + 1, high - 1
    return order


def tile_group(i, dims):
    nz, nx, _ = dims
    i = jnp.minimum(i, nz * nx - 1)
    j = i // nx
    t = jnp.where(j % 2 == 0, j // 2, nz - 1 - j // 2)
    return t * nx + i % nx


class Place:
    def __init__(self, dims):
        self.nz, self.nx, self.ny = dims
        gi, ei = lax.axis_index("grp"), lax.axis_index("exp")
        self.z, self.x = gi // self.nx, gi % self.nx
        self.y, self.c = ei // 2, ei % 2

    def device(self, z, x, y, c):
        return (z * self.nx + x, y * 2 + c)

    def core(self):
        return self.device(self.z, self.x, self.y, 1 - self.c)

    def along_x(self):
        return self.device(self.z, 1 - self.x, self.y, self.c)

    def along_y(self):
        return self.device(self.z, self.x, 1 - self.y, self.c)

    def along_z(self, by):
        return self.device(self.z + by, self.x, self.y, self.c)

    def greet(self):
        barrier = pltpu.get_barrier_semaphore()

        def signal(device):
            pl.semaphore_signal(barrier, inc=1, device_id=device, device_id_type=MESH)

        signal(self.along_x())
        signal(self.along_y())
        signal(self.core())
        pl.when(self.z > 0)(lambda: signal(self.along_z(-1)))
        pl.when(self.z < self.nz - 1)(lambda: signal(self.along_z(1)))

    def greeted(self):
        inner = (self.z > 0).astype(jnp.int32) + (self.z < self.nz - 1).astype(jnp.int32)
        pl.semaphore_wait(pltpu.get_barrier_semaphore(), 3 + inner)


def remote(src, dst, sent, came, device):
    return pltpu.make_async_remote_copy(
        src_ref=src, dst_ref=dst, send_sem=sent, recv_sem=came, device_id=device, device_id_type=MESH
    )


def scatter_scratch(dims, rows, width):
    nz, nx, _ = dims
    tiles, half = nz * nx, rows // 2
    D, V = pltpu.SemaphoreType.DMA, lambda *s: pltpu.VMEM(s, bf16)
    return [
        V(2, 4 * rows, width),
        V(4, 2, rows, width),
        V(tiles, 2, rows, width),
        V(tiles, half, width), V(nz, 2, half, width),
        V(nz, half, width), V(nz, half, width),
        V(nz + 1, rows, width),
        D((tiles * 2,)), D((tiles * 2,)), D((tiles,)), D((tiles,)), D((nz * 2,)), D((nz * 2,)),
        D((nz,)), D((nz,)), D((nz,)), D((nz,)), D((nz,)), D((nz + 1,)),
    ]


SCATTER_REFS = 20


class Scatter:
    def __init__(self, dims, place, out, refs):
        self.dims, self.place, self.out = dims, place, out
        (self.tile, self.crv, self.acc, self.ya, self.xb, self.xa, self.yb, self.zv,
         self.cs, self.cr, self.yas, self.yar, self.xbs, self.xbr,
         self.xas, self.xar, self.ybs, self.ybr, self.zs, self.zr) = refs
        self.rows = out.shape[0]
        self.half = self.rows // 2
        self.order = target_order(dims[0])
        self.tiles = dims[0] * dims[1]
        self.steps = self.tiles + 2 + dims[0]

    def add(self, into, *others):
        def step(r, _):
            at = rows_at(r, 16)
            total = others[0][at, :].astype(f32)
            for o in others[1:]:
                total = total + o[at, :].astype(f32)
            into[at, :] = total.astype(into.dtype)
            return 0

        lax.fori_loop(0, into.shape[0] // 16, step, 0)

    def low(self, k, q):
        return self.acc.at[k, q, pl.ds(0, self.half)]

    def high(self, k, q):
        return self.acc.at[k, q, pl.ds(self.half, self.half)]

    def shard(self, k, q, c):
        return self.tile.at[k % 2, rows_at(q * 2 + c, self.rows)]

    def c_core(self, k, q):
        p, s = self.place, k * 2 + q
        return remote(self.shard(k, q, 1 - p.c), self.crv.at[k % 4, q], self.cs.at[s], self.cr.at[s], p.core())

    def c_ya(self, k):
        p = self.place
        return remote(self.low(k, 1 - p.y), self.ya.at[k], self.yas.at[k], self.yar.at[k], p.along_y())

    def c_xb(self, k, q):
        p, j = self.place, k // 2
        s = j * 2 + q
        return remote(self.high(k, q), self.xb.at[j, q], self.xbs.at[s], self.xbr.at[s], p.along_x())

    def c_xa(self, k):
        p, j = self.place, k // 2
        return remote(self.low(k, p.y), self.xa.at[j], self.xas.at[j], self.xar.at[j], p.along_x())

    def c_yb(self, k):
        p, j = self.place, k // 2
        return remote(self.high(k, 1 - p.y), self.yb.at[j], self.ybs.at[j], self.ybr.at[j], p.along_y())

    def c_z(self, k, way):
        p, t = self.place, self.order[k // 2]
        slot = t if way > 0 else jnp.where(p.z - 1 == t, self.dims[0], t)
        return remote(self.acc.at[k, p.y], self.zv.at[slot], self.zs.at[t], self.zr.at[slot], p.along_z(way))

    def z_wait(self, k, slot):
        remote(self.acc.at[k, self.place.y], self.zv.at[slot], self.zs.at[0], self.zr.at[slot], self.place.core()).wait_recv()

    def phase_s(self, k):
        for q in range(2):
            self.c_core(k, q).start()

    def phase_b(self, k):
        p = self.place
        for q in range(2):
            self.c_core(k, q).wait_recv()
            self.add(self.acc.at[k, q], self.shard(k, q, p.c), self.crv.at[k % 4, q])
        self.c_ya(k).start()

        def give():
            for q in range(2):
                self.c_xb(k, q).start()

        pl.when(p.x != k % 2)(give)
        for q in range(2):
            self.c_core(k, q).wait_send()

    def phase_c(self, k):
        p, j = self.place, k // 2

        def give():
            self.c_ya(k).wait_recv()
            self.add(self.low(k, p.y), self.low(k, p.y), self.ya.at[k])
            self.c_xa(k).start()

        def keep():
            self.c_xb(k, 1 - p.y).wait_recv()
            self.add(self.high(k, 1 - p.y), self.high(k, 1 - p.y), self.xb.at[j, 1 - p.y])
            self.c_yb(k).start()

        pl.when(p.x != k % 2)(give)
        pl.when(p.x == k % 2)(keep)

    def phase_d(self, k):
        p, j, t, nz = self.place, k // 2, self.order[k // 2], self.dims[0]

        def keep():
            self.c_ya(k).wait_recv()
            self.c_xa(k).wait_recv()
            self.add(self.low(k, p.y), self.low(k, p.y), self.ya.at[k], self.xa.at[j])
            self.c_xb(k, p.y).wait_recv()
            self.c_yb(k).wait_recv()
            self.add(self.high(k, p.y), self.high(k, p.y), self.xb.at[j, p.y], self.yb.at[j])
            if t > 0:
                pl.when(p.z == 0)(lambda: self.c_z(k, 1).start())
            if t < nz - 1:
                pl.when(p.z == nz - 1)(lambda: self.c_z(k, -1).start())

        pl.when(p.x == k % 2)(keep)

    def phase_e(self, k, h):
        p, t, nz = self.place, self.order[k // 2], self.dims[0]
        mine = p.x == k % 2
        acc = self.acc.at[k, p.y]

        def pass_on(way):
            def run():
                self.z_wait(k, t)
                self.add(acc, acc, self.zv.at[t])
                self.c_z(k, way).start()

            return run

        if h < t:
            pl.when(mine & (p.z == h))(pass_on(1))
        if nz - 1 - h > t:
            pl.when(mine & (p.z == nz - 1 - h))(pass_on(-1))
        if h == max(t, nz - 1 - t):

            def last():
                others = [acc]
                for there, slot in ((t > 0, t), (t < nz - 1, nz)):
                    if there:
                        self.z_wait(k, slot)
                        others.append(self.zv.at[slot])
                self.add(self.out, *others)

            pl.when(mine & (p.z == t))(last)

    def drain(self):
        p = self.place
        for k in range(self.tiles):
            self.c_ya(k).wait_send()

            def give(k=k):
                self.c_xa(k).wait_send()
                for q in range(2):
                    self.c_xb(k, q).wait_send()

            def keep(k=k):
                self.c_yb(k).wait_send()
                pl.when(p.z != self.order[k // 2])(lambda: self.c_z(k, 1).wait_send())

            pl.when(p.x != k % 2)(give)
            pl.when(p.x == k % 2)(keep)

    def run(self, i):
        for step in range(self.steps):

            def phases(step=step):
                for lag, phase in enumerate([self.phase_s, self.phase_b, self.phase_c, self.phase_d]):
                    if 0 <= step - lag < self.tiles:
                        phase(step - lag)
                for h in range(1, self.dims[0]):
                    if 0 <= step - 3 - h < self.tiles:
                        self.phase_e(step - 3 - h, h)
                if step == self.steps - 1:
                    self.drain()

            pl.when(i == step)(phases)


def scatter_kernel_body(dims, src, out, *refs):
    i = pl.program_id(0)
    place = Place(dims)
    s = Scatter(dims, place, out, refs)

    @pl.when(i == 0)
    def _():
        place.greet()
        place.greeted()

    @pl.when(i < s.tiles)
    def _():
        def copy(r):
            at = rows_at(r, 64)
            s.tile[i % 2, at, :] = src[at, :]
        loop(src.shape[0] // 64, copy)

    s.run(i)


def scatter_kernel(p, dims, cid):
    nz, nx, ny = dims
    n, rows, width = p.shape
    groups = nz * nx
    p = p.reshape(n * rows, width)
    return pl.pallas_call(
        functools.partial(scatter_kernel_body, dims),
        grid=(groups + 2 + nz,),
        in_specs=[pl.BlockSpec((4 * rows, width), lambda i: (tile_group(i, dims), 0))],
        out_specs=whole_block((rows, width)),
        out_shape=jax.ShapeDtypeStruct((rows, width), f32),
        scratch_shapes=scatter_scratch(dims, rows, width),
        compiler_params=pltpu.CompilerParams(collective_id=cid, has_side_effects=True, vmem_limit_bytes=60 * MB),
    )(p)


def layout(first, order, group_rows, block):
    places = jnp.arange(group_rows, dtype=jnp.int32)
    anchor = jnp.repeat(order, block, axis=1) * block + places % block
    doc = (anchor >= first).astype(jnp.int32)
    return (anchor, anchor - doc * first)


def rotary_tables(place):
    half = LANES // 2
    freq = jnp.exp(jnp.arange(half, dtype=f32) * (-2.0 * math.log(10000.0) / LANES))
    angle = place.astype(f32)[:, None] * freq[None, :]
    cos, sin = jnp.cos(angle), jnp.sin(angle)
    return (jnp.concatenate([cos, cos], axis=1), jnp.concatenate([-sin, sin], axis=1))


def logit_grad(route, gates, difference, experts):
    moved = gates[:, 0:1] * gates[:, 1:2] * difference
    names = jnp.arange(experts, dtype=jnp.int32)[None, :]
    return jnp.where(route[:, 0:1] == names, moved, 0.0) - jnp.where(
        route[:, 1:2] == names, moved, 0.0
    )


def norm_back(grad_hidden, normed, inverse, gain):
    grad_normed = grad_hidden * gain
    gain_grad = jnp.sum(grad_hidden * normed, axis=0)
    mean_term = jnp.mean(grad_normed * normed, axis=1, keepdims=True)
    return (inverse * (grad_normed - normed * mean_term), gain_grad)


def body(
    dims,
    layer_input,
    out_grad,
    doc_lengths,
    block_order,
    attn_route,
    ffn_route,
    norm_gains,
    kv_master,
    router_master,
    query_master,
    output_master,
    gate_up_master,
    down_master,
):
    own_rows, width = layer_input.shape
    members, groups = lax.axis_size("exp"), lax.axis_size("grp")
    member, group = lax.axis_index("exp"), lax.axis_index("grp")
    experts = members
    capacity = 3 * own_rows // experts
    group_rows = own_rows * members
    total = group_rows * groups
    devices = groups * members
    cw = width // groups
    depth = kv_master.shape[0]
    scale = 1.0 / math.sqrt(LANES)
    me = member.reshape(1).astype(jnp.int32)
    both = ("grp", "exp")

    def gather_all(v, cid):
        if dims is None:
            return lax.all_gather(kept(v), both, axis=0, tiled=True)
        return gather_kernel(v, dims, cid)

    def scatter_all(v, cid):
        v = v.reshape(devices, own_rows, v.shape[-1])
        if dims is None:
            return lax.psum_scatter(v, both, scatter_dimension=0, tiled=False).astype(f32)
        return scatter_kernel(v, dims, cid)

    def summed(parts):
        return jnp.concatenate([scatter_all(v, 0) for v in parts], axis=1) if dims is None else parts[0]

    blocks = block_order.shape[1]
    start_row = member * own_rows
    own_attn_route = lax.dynamic_slice_in_dim(attn_route, start_row, own_rows)
    own_ffn_route = lax.dynamic_slice_in_dim(ffn_route, start_row, own_rows)
    tall = lambda v: jnp.pad(v.astype(bf16), ((0, own_rows - v.shape[0]), (0, 0)))
    first_doc = doc_lengths[:, 0]
    small = jnp.concatenate(
        [
            tall(norm_gains),
            tall(router_master),
            own_attn_route.astype(bf16),
            own_ffn_route.astype(bf16),
            tall(jnp.concatenate([first_doc // 16, first_doc % 16, block_order[0]])[:, None]),
        ],
        axis=1,
    )
    at_route = 2 + 2 * experts
    small = jnp.pad(small, ((0, 0), (0, LANES - small.shape[1])))
    if dims is None:
        tokens = gather_all(layer_input, 1).reshape(total, width)
        extra = gather_all(small, 2).reshape(total, LANES)
    else:
        sent = jnp.concatenate([layer_input, small], axis=1)
        tokens = gather_all(sent, 1).reshape(total, width + LANES)
        extra = tokens[:, width:]

    query_low = query_master[0].astype(bf16)
    kv_low = kv_master.astype(bf16).reshape(depth * 2, groups, cw)
    pieces_out = jnp.concatenate(
        [query_low.reshape(query_low.shape[0], groups, cw), kv_low], axis=0
    ).transpose(1, 0, 2)
    pieces_in = lax.all_to_all(pieces_out, "grp", split_axis=0, concat_axis=0, tiled=True)
    query_weight = pieces_in[:, : query_low.shape[0]].reshape(width, cw)
    kv_all = lax.all_gather(pieces_in[:, query_low.shape[0] :], "exp", axis=1, tiled=False)
    kv_weight = kv_all.reshape(width, 2 * cw)
    output_weight = output_master[0].astype(bf16)

    tables = extra.reshape(devices, own_rows, LANES)[:, :depth, :at_route].reshape(width, at_route)
    gains = tables[:, :2].astype(f32)
    router = tables[:, 2:]
    router_float = router.astype(f32)
    wide = lambda v: jnp.pad(v, ((0, 0), (0, LANES - v.shape[1])))
    routes = extra[:, at_route : at_route + 4].astype(jnp.int32)
    column = extra.reshape(groups, group_rows, LANES)[:, : blocks + 2, at_route + 4].astype(jnp.int32)

    def where_rows_stand(column):
        anchor, place = layout(
            column[:, 0:1] * 16 + column[:, 1:2], column[:, 2:], group_rows, own_rows // 2
        )
        cos, sin = rotary_tables(place.reshape(total))
        meta = jnp.concatenate(
            [anchor.reshape(total, 1), (anchor - place).reshape(total, 1), routes, routes[:, :2]], axis=1
        )
        return cos, sin, meta, jnp.broadcast_to(anchor[:, None, :], (groups, 8, group_rows))

    cos, sin, meta, key_rows = where_rows_stand(column)
    gain_one, gain_two = gains[:, 0], gains[:, 1]
    w_all = jnp.concatenate([query_weight, kv_weight, wide(router[:, :experts])], axis=1)

    qkv, att, aux, attn_sum = attn_forward(
        dims, 3, me, tokens, gain_one[None], w_all, output_weight, cos, sin, meta, key_rows, groups, scale
    )
    own = (group * members + member) * own_rows
    attn_gates = lax.dynamic_slice(aux, (own, 2), (own_rows, 2))
    inputs = layer_input.astype(f32)
    middle = inputs + summed([attn_sum])
    inverse_two = lax.rsqrt(jnp.mean(middle * middle, axis=1, keepdims=True) + epsilon)
    normed_two = middle * inverse_two
    hidden_two = (normed_two * gain_two).astype(bf16)
    if dims is None:
        out_grad, hidden_two = lax.optimization_barrier((out_grad, hidden_two))
    h2 = gather_all(hidden_two, 4).reshape(total, width)
    tops = lax.all_gather(out_grad, both, axis=0, tiled=True)

    named = (routes[:, 2] == member) | (routes[:, 3] == member)
    named = named.reshape(devices, own_rows)
    position = jnp.cumsum(named.astype(jnp.int32), axis=1) - 1
    position = jnp.where(named, position, -1)
    tile_blocks = 4
    position = position.reshape(devices // tile_blocks, tile_blocks, own_rows)
    produced, ffn_aux, act, dgate, dup, *dh2_parts = ffn(
        dims, 5, me, h2, tops, wide(router[:, experts:]), meta, position,
        gate_up_master[0], down_master[0], capacity,
    )
    if dims is None:
        gate_up_grad, down_grad = ffn_weights(
            dims, 0, h2, tops, ffn_aux, position, act, dgate, dup, None, None, capacity
        )
        gate_up_grad, dh2_parts, produced = lax.optimization_barrier((gate_up_grad, dh2_parts, produced))
        back = summed(dh2_parts)
        produced, back = lax.optimization_barrier((produced, back))
        ffn_sum = scatter_all(produced, 0)
        ffn_sum, back = lax.optimization_barrier((ffn_sum, back))
    else:
        back = summed(dh2_parts)
    ffn_gates = lax.dynamic_slice(ffn_aux, (own, 2), (own_rows, 2))
    top_grad = out_grad.astype(f32)
    ffn_logit_grad = logit_grad(own_ffn_route, ffn_gates, back[:, width : width + 1], experts)
    hidden_two_grad = back[:, :width] + jnp.einsum(
        "te,de->td", ffn_logit_grad, router_float[:, experts:], precision=highest
    )
    middle_part, gain_two_grad = norm_back(hidden_two_grad, normed_two, inverse_two, gain_two)
    middle_grad = top_grad + middle_part
    dmid = gather_all(middle_grad.astype(bf16), 6).reshape(total, width)

    if dims is None:
        again, dmid = lax.optimization_barrier((layer_input, dmid))
        tokens = gather_all(again, 9).reshape(total, width)
        column, dmid = lax.optimization_barrier((column, dmid))
        cos, sin, meta, key_rows = where_rows_stand(column)
    dw, do, *dh1_parts = attn_backward(
        dims, 8, dmid, tokens, gain_one[None], qkv, att, aux, cos, sin, meta, key_rows, w_all, output_weight, groups, scale
    )
    back = summed(dh1_parts)
    inverse_one = lax.rsqrt(jnp.mean(inputs * inputs, axis=1, keepdims=True) + epsilon)
    normed_one = inputs * inverse_one
    hidden_one = (normed_one * gain_one).astype(bf16)
    attn_logit_grad = logit_grad(own_attn_route, attn_gates, back[:, width : width + 1], experts)
    hidden_one_grad = back[:, :width] + jnp.einsum(
        "te,de->td", attn_logit_grad, router_float[:, :experts], precision=highest
    )
    input_part, gain_one_grad = norm_back(hidden_one_grad, normed_one, inverse_one, gain_one)
    input_grad = middle_grad + input_part
    route_grad = [
        jnp.einsum("td,te->de", a.astype(f32), b, precision=highest)
        for a, b in ((hidden_one, attn_logit_grad), (hidden_two, ffn_logit_grad))
    ]
    sums = jnp.concatenate(
        [gain_one_grad[:, None], gain_two_grad[:, None], route_grad[0], route_grad[1]], axis=1
    )

    kv_part = dw[cw:].reshape(2 * cw, groups, members, depth)
    kv_part = lax.psum_scatter(kv_part.astype(bf16), "exp", scatter_dimension=2, tiled=False)
    if dims is None:
        sums = lax.psum_scatter(sums, both, scatter_dimension=0, tiled=True)
    else:
        beside = jnp.pad(
            sums.astype(bf16).reshape(devices, depth, sums.shape[1]),
            ((0, 0), (0, own_rows - depth), (0, LANES - sums.shape[1])),
        ).reshape(total, LANES)
        gate_up_grad, down_grad, ffn_sum = ffn_weights(
            dims, 7, h2, tops, ffn_aux, position, act, dgate, dup, beside, produced, capacity
        )
        kv_part, ffn_sum = lax.optimization_barrier((kv_part, ffn_sum))
        sums = ffn_sum[:depth, width : width + sums.shape[1]]
        ffn_sum = ffn_sum[:, :width]
    query_part = dw[:cw].astype(bf16).reshape(cw, groups, width // groups)
    pieces_out = jnp.concatenate(
        [query_part.transpose(1, 0, 2).reshape(groups, -1), kv_part.transpose(1, 0, 2).reshape(groups, -1)],
        axis=1,
    )
    pieces_in = lax.all_to_all(pieces_out, "grp", split_axis=0, concat_axis=0, tiled=True)
    final = middle + ffn_sum
    cut = cw * (width // groups)
    query_grad = pieces_in[:, :cut].reshape(width, width // groups).T.astype(f32)
    kv_grad = (
        pieces_in[:, cut:].reshape(groups, 2, cw, depth).transpose(3, 1, 0, 2).reshape(depth, 2 * width)
    ).astype(f32)
    return (
        final.astype(bf16),
        input_grad,
        sums[:, :2],
        kv_grad,
        sums[:, 2:],
        query_grad[None],
        do[None],
        gate_up_grad[None],
        down_grad[None],
    )


def solution(mesh):
    groups, members = mesh.shape["grp"], mesh.shape["exp"]
    dims = (groups // 2, 2, members // 2) if groups <= 8 and members == 4 else None
    in_specs = (
        P(("grp", "exp"), None),
        P(("grp", "exp"), None),
        P("grp", None),
        P("grp", None),
        P("grp", None),
        P("grp", None),
        P(("grp", "exp"), None),
        P(("grp", "exp"), None),
        P(("grp", "exp"), None),
        P("exp", "grp", None),
        P("exp", "grp", None),
        P("exp", "grp", None, None),
        P("exp", "grp", None),
    )
    out_specs = (
        P(("grp", "exp"), None),
        P(("grp", "exp"), None),
        P(("grp", "exp"), None),
        P(("grp", "exp"), None),
        P(("grp", "exp"), None),
        P("exp", "grp", None),
        P("exp", "grp", None),
        P("exp", "grp", None, None),
        P("exp", "grp", None),
    )
    return jax.shard_map(
        functools.partial(body, dims),
        mesh=mesh,
        in_specs=in_specs,
        out_specs=out_specs,
        check_vma=False,
    )
```

```python
import functools
import math

import jax
import jax.numpy as jnp
from jax import lax
from jax.experimental import pallas as pl
from jax.experimental.pallas import tpu as pltpu
from jax.sharding import PartitionSpec as P

HEADS = 16
LANES = 128
MESH = pl.DeviceIdType.MESH
MB = 1024 * 1024

epsilon = 1e-05
negative = -1e30
highest = lax.Precision.HIGHEST
f32 = jnp.float32
bf16 = jnp.bfloat16


def nn(a, b):
    return jnp.dot(a, b, preferred_element_type=f32)


def nt(a, b):
    return lax.dot_general(a, b, (((1,), (1,)), ((), ())), preferred_element_type=f32)


def tn(a, b):
    return lax.dot_general(a, b, (((0,), (0,)), ((), ())), preferred_element_type=f32)


def loop(count, step):
    def run(i, carry):
        step(i)
        return carry

    lax.fori_loop(0, count, run, 0)


def rows_at(i, size):
    return pl.ds(pl.multiple_of(i * size, size), size)


def kept(v):
    def copy(src, dst):
        dst[...] = src[...]

    return pl.pallas_call(copy, out_shape=jax.ShapeDtypeStruct(v.shape, v.dtype))(v)


def turn(v, cos, sin):
    return v * cos + pltpu.roll(v, LANES // 2, 1) * sin


def gate_columns(logits, r0, r1, me):
    lane = lax.broadcasted_iota(jnp.int32, logits.shape, 1)
    l0 = jnp.sum(jnp.where(lane == r0, logits, 0.0), axis=1, keepdims=True)
    l1 = jnp.sum(jnp.where(lane == r1, logits, 0.0), axis=1, keepdims=True)
    top = jnp.maximum(l0, l1)
    e0, e1 = jnp.exp(l0 - top), jnp.exp(l1 - top)
    g0, g1 = e0 / (e0 + e1), e1 / (e0 + e1)
    weight = jnp.where(r0 == me, g0, 0.0) + jnp.where(r1 == me, g1, 0.0)
    sign = jnp.where(r0 == me, 1.0, 0.0) - jnp.where(r1 == me, 1.0, 0.0)
    return jnp.where(
        lane == 0,
        weight,
        jnp.where(lane == 1, sign, jnp.where(lane == 2, g0, jnp.where(lane == 3, g1, 0.0))),
    )


def attn_forward_kernel(
    cw, scale, me, tokens, gain, w_all, ow, cos, sin, meta, krow, qkv, att, aux, part, h1, inv
):
    count, width = h1.shape
    heads = cw // LANES
    step_rows = 256

    def normalise(i):
        at = rows_at(i, 64)
        v = tokens[at, :].astype(f32)
        inverse = lax.rsqrt(jnp.mean(v * v, axis=1, keepdims=True) + epsilon)
        inv[at, :] = jnp.broadcast_to(inverse, (64, LANES))
        h1[at, :] = (v * inverse * gain[...]).astype(bf16)

    loop(count // 64, normalise)

    def project(i):
        at = rows_at(i, step_rows)
        y = nn(h1[at, :], w_all[...])
        c, s = cos[at, :], sin[at, :]
        for h in range(2 * heads):
            qkv[at, h * LANES : (h + 1) * LANES] = turn(
                y[:, h * LANES : (h + 1) * LANES], c, s
            ).astype(bf16)
        qkv[at, 2 * cw : 3 * cw] = y[:, 2 * cw : 3 * cw].astype(bf16)
        found = gate_columns(y[:, 3 * cw : 3 * cw + LANES], meta[at, 2:3], meta[at, 3:4], me[0])
        lane = lax.broadcasted_iota(jnp.int32, found.shape, 1)
        aux[at, :] = jnp.where(lane == 4, inv[at, :], found)

    loop(count // step_rows, project)

    for h in range(heads):

        def attend(i, h=h):
            at = rows_at(i, LANES)
            q = qkv[at, h * LANES : (h + 1) * LANES]
            k = qkv[:, cw + h * LANES : cw + (h + 1) * LANES]
            v = qkv[:, 2 * cw + h * LANES : 2 * cw + (h + 1) * LANES]
            ak = krow[0, 0:1, :]
            allowed = (ak <= meta[at, 0:1]) & (ak >= meta[at, 1:2])
            scores = jnp.where(allowed, nt(q, k) * scale, negative)
            top = jnp.max(scores, axis=1, keepdims=True)
            raised = jnp.exp(scores - top)
            total = jnp.sum(raised, axis=1, keepdims=True)
            probs = (raised * (1.0 / total)).astype(bf16)
            att[at, h * LANES : (h + 1) * LANES] = nn(probs, v).astype(bf16)
            old = aux[at, :]
            lane = lax.broadcasted_iota(jnp.int32, old.shape, 1)
            aux[at, :] = jnp.where(lane == 8 + h, top + jnp.log(total), old)

        loop(count // LANES, attend)

    def output(i):
        at = rows_at(i, step_rows)
        scaled = (aux[at, 0:1] * att[at, :].astype(f32)).astype(bf16)
        part[at, :] = nn(scaled, ow[...]).astype(bf16)

    loop(count // step_rows, output)


def attn_backward_kernel(
    cw, scale, dmid, tokens, gain, qkv, att, aux, cos, sin, meta, krow, w_all, ow,
    dh1, side, dw, do, h1, datt, watt, dqkv, dk_sum, dv_sum,
):
    count, width = h1.shape
    heads = cw // LANES
    step_rows = 256

    @pl.when(pl.program_id(0) == 0)
    def _():
        dw[...] = jnp.zeros_like(dw)
        do[...] = jnp.zeros_like(do)

    def normalise(i):
        at = rows_at(i, 64)
        h1[at, :] = (tokens[at, :].astype(f32) * aux[at, 4:5] * gain[...]).astype(bf16)

    loop(count // 64, normalise)

    def incoming(i):
        at = rows_at(i, step_rows)
        raw = nt(dmid[at, :], ow[...])
        a = att[at, :].astype(f32)
        weight, sign = aux[at, 0:1], aux[at, 1:2]
        share = sign * jnp.sum(raw * a, axis=1, keepdims=True)
        side[at, :] = jnp.broadcast_to(share, (step_rows, LANES)).astype(bf16)
        datt[at, :] = (weight * raw).astype(bf16)
        watt[at, :] = (weight * a).astype(bf16)

    loop(count // step_rows, incoming)

    def out_weight(i):
        at = rows_at(i, 512)
        do[:, at] += tn(watt[...], dmid[:, at])

    loop(width // 512, out_weight)

    for h in range(heads):
        hs = slice(h * LANES, (h + 1) * LANES)
        ks = slice(cw + h * LANES, cw + (h + 1) * LANES)
        vs = slice(2 * cw + h * LANES, 2 * cw + (h + 1) * LANES)
        dk_sum[...] = jnp.zeros_like(dk_sum)
        dv_sum[...] = jnp.zeros_like(dv_sum)

        def back(i, h=h, hs=hs, ks=ks, vs=vs):
            at = rows_at(i, LANES)
            q, k, v = qkv[at, hs], qkv[:, ks], qkv[:, vs]
            ak = krow[0, 0:1, :]
            allowed = (ak <= meta[at, 0:1]) & (ak >= meta[at, 1:2])
            scores = jnp.where(allowed, nt(q, k) * scale, negative)
            probs = jnp.exp(scores - aux[at, 8 + h : 9 + h])
            grad = datt[at, hs]
            dprobs = nt(grad, v)
            inner = jnp.sum(probs * dprobs, axis=1, keepdims=True)
            dscores = (probs * (dprobs - inner)).astype(bf16)
            dqkv[at, hs] = turn(nn(dscores, k) * scale, cos[at, :], -sin[at, :]).astype(bf16)
            dk_sum[...] += tn(dscores, q)
            dv_sum[...] += tn(probs.astype(bf16), grad)

        loop(count // LANES, back)
        dqkv[:, ks] = turn(dk_sum[...] * scale, cos[...], -sin[...]).astype(bf16)
        dqkv[:, vs] = dv_sum[...].astype(bf16)

    def to_hidden(i):
        at = rows_at(i, step_rows)
        dh1[at, :width] = nt(dqkv[at, :], w_all[:, : 3 * cw]).astype(bf16)

    loop(count // step_rows, to_hidden)

    def weights(i):
        at = rows_at(i, 512)
        dw[:, at] += tn(dqkv[...], h1[:, at])

    loop(width // 512, weights)


def whole_block(shape):
    return pl.BlockSpec(shape, lambda i: (0,) * len(shape))


def once(shape):
    return pl.BlockSpec(shape, lambda i: (0,) * len(shape), pipeline_mode=pl.Buffered(1))


def attn_forward_plain(cw, scale, me, tokens, gain, w_all, ow, cos, sin, meta, krow, gate_up, down, qkv, att, aux, wg, wu, wd, part, h1, inv, *more):
    i = pl.program_id(0)
    Masters(gate_up, down, wg, wu, wd, *more).step(i, 1, 4)
    attn_forward_kernel(cw, scale, me, tokens, gain, w_all, ow, cos, sin, meta, krow, qkv, att, aux, part, h1, inv)


def attn_forward_fused(dims, cw, scale, me, tokens, gain, w_all, ow, cos, sin, meta, krow, gate_up, down, qkv, att, aux, wg, wu, wd, out, h1, inv, stage, low, sems, out_sems, *refs):
    i = pl.program_id(0)
    place = Place(dims)
    sums = Scatter(dims, place, out, refs)
    Masters(gate_up, down, wg, wu, wd, stage, low, sems, out_sems).step(i, sums.tiles, 5)
    pl.when(i == 0)(place.greet)

    @pl.when(i < sums.tiles)
    def _():
        attn_forward_kernel(cw, scale, me, tokens, gain, w_all, ow, cos, sin, meta, krow, qkv, att, aux, sums.tile.at[i % 2], h1, inv)

    pl.when(i == 0)(place.greeted)
    sums.run(i)


def attn_forward(dims, cid, me, tokens, gain, w_all, ow, cos, sin, meta, krow, gate_up, down, groups, scale):
    total = tokens.shape[0]
    cw, width = ow.shape
    count = total // groups
    at = (lambda i: tile_group(i, dims)) if dims else (lambda i: i)
    row = lambda w: pl.BlockSpec((count, w), lambda i: (at(i), 0))
    hbm = pl.BlockSpec(memory_space=pl.ANY)
    shape = lambda w, t: jax.ShapeDtypeStruct((total, w), t)
    if dims:
        own = count // 4
        kernel = functools.partial(attn_forward_fused, dims, cw, scale)
        last_spec, last_shape = whole_block((own, width)), jax.ShapeDtypeStruct((own, width), f32)
        params, more = dict(collective_id=cid, has_side_effects=True), scatter_scratch(dims, own, width)
    else:
        kernel = functools.partial(attn_forward_plain, cw, scale)
        last_spec, last_shape, params, more = row(width), shape(width, bf16), {}, []
    return pl.pallas_call(
        kernel,
        grid=(groups + 2 + dims[0] if dims else groups,),
        in_specs=[
            pl.BlockSpec(memory_space=pltpu.SMEM), row(width), whole_block(gain.shape),
            once(w_all.shape), once(ow.shape), row(LANES), row(LANES), row(8),
            pl.BlockSpec((1, 8, count), lambda i: (at(i), 0, 0)), hbm, hbm,
        ],
        out_specs=[row(3 * cw), row(cw), row(LANES), hbm, hbm, hbm, last_spec],
        out_shape=[shape(3 * cw, bf16), shape(cw, bf16), shape(LANES, f32)] + [jax.ShapeDtypeStruct(down.shape, bf16)] * 3 + [last_shape],
        scratch_shapes=[pltpu.VMEM((count, width), bf16), pltpu.VMEM((count, LANES), f32)] + masters_scratch(down.shape[0], width) + more,
        compiler_params=pltpu.CompilerParams(vmem_limit_bytes=60 * MB, **params),
    )(me, tokens, gain, w_all, ow, cos, sin, meta, krow, gate_up, down)


def attn_backward_plain(cw, scale, dmid, tokens, gain, qkv, att, aux, cos, sin, meta, krow, w_all, ow, dw_hbm, do_hbm, dh1, side, dw, do, sems, *more):
    attn_backward_kernel(cw, scale, dmid, tokens, gain, qkv, att, aux, cos, sin, meta, krow, w_all, ow, dh1, side, dw, do, *more)
    pl.when(pl.program_id(0) == pl.num_programs(0) - 1)(lambda: attn_weights_out(dw, do, dw_hbm, do_hbm, sems))


def attn_weights_out(dw, do, dw_hbm, do_hbm, sems):
    copies = [pltpu.make_async_copy(a, b, sems.at[n]) for n, (a, b) in enumerate(((dw, dw_hbm), (do, do_hbm)))]
    for c in copies:
        c.start()
    for c in copies:
        c.wait()


def attn_backward_fused(dims, cw, scale, dmid, tokens, gain, qkv, att, aux, cos, sin, meta, krow, w_all, ow, dw_hbm, do_hbm, out, dw, do, sems, h1, datt, watt, dqkv, dk_sum, dv_sum, *refs):
    i = pl.program_id(0)
    place = Place(dims)
    sums = Scatter(dims, place, out, refs)
    pl.when(i == 0)(place.greet)

    @pl.when(i < sums.tiles)
    def _():
        tile, side = sums.tile.at[i % 2], sums.tile.at[i % 2, :, pl.ds(dmid.shape[1], LANES)]
        attn_backward_kernel(cw, scale, dmid, tokens, gain, qkv, att, aux, cos, sin, meta, krow, w_all, ow, tile, side, dw, do, h1, datt, watt, dqkv, dk_sum, dv_sum)

    pl.when(i == 0)(place.greeted)
    sums.run(i)
    pl.when(i == sums.tiles)(lambda: attn_weights_out(dw, do, dw_hbm, do_hbm, sems))


def attn_backward(dims, cid, dmid, tokens, gain, qkv, att, aux, cos, sin, meta, krow, w_all, ow, groups, scale):
    total, width = dmid.shape
    cw = ow.shape[0]
    count = total // groups
    at = (lambda i: tile_group(i, dims)) if dims else (lambda i: i)
    row = lambda w: pl.BlockSpec((count, w), lambda i: (at(i), 0))
    wide = width + LANES
    hbm = pl.BlockSpec(memory_space=pl.ANY)
    if dims:
        own = count // 4
        kernel = functools.partial(attn_backward_fused, dims, cw, scale)
        last_spec, last_shape = [whole_block((own, wide))], [jax.ShapeDtypeStruct((own, wide), f32)]
        params, more = dict(collective_id=cid, has_side_effects=True), scatter_scratch(dims, own, wide)
    else:
        kernel = functools.partial(attn_backward_plain, cw, scale)
        last_spec = [row(width), row(LANES)]
        last_shape = [jax.ShapeDtypeStruct((total, w), bf16) for w in (width, LANES)]
        params, more = {}, []
    return pl.pallas_call(
        kernel,
        grid=(groups + 2 + dims[0] if dims else groups,),
        in_specs=[
            row(width), row(width), whole_block(gain.shape), row(3 * cw), row(cw), row(LANES), row(LANES), row(LANES), row(8),
            pl.BlockSpec((1, 8, count), lambda i: (at(i), 0, 0)),
            once(w_all.shape), once(ow.shape),
        ],
        out_specs=[hbm, hbm] + last_spec,
        out_shape=[jax.ShapeDtypeStruct((3 * cw, width), f32), jax.ShapeDtypeStruct((cw, width), f32)] + last_shape,
        scratch_shapes=[
            pltpu.VMEM((3 * cw, width), f32), pltpu.VMEM((cw, width), f32), pltpu.SemaphoreType.DMA((2,)),
            pltpu.VMEM((count, width), bf16), pltpu.VMEM((count, cw), bf16), pltpu.VMEM((count, cw), bf16), pltpu.VMEM((count, 3 * cw), bf16),
            pltpu.VMEM((count, LANES), f32), pltpu.VMEM((count, LANES), f32),
        ] + more,
        compiler_params=pltpu.CompilerParams(vmem_limit_bytes=62 * MB, **params),
    )(dmid, tokens, gain, qkv, att, aux, cos, sin, meta, krow, w_all, ow)


def pieces(total, size):
    return [(at, min(size, total - at)) for at in range(0, total, size)]


def chosen(posrow, i, cap):
    slot = lax.broadcasted_iota(jnp.int32, (cap, LANES), 0)
    return (slot == posrow[0, pl.ds(i, 1), :]).astype(bf16)


def is_dense(cap):
    return 2 * cap > LANES


def chosen_scratch(cap, few, width):
    return [pltpu.VMEM((16 if is_dense(cap) else few, width), bf16), pltpu.VMEM((few, width), bf16)]


def gated(top, weight, at, cs):
    return (weight * top[at, cs].astype(f32)).astype(bf16)


def compact(cap, h2, top, posrow, weight, xc, gc):
    def block(i):
        at, to = rows_at(i, LANES), rows_at(i, cap)
        w = weight(at)
        choose = None if is_dense(cap) else chosen(posrow, i, cap)
        for start, size in pieces(h2.shape[1], 512):
            cs = slice(start, start + size)
            if is_dense(cap):
                gc[at, cs] = gated(top, w, at, cs)
            else:
                xc[to, cs] = nn(choose, h2[at, cs]).astype(bf16)
                gc[to, cs] = nn(choose, gated(top, w, at, cs)).astype(bf16)

    loop(h2.shape[0] // LANES, block)


def stage_rows(hidden):
    return max(r for r in range(16, 177, 16) if hidden % r == 0)


class Masters:
    def __init__(self, gate_up, down, wg, wu, wd, stage, low, sems, out_sems):
        part = stage.shape[1]
        self.jobs = [
            (src.at[pl.ds(n * part, part)], dst.at[pl.ds(n * part, part)])
            for n in range(down.shape[0] // part)
            for src, dst in ((gate_up.at[:, 0, :], wg), (gate_up.at[:, 1, :], wu), (down, wd))
        ]
        self.stage, self.low, self.sems, self.out_sems = stage, low, sems, out_sems

    def load(self, n):
        return pltpu.make_async_copy(self.jobs[n][0], self.stage.at[n % 2], self.sems.at[n % 2])

    def store(self, n):
        return pltpu.make_async_copy(self.low.at[n % 2], self.jobs[n][1], self.out_sems.at[n % 2])

    def run(self, first, last):
        for n in range(first, last):
            self.load(n).wait()
            if n >= 2:
                self.store(n - 2).wait()

            def cast(r, n=n):
                at = rows_at(r, 16)
                self.low[n % 2, at, :] = self.stage[n % 2, at, :].astype(bf16)

            loop(self.low.shape[1] // 16, cast)
            self.store(n).start()
            if n + 2 < len(self.jobs):
                self.load(n + 2).start()

    def finish(self):
        for n in range(max(len(self.jobs) - 2, 0), len(self.jobs)):
            self.store(n).wait()

    def step(self, i, first_step, steps):
        count = len(self.jobs)

        @pl.when(i == first_step - 1)
        def _():
            for n in range(min(2, count)):
                self.load(n).start()

        for k in range(steps):
            pl.when(i == first_step + k)(
                lambda k=k: self.run(count * k // steps, count * (k + 1) // steps)
            )
        pl.when(i == first_step + steps - 1)(self.finish)


def masters_scratch(hidden, width):
    part = stage_rows(hidden)
    D = pltpu.SemaphoreType.DMA
    return [pltpu.VMEM((2, part, width), f32), pltpu.VMEM((2, part, width), bf16), D((2,)), D((2,))]


def ffn_compute(cap, me, h2, top, router, meta, posrow, produced, dh2, side, aux, act, dgate, dup, wg, wu, wd, xc, gc):
    rows, width = h2.shape
    hidden = wd.shape[0]
    blocks = rows // LANES

    aux[...] = gate_columns(nn(h2[...], router[...]), meta[:, 4:5], meta[:, 5:6], me[0])
    compact(cap, h2, top, posrow, lambda at: aux[at, 0:1], xc, gc)
    xs = h2 if is_dense(cap) else xc

    for start, size in pieces(hidden, 256):
        fs = slice(start, start + size)
        gate, up, dact = nt(xs[...], wg[fs, :]), nt(xs[...], wu[fs, :]), nt(gc[...], wd[fs, :])
        sigmoid = 1.0 / (1.0 + jnp.exp(-gate))
        silu = gate * sigmoid
        act[:, fs] = (silu * up).astype(bf16)
        dgate[:, fs] = (dact * up * sigmoid * (1.0 + gate * (1.0 - sigmoid))).astype(bf16)
        dup[:, fs] = (dact * silu).astype(bf16)

    if is_dense(cap):
        shares = jnp.zeros((rows, 1), f32)
        for start, size in pieces(width, 512):
            cs = slice(start, start + size)
            y = nn(act[...], wd[:, cs])
            shares = shares + jnp.sum(y * top[:, cs].astype(f32), axis=1, keepdims=True)
            produced[:, cs] = (aux[:, 0:1] * y).astype(bf16)
            dh2[:, cs] = (nn(dgate[...], wg[:, cs]) + nn(dup[...], wu[:, cs])).astype(bf16)
        side[...] = jnp.broadcast_to(aux[:, 1:2] * shares, (rows, LANES)).astype(bf16)
        return

    yc, bc = gc, xc

    def results(i):
        at = rows_at(i, 512)
        yc[:, at] = nn(act[...], wd[:, at]).astype(bf16)
        bc[:, at] = (nn(dgate[...], wg[:, at]) + nn(dup[...], wu[:, at])).astype(bf16)

    loop(width // 512, results)

    def scatter(i):
        at, of = rows_at(i, LANES), rows_at(i, cap)
        choose = chosen(posrow, i, cap)
        found = aux[at, :]
        share = jnp.zeros((LANES, 1), f32)
        for start, size in pieces(width, 512):
            cs = slice(start, start + size)
            y = tn(choose, yc[of, cs])
            share = share + jnp.sum(y * top[at, cs].astype(f32), axis=1, keepdims=True)
            produced[at, cs] = (found[:, 0:1] * y).astype(bf16)
            dh2[at, cs] = tn(choose, bc[of, cs]).astype(bf16)
        side[at, :] = jnp.broadcast_to(found[:, 1:2] * share, (LANES, LANES)).astype(bf16)

    loop(blocks, scatter)


def ffn_kernel(cap, me, h2, top, router, meta, posrow, wg, wu, wd, produced, aux, act, dgate, dup, dh2, side, xc, gc):
    ffn_compute(cap, me, h2, top, router, meta, posrow, produced, dh2, side, aux, act, dgate, dup, wg, wu, wd, xc, gc)


def ffn_fused_kernel(dims, cap, me, h2, top, router, meta, posrow, wg, wu, wd, produced, aux, act, dgate, dup, out, xc, gc, *refs):
    i = pl.program_id(0)
    place = Place(dims)
    sums = Scatter(dims, place, out, refs)

    pl.when(i == 0)(place.greet)

    @pl.when(i < sums.tiles)
    def _():
        tile, side = sums.tile.at[i % 2], sums.tile.at[i % 2, :, pl.ds(h2.shape[1], LANES)]
        ffn_compute(cap, me, h2, top, router, meta, posrow, produced, tile, side, aux, act, dgate, dup, wg, wu, wd, xc, gc)

    pl.when(i == 0)(place.greeted)
    sums.run(i)


def ffn(dims, cid, me, h2, top, router, meta, posrow, wg, wu, wd, cap):
    total, width = h2.shape
    hidden = wd.shape[0]
    tile = posrow.shape[1] * LANES
    few = tile if is_dense(cap) else tile // LANES * cap
    tiles = total // tile
    at = (lambda i: tile_group(i, dims)) if dims else (lambda i: i)
    row = lambda w: pl.BlockSpec((tile, w), lambda i: (at(i), 0))
    some = pl.BlockSpec((few, hidden), lambda i: (at(i), 0))
    own = total // (dims[0] * dims[1] * dims[2] * 2) if dims else 0
    wide = width + LANES
    if dims:
        kernel = functools.partial(ffn_fused_kernel, dims, cap)
        last_spec, last_shape = [whole_block((own, wide))], [jax.ShapeDtypeStruct((own, wide), f32)]
        params = dict(collective_id=cid, has_side_effects=True)
    else:
        kernel = functools.partial(ffn_kernel, cap)
        last_spec = [row(width), row(LANES)]
        last_shape = [jax.ShapeDtypeStruct((total, w), bf16) for w in (width, LANES)]
        params = {}
    return pl.pallas_call(
        kernel,
        grid=(tiles + 2 + dims[0] if dims else tiles,),
        in_specs=[
            pl.BlockSpec(memory_space=pltpu.SMEM), row(width), row(width), whole_block(router.shape), row(8),
            pl.BlockSpec((1,) + posrow.shape[1:], lambda i: (at(i), 0, 0)), once(wg.shape), once(wu.shape), once(wd.shape),
        ],
        out_specs=[row(width), row(LANES), some, some, some] + last_spec,
        out_shape=[
            jax.ShapeDtypeStruct((total, width), bf16),
            jax.ShapeDtypeStruct((total, LANES), f32),
        ] + [jax.ShapeDtypeStruct((tiles * few, hidden), bf16)] * 3 + last_shape,
        scratch_shapes=chosen_scratch(cap, few, width)
        + (scatter_scratch(dims, own, wide) if dims else []),
        compiler_params=pltpu.CompilerParams(vmem_limit_bytes=63 * MB, **params),
    )(me, h2, top, router, meta, posrow, wg, wu, wd)


def ffn_weights_compute(cap, first, h2, top, aux, posrow, act, dgate, dup, sg, su, sd, xc, gc):
    width = h2.shape[1]
    hidden = sd.shape[0]

    @pl.when(first)
    def _():
        for s in (sg, su, sd):

            def clear(i, s=s):
                s[rows_at(i, 32), :] = jnp.zeros((32, width), f32)

            loop(hidden // 32, clear)

    compact(cap, h2, top, posrow, lambda at: aux[at, 0:1], xc, gc)
    xs = h2 if is_dense(cap) else xc
    for start, size in pieces(hidden, 256):
        fs = slice(start, start + size)

        def grads(i, fs=fs):
            at = rows_at(i, 512)
            sd[fs, at] += tn(act[:, fs], gc[:, at])
            sg[fs, at] += tn(dgate[:, fs], xs[:, at])
            su[fs, at] += tn(dup[:, fs], xs[:, at])

        loop(width // 512, grads)


def ffn_weights_out(gate_up_grad, down_grad, sg, su, sd, sems):
    pairs = [(sg, gate_up_grad.at[:, 0, :]), (su, gate_up_grad.at[:, 1, :]), (sd, down_grad)]
    return [pltpu.make_async_copy(a, b, sems.at[i]) for i, (a, b) in enumerate(pairs)]


def ffn_weights_kernel(cap, h2, top, aux, posrow, act, dgate, dup, gate_up_grad, down_grad, sg, su, sd, xc, gc, sems):
    i = pl.program_id(0)
    ffn_weights_compute(cap, i == 0, h2, top, aux, posrow, act, dgate, dup, sg, su, sd, xc, gc)

    @pl.when(i == pl.num_programs(0) - 1)
    def _():
        copies = ffn_weights_out(gate_up_grad, down_grad, sg, su, sd, sems)
        for c in copies:
            c.start()
        for c in copies:
            c.wait()


class GradExchange:
    def __init__(self, dims, place, q_src, kv_src, q_out, kv_out, other_out, own, landed, along, refs):
        groups = dims[0] * dims[1]
        qs, qr, ql, ks, kr, kl, self.ls, self.ss, self.sr = refs
        self.place, self.kv_src, self.kv_out, self.other_out = place, kv_src, kv_out, other_out
        self.own, self.landed, self.along = own, landed, along
        self.query = Exchange(groups, q_src, q_out, qs, qr, ql)
        self.kv = Exchange(groups, own.at[place.y], kv_out, ks, kr, kl)

    def load(self):
        return pltpu.make_async_copy(self.kv_src.at[self.place.c], self.own, self.ls)

    def c_core(self):
        p = self.place
        return remote(self.kv_src.at[1 - p.c], self.landed, self.ss.at[0], self.sr.at[0], p.core())

    def c_y(self):
        p = self.place
        return remote(self.own.at[1 - p.y], self.along, self.ss.at[1], self.sr.at[1], p.along_y())

    def c_last(self):
        return remote(self.kv_out, self.other_out, self.ss.at[2], self.sr.at[2], self.place.core())

    def add(self, into, other):
        groups, rows, _ = into.shape

        def step(n):
            at = rows_at(n % (rows // 64), 64)
            g = n // (rows // 64)
            into[g, at, :] = (into[g, at, :].astype(f32) + other[g, at, :].astype(f32)).astype(bf16)

        loop(groups * (rows // 64), step)

    def step(self, i, last):
        @pl.when(i == 0)
        def _():
            self.c_core().start()
            self.load().start()
            self.query.start()

        @pl.when(i == 1)
        def _():
            self.load().wait()
            self.c_core().wait_recv()
            for n in range(2):
                self.add(self.own.at[n], self.landed.at[n])
            self.c_y().start()

        @pl.when(i == 3)
        def _():
            self.c_y().wait_recv()
            self.add(self.own.at[self.place.y], self.along)
            self.kv.start()

        @pl.when(i == 7)
        def _():
            self.kv.wait_came()
            self.c_last().start()

        @pl.when(i == last)
        def _():
            self.query.wait_came()
            self.c_last().wait_recv()
            for c in (self.c_core(), self.c_y(), self.c_last()):
                c.wait_send()
            self.query.wait_sent()
            self.kv.wait_sent()


def grad_exchange_scratch(groups, cw):
    D = pltpu.SemaphoreType.DMA
    V = lambda *s: pltpu.VMEM(s + (groups, cw, LANES), bf16)
    return [V(2), V(2), V()], exchange_scratch(groups) * 2 + [D, D((3,)), D((3,))]


def ffn_weights_fused(dims, cap, h2, top, aux, posrow, act, dgate, dup, extra, produced, q_src, kv_src, gate_up_grad, down_grad, out, q_out, kv_out, other_out, sg, su, sd, xc, gc, sems, load, own, landed, along, *refs):
    i = pl.program_id(0)
    place = Place(dims)
    sums = Scatter(dims, place, out, refs[:SCATTER_REFS])
    grads = GradExchange(dims, place, q_src, kv_src, q_out, kv_out, other_out, own, landed, along, refs[SCATTER_REFS:])
    rows, width = h2.shape
    copies = ffn_weights_out(gate_up_grad, down_grad, sg, su, sd, sems)

    @pl.when(i == 0)
    def _():
        place.greet_plane()
        place.greeted_plane()

    grads.step(i, sums.steps - 1)

    @pl.when(i < sums.tiles)
    def _():
        tile = sums.tile.at[i % 2]
        fetch = pltpu.make_async_copy(produced.at[rows_at(tile_group(i, dims), rows)], tile.at[:, pl.ds(0, width)], load)
        fetch.start()
        tile[:, width:] = extra[...]
        ffn_weights_compute(cap, i == 0, h2, top, aux, posrow, act, dgate, dup, sg, su, sd, xc, gc)
        fetch.wait()

    @pl.when(i == sums.tiles)
    def _():
        for c in copies:
            c.start()

    sums.run(i)

    @pl.when(i == sums.steps - 1)
    def _():
        for c in copies:
            c.wait()


def ffn_weights(dims, cid, h2, top, aux, posrow, act, dgate, dup, extra, produced, q_src, kv_src, cap):
    total, width = h2.shape
    hidden = act.shape[1]
    tile = posrow.shape[1] * LANES
    few = tile if is_dense(cap) else tile // LANES * cap
    tiles = total // tile
    at = (lambda i: tile_group(i, dims)) if dims else (lambda i: i)
    row = lambda w: pl.BlockSpec((tile, w), lambda i: (at(i), 0))
    some = pl.BlockSpec((few, hidden), lambda i: (at(i), 0))
    hbm = pl.BlockSpec(memory_space=pl.ANY)
    V = pltpu.VMEM
    scratch = [V((hidden, width), f32)] * 3 + chosen_scratch(cap, few, width) + [pltpu.SemaphoreType.DMA((3,))]
    out_specs = [hbm, hbm]
    out_shape = [jax.ShapeDtypeStruct((hidden, 2, width), f32), jax.ShapeDtypeStruct((hidden, width), f32)]
    in_specs = [
        row(width), row(width), row(LANES), pl.BlockSpec((1,) + posrow.shape[1:], lambda i: (at(i), 0, 0)), some, some, some,
    ]
    operands = [h2, top, aux, posrow, act, dgate, dup]
    if dims:
        own = tile // 4
        kernel = functools.partial(ffn_weights_fused, dims, cap)
        wide = width + LANES
        operands, in_specs = operands + [extra, produced, q_src, kv_src], in_specs + [row(LANES), hbm, hbm, hbm]
        groups, cw = q_src.shape[:2]
        out_specs = out_specs + [once((own, wide)), hbm, hbm, hbm]
        out_shape = out_shape + [jax.ShapeDtypeStruct((own, wide), f32), jax.ShapeDtypeStruct(q_src.shape, bf16)]
        out_shape = out_shape + [jax.ShapeDtypeStruct((groups, cw, LANES), bf16)] * 2
        buffers, marks = grad_exchange_scratch(groups, cw)
        scratch = scratch + [pltpu.SemaphoreType.DMA] + buffers + scatter_scratch(dims, own, wide) + marks
        params = dict(collective_id=cid, has_side_effects=True)
    else:
        kernel, params = functools.partial(ffn_weights_kernel, cap), {}
    return pl.pallas_call(
        kernel,
        grid=(tiles + 2 + dims[0] if dims else tiles,),
        in_specs=in_specs,
        out_specs=out_specs,
        out_shape=out_shape,
        scratch_shapes=scratch,
        compiler_params=pltpu.CompilerParams(vmem_limit_bytes=63 * MB, **params),
    )(*operands)


class Exchange:
    def __init__(self, groups, src, dst, sent, came, local):
        self.groups, self.src, self.dst, self.sent, self.came, self.local = groups, src, dst, sent, came, local
        self.gi, self.ei = lax.axis_index("grp"), lax.axis_index("exp")

    def peers(self):
        return [((self.gi + r) % self.groups, self.ei) for r in range(1, self.groups)]

    def copy(self, r, arriving=False):
        to, of = (self.gi + r) % self.groups, (self.gi + self.groups - r) % self.groups
        return pltpu.make_async_remote_copy(
            src_ref=self.src.at[to], dst_ref=self.dst.at[of if arriving else self.gi],
            send_sem=self.sent.at[r], recv_sem=self.came.at[r], device_id=(to, self.ei), device_id_type=MESH,
        )

    def own(self):
        return pltpu.make_async_copy(self.src.at[self.gi], self.dst.at[self.gi], self.local)

    def start(self):
        self.own().start()
        for r in range(1, self.groups):
            self.copy(r).start()

    def wait_came(self):
        self.own().wait()
        for r in range(1, self.groups):
            self.copy(r, True).wait_recv()

    def wait_sent(self):
        for r in range(1, self.groups):
            self.copy(r).wait_send()


def exchange_scratch(groups):
    D = pltpu.SemaphoreType.DMA
    return [D((groups,)), D((groups,)), D]


def ag_kernel(dims, halves, shared_rows, *refs):
    if shared_rows:
        src, ex_src, out, ex_out, shared, local_sem, zs, zr, xs, xr, ys, yr, cs, cr, exs, exr, exl, shs, shr, shl = refs
        ex = Exchange(dims[0] * dims[1], ex_src, ex_out, exs, exr, exl)
    else:
        src, out, local_sem, zs, zr, xs, xr, ys, yr, cs, cr = refs
        ex = None
    nz, nx, ny = dims
    gi = lax.axis_index("grp"); ei = lax.axis_index("exp")
    z, x = gi // nx, gi % nx
    y, c = ei // 2, ei % 2
    ne = ny * 2
    rows = src.shape[0]
    part = rows // halves
    def dev(z_, x_, y_, c_):
        return (z_ * nx + x_, y_ * 2 + c_)
    def slot(z_, x_, y_, c_):
        return (z_ * nx + x_) * ne + y_ * 2 + c_
    barrier = pltpu.get_barrier_semaphore()
    def sig(d):
        pl.semaphore_signal(barrier, inc=1, device_id=d, device_id_type=MESH)
    sig(dev(z, x, 1 - y, c))
    sig(dev(z, x, y, 1 - c))
    if ex is None:
        sig(dev(z, 1 - x, y, c))
        pl.when(z > 0)(lambda: sig(dev(z - 1, x, y, c)))
        pl.when(z < nz - 1)(lambda: sig(dev(z + 1, x, y, c)))
        pl.semaphore_wait(barrier, 3 + (z > 0).astype(jnp.int32) + (z < nz - 1).astype(jnp.int32))
    else:
        for peer in ex.peers():
            sig(peer)
        pl.semaphore_wait(barrier, 2 + len(ex.peers()))
    own = pltpu.make_async_copy(src, out.at[slot(z, x, y, c)], local_sem)
    own.start()
    span = 2 * nz - 1
    def piece(sl, h):
        return out.at[sl, pl.ds(h * part, part)]
    def copy(sl, h, is_own, ssem, rsem, d):
        s = src.at[pl.ds(h * part, part)] if is_own else piece(sl, h)
        return pltpu.make_async_remote_copy(src_ref=s, dst_ref=piece(sl, h), send_sem=ssem, recv_sem=rsem, device_id=d, device_id_type=MESH)
    def zcopy(h, delta, direction, arriving):
        zz = z - delta * direction
        k = (h * 2 + (0 if direction > 0 else 1)) * nz
        if arriving:
            return copy(slot(zz, x, y, c), h, False, zs.at[k + delta], zr.at[k + delta], dev(z, x, y, c) if False else dev(z, x, y, 1 - c))
        return copy(slot(zz, x, y, c), h, delta == 0, zs.at[k + delta + 1], zr.at[k + delta + 1], dev(z + direction, x, y, c))
    def valid(delta):
        zz = z + delta
        return (zz >= 0) & (zz < nz)
    def when(cond, f):
        pl.when(cond)(f)
    sends = []
    def order(h):
        return ("x", "y") if h % 2 == 0 else ("y", "x")
    def first(h, delta):
        a = order(h)[0]
        sems = (xs, xr) if a == "x" else (ys, yr)
        k = h * 2 * span + delta + nz - 1
        d = dev(z, 1 - x, y, c) if a == "x" else dev(z, x, 1 - y, c)
        return copy(slot(z + delta, x, y, c), h, delta == 0, sems[0].at[k], sems[1].at[k], d), (
            lambda: copy(slot(z + delta, 1 - x if a == "x" else x, 1 - y if a == "y" else y, c), h, False, sems[0].at[k], sems[1].at[k], d))
    def second(h, delta, rel):
        a0, a = order(h)
        sems = (xs, xr) if a == "x" else (ys, yr)
        k = h * 2 * span + (rel * span) + delta + nz - 1
        d = dev(z, 1 - x, y, c) if a == "x" else dev(z, x, 1 - y, c)
        x0 = (1 - x if rel else x) if a0 == "x" else x
        y0 = (1 - y if rel else y) if a0 == "y" else y
        snd = copy(slot(z + delta, x0, y0, c), h, delta == 0 and rel == 0, sems[0].at[k], sems[1].at[k], d)
        x1 = 1 - x if a == "x" else x0
        y1 = 1 - y if a == "y" else y0
        rcv = copy(slot(z + delta, x1, y1, c), h, False, sems[0].at[k], sems[1].at[k], d)
        return snd, rcv
    def core(h, delta, rx, ry):
        k = h * 4 * span + (rx * 2 + ry) * span + delta + nz - 1
        d = dev(z, x, y, 1 - c)
        xx = 1 - x if rx else x
        yy = 1 - y if ry else y
        return (copy(slot(z + delta, xx, yy, c), h, delta == 0 and not rx and not ry, cs.at[k], cr.at[k], d),
                copy(slot(z + delta, xx, yy, 1 - c), h, False, cs.at[k], cr.at[k], d))
    hs = range(halves)
    def have_z(delta):
        for h in hs:
            if delta <= 0:
                when(z < nz - 1, lambda h=h: zcopy(h, -delta, 1, False).start())
            if delta >= 0:
                when(z > 0, lambda h=h: zcopy(h, delta, -1, False).start())
            first(h, delta)[0].start()
            second(h, delta, 0)[0].start()
            core(h, delta, 0, 0)[0].start()
    have_z(0)
    def share(n):
        part = ex_out.at[:, pl.ds(ex_out.shape[1] - shared_rows, shared_rows)]
        number = (1 - y if n == 2 else y) * 2 + c
        return pltpu.make_async_remote_copy(
            src_ref=shared.at[number] if n == 2 else part, dst_ref=shared.at[number],
            send_sem=shs.at[n], recv_sem=shr.at[n],
            device_id=dev(z, x, 1 - y, c) if n == 0 else dev(z, x, y, 1 - c), device_id_type=MESH,
        )
    def share_own():
        part = ex_out.at[:, pl.ds(ex_out.shape[1] - shared_rows, shared_rows)]
        return pltpu.make_async_copy(part, shared.at[y * 2 + c], shl)
    def shared_came(n):
        number = ((1 - y) * 2 + c, y * 2 + 1 - c, (1 - y) * 2 + 1 - c)[n]
        return pltpu.make_async_remote_copy(
            src_ref=shared.at[number], dst_ref=shared.at[number], send_sem=shs.at[n], recv_sem=shr.at[n],
            device_id=dev(z, x, y, 1 - c), device_id_type=MESH,
        )
    if ex is not None:
        ex.start()
    def get_z(delta):
        def f():
            for h in hs:
                zcopy(h, abs(delta), -1 if delta > 0 else 1, True).wait_recv()
            have_z(delta)
        when(valid(delta), f)
    def get_first(delta):
        def f():
            for h in hs:
                first(h, delta)[1]().wait_recv()
                second(h, delta, 1)[0].start()
                rx = 1 if order(h)[0] == "x" else 0
                core(h, delta, rx, 1 - rx)[0].start()
        when(valid(delta), f)
    def get_second(delta):
        def f():
            for h in hs:
                for rel in range(2):
                    second(h, delta, rel)[1].wait_recv()
                    a0, a = order(h)
                    rx = 1 if a == "x" else (rel if a0 == "x" else 0)
                    ry = 1 if a == "y" else (rel if a0 == "y" else 0)
                    core(h, delta, rx, ry)[0].start()
        when(valid(delta), f)
    for step in range(nz + 2):
        for dist, fn in ((step, get_z), (step - 1, get_first), (step - 2, get_second)):
            if 0 <= dist < nz:
                if dist == 0:
                    if fn is not get_z: fn(0)
                else:
                    fn(-dist); fn(dist)
        if ex is not None and step == nz - 1:
            ex.wait_came()
            share_own().start()
            share(0).start()
            share(1).start()
        if ex is not None and step == nz + 1:
            shared_came(0).wait_recv()
            share(2).start()
    own.wait()
    if ex is not None:
        shared_came(1).wait_recv()
        shared_came(2).wait_recv()
        share_own().wait()
        for n in range(3):
            share(n).wait_send()
        ex.wait_sent()
    for delta in range(-(nz - 1), nz):
        def f(delta=delta):
            for h in hs:
                for rx in range(2):
                    for ry in range(2):
                        a, b = core(h, delta, rx, ry)
                        b.wait_recv(); a.wait_send()
                first(h, delta)[0].wait_send()
                for rel in range(2):
                    second(h, delta, rel)[0].wait_send()
                if delta <= 0:
                    when(z < nz - 1, lambda h=h: zcopy(h, -delta, 1, False).wait_send())
                if delta >= 0:
                    when(z > 0, lambda h=h: zcopy(h, delta, -1, False).wait_send())
        when(valid(delta), f)

def gather_kernel(v, dims, cid, exchanged=None, shared_rows=0, halves=2):
    nz, nx, ny = dims
    n = nz * nx * ny * 2
    span = 2 * nz - 1
    D = pltpu.SemaphoreType.DMA
    hbm = pl.BlockSpec(memory_space=pl.ANY)
    operands, out_shape, more = [v], [jax.ShapeDtypeStruct((n,) + v.shape, v.dtype)], []
    if shared_rows:
        e = exchanged
        operands += [e]
        out_shape += [jax.ShapeDtypeStruct(e.shape, e.dtype), jax.ShapeDtypeStruct((ny * 2, e.shape[0], shared_rows, e.shape[2]), e.dtype)]
        more = exchange_scratch(nz * nx) + [D((3,)), D((3,)), D]
    out = pl.pallas_call(
        functools.partial(ag_kernel, dims, halves, shared_rows),
        out_shape=out_shape,
        in_specs=[hbm] * len(operands),
        out_specs=[hbm] * len(out_shape),
        scratch_shapes=[D] + [D((halves * 2 * (nz + 1),))] * 2 + [D((halves * 2 * span,))] * 4 + [D((halves * 4 * span,))] * 2 + more,
        compiler_params=pltpu.CompilerParams(collective_id=cid, has_side_effects=True),
    )(*operands)
    return out if shared_rows else out[0]


def target_order(nz):
    low, high, order = 0, nz - 1, []
    while low <= high:
        order += [low] if low == high else [low, high]
        low, high = low + 1, high - 1
    return order


def tile_group(i, dims):
    nz, nx, _ = dims
    i = jnp.minimum(i, nz * nx - 1)
    j = i // nx
    t = jnp.where(j % 2 == 0, j // 2, nz - 1 - j // 2)
    return t * nx + i % nx


class Place:
    def __init__(self, dims):
        self.nz, self.nx, self.ny = dims
        gi, ei = lax.axis_index("grp"), lax.axis_index("exp")
        self.z, self.x = gi // self.nx, gi % self.nx
        self.y, self.c = ei // 2, ei % 2

    def device(self, z, x, y, c):
        return (z * self.nx + x, y * 2 + c)

    def core(self):
        return self.device(self.z, self.x, self.y, 1 - self.c)

    def along_x(self):
        return self.device(self.z, 1 - self.x, self.y, self.c)

    def along_y(self):
        return self.device(self.z, self.x, 1 - self.y, self.c)

    def along_z(self, by):
        return self.device(self.z + by, self.x, self.y, self.c)

    def greet(self):
        barrier = pltpu.get_barrier_semaphore()

        def signal(device):
            pl.semaphore_signal(barrier, inc=1, device_id=device, device_id_type=MESH)

        signal(self.along_x())
        signal(self.along_y())
        signal(self.core())
        pl.when(self.z > 0)(lambda: signal(self.along_z(-1)))
        pl.when(self.z < self.nz - 1)(lambda: signal(self.along_z(1)))

    def greet_plane(self):
        barrier = pltpu.get_barrier_semaphore()
        groups = self.nz * self.nx
        gi, ei = lax.axis_index("grp"), lax.axis_index("exp")
        peers = [((gi + r) % groups, ei) for r in range(1, groups)] + [self.along_y(), self.core()]
        for device in peers:
            pl.semaphore_signal(barrier, inc=1, device_id=device, device_id_type=MESH)

    def greeted_plane(self):
        pl.semaphore_wait(pltpu.get_barrier_semaphore(), self.nz * self.nx + 1)

    def greeted(self):
        inner = (self.z > 0).astype(jnp.int32) + (self.z < self.nz - 1).astype(jnp.int32)
        pl.semaphore_wait(pltpu.get_barrier_semaphore(), 3 + inner)


def remote(src, dst, sent, came, device):
    return pltpu.make_async_remote_copy(
        src_ref=src, dst_ref=dst, send_sem=sent, recv_sem=came, device_id=device, device_id_type=MESH
    )


def scatter_scratch(dims, rows, width):
    nz, nx, _ = dims
    tiles, half = nz * nx, rows // 2
    D, V = pltpu.SemaphoreType.DMA, lambda *s: pltpu.VMEM(s, bf16)
    return [
        V(2, 4 * rows, width),
        V(2, 2, rows, width),
        V(tiles, 2, rows, width),
        V(tiles, half, width), V(nz, 2, half, width),
        V(nz, half, width), V(nz, half, width),
        V(nz + 1, rows, width),
        D((tiles * 2,)), D((tiles * 2,)), D((tiles,)), D((tiles,)), D((nz * 2,)), D((nz * 2,)),
        D((nz,)), D((nz,)), D((nz,)), D((nz,)), D((nz * 2,)), D((nz * 2 + 2,)),
    ]


SCATTER_REFS = 20


class Scatter:
    def __init__(self, dims, place, out, refs):
        self.dims, self.place, self.out = dims, place, out
        (self.tile, self.crv, self.acc, self.ya, self.xb, self.xa, self.yb, self.zv,
         self.cs, self.cr, self.yas, self.yar, self.xbs, self.xbr,
         self.xas, self.xar, self.ybs, self.ybr, self.zs, self.zr) = refs
        self.rows = out.shape[0]
        self.half = self.rows // 2
        self.order = target_order(dims[0])
        self.tiles = dims[0] * dims[1]
        self.steps = self.tiles + 2 + dims[0]

    def add(self, into, *others):
        def step(r, _):
            at = rows_at(r, 16)
            total = others[0][at, :].astype(f32)
            for o in others[1:]:
                total = total + o[at, :].astype(f32)
            into[at, :] = total.astype(into.dtype)
            return 0

        lax.fori_loop(0, into.shape[0] // 16, step, 0)

    def low(self, k, q):
        return self.acc.at[k, q, pl.ds(0, self.half)]

    def high(self, k, q):
        return self.acc.at[k, q, pl.ds(self.half, self.half)]

    def shard(self, k, q, c):
        return self.tile.at[k % 2, rows_at(q * 2 + c, self.rows)]

    def c_core(self, k, q):
        p, s = self.place, k * 2 + q
        return remote(self.shard(k, q, 1 - p.c), self.crv.at[k % 2, q], self.cs.at[s], self.cr.at[s], p.core())

    def c_ya(self, k):
        p = self.place
        return remote(self.low(k, 1 - p.y), self.ya.at[k], self.yas.at[k], self.yar.at[k], p.along_y())

    def c_xb(self, k, q):
        p, j = self.place, k // 2
        s = j * 2 + q
        return remote(self.high(k, q), self.xb.at[j, q], self.xbs.at[s], self.xbr.at[s], p.along_x())

    def c_xa(self, k):
        p, j = self.place, k // 2
        return remote(self.low(k, p.y), self.xa.at[j], self.xas.at[j], self.xar.at[j], p.along_x())

    def c_yb(self, k):
        p, j = self.place, k // 2
        return remote(self.high(k, 1 - p.y), self.yb.at[j], self.ybs.at[j], self.ybr.at[j], p.along_y())

    def own_half(self, k, h):
        return self.acc.at[k, self.place.y, pl.ds(h * self.half, self.half)]

    def z_half(self, slot, h):
        return self.zv.at[slot, pl.ds(h * self.half, self.half)]

    def c_z(self, k, way, h):
        p, t = self.place, self.order[k // 2]
        slot = t if way > 0 else jnp.where(p.z - 1 == t, self.dims[0], t)
        return remote(self.own_half(k, h), self.z_half(slot, h), self.zs.at[t * 2 + h], self.zr.at[slot * 2 + h], p.along_z(way))

    def z_wait(self, k, slot, h):
        remote(self.own_half(k, h), self.z_half(slot, h), self.zs.at[h], self.zr.at[slot * 2 + h], self.place.core()).wait_recv()

    def phase_s(self, k):
        for q in range(2):
            self.c_core(k, q).start()

    def phase_b(self, k):
        p = self.place
        away = p.x != k % 2
        for q in (1 - p.y, p.y):
            self.c_core(k, q).wait_recv()
            self.add(self.acc.at[k, q], self.shard(k, q, p.c), self.crv.at[k % 2, q])
            if q is not p.y:
                self.c_ya(k).start()
            pl.when(away)(lambda q=q: self.c_xb(k, q).start())
        for q in range(2):
            self.c_core(k, q).wait_send()

    def phase_c(self, k):
        p, j = self.place, k // 2

        def give():
            self.c_ya(k).wait_recv()
            self.add(self.low(k, p.y), self.low(k, p.y), self.ya.at[k])
            self.c_xa(k).start()

        def keep():
            self.c_xb(k, 1 - p.y).wait_recv()
            self.add(self.high(k, 1 - p.y), self.high(k, 1 - p.y), self.xb.at[j, 1 - p.y])
            self.c_yb(k).start()

        pl.when(p.x != k % 2)(give)
        pl.when(p.x == k % 2)(keep)

    def phase_d(self, k):
        p, j, t, nz = self.place, k // 2, self.order[k // 2], self.dims[0]

        def ends(h):
            if t > 0:
                pl.when(p.z == 0)(lambda: self.c_z(k, 1, h).start())
            if t < nz - 1:
                pl.when(p.z == nz - 1)(lambda: self.c_z(k, -1, h).start())

        def keep():
            self.c_ya(k).wait_recv()
            self.c_xa(k).wait_recv()
            self.add(self.low(k, p.y), self.low(k, p.y), self.ya.at[k], self.xa.at[j])
            ends(0)
            self.c_xb(k, p.y).wait_recv()
            self.c_yb(k).wait_recv()
            self.add(self.high(k, p.y), self.high(k, p.y), self.xb.at[j, p.y], self.yb.at[j])
            ends(1)

        pl.when(p.x == k % 2)(keep)

    def phase_e(self, k, hop):
        p, t, nz = self.place, self.order[k // 2], self.dims[0]
        mine = p.x == k % 2

        def pass_on(way):
            def run():
                for h in range(2):
                    self.z_wait(k, t, h)
                    self.add(self.own_half(k, h), self.own_half(k, h), self.z_half(t, h))
                    self.c_z(k, way, h).start()

            return run

        if hop < t:
            pl.when(mine & (p.z == hop))(pass_on(1))
        if nz - 1 - hop > t:
            pl.when(mine & (p.z == nz - 1 - hop))(pass_on(-1))
        if hop == max(t, nz - 1 - t):

            def last():
                for h in range(2):
                    others = [self.own_half(k, h)]
                    for there, slot in ((t > 0, t), (t < nz - 1, nz)):
                        if there:
                            self.z_wait(k, slot, h)
                            others.append(self.z_half(slot, h))
                    self.add(self.out.at[pl.ds(h * self.half, self.half)], *others)

            pl.when(mine & (p.z == t))(last)

    def drain(self):
        p = self.place
        for k in range(self.tiles):
            self.c_ya(k).wait_send()

            def give(k=k):
                self.c_xa(k).wait_send()
                for q in range(2):
                    self.c_xb(k, q).wait_send()

            def keep(k=k):
                self.c_yb(k).wait_send()

                def along(k=k):
                    for h in range(2):
                        self.c_z(k, 1, h).wait_send()

                pl.when(p.z != self.order[k // 2])(along)

            pl.when(p.x != k % 2)(give)
            pl.when(p.x == k % 2)(keep)

    def run(self, i):
        for step in range(self.steps):

            def phases(step=step):
                for lag, phase in ((1, self.phase_b), (0, self.phase_s), (2, self.phase_c), (3, self.phase_d)):
                    if 0 <= step - lag < self.tiles:
                        phase(step - lag)
                for h in range(1, self.dims[0]):
                    if 0 <= step - 3 - h < self.tiles:
                        self.phase_e(step - 3 - h, h)
                if step == self.steps - 1:
                    self.drain()

            pl.when(i == step)(phases)


def scatter_kernel_body(dims, src, out, *refs):
    i = pl.program_id(0)
    place = Place(dims)
    s = Scatter(dims, place, out, refs)

    @pl.when(i == 0)
    def _():
        place.greet()
        place.greeted()

    @pl.when(i < s.tiles)
    def _():
        def copy(r):
            at = rows_at(r, 64)
            s.tile[i % 2, at, :] = src[at, :]
        loop(src.shape[0] // 64, copy)

    s.run(i)


def scatter_kernel(p, dims, cid):
    nz, nx, ny = dims
    n, rows, width = p.shape
    groups = nz * nx
    p = p.reshape(n * rows, width)
    return pl.pallas_call(
        functools.partial(scatter_kernel_body, dims),
        grid=(groups + 2 + nz,),
        in_specs=[pl.BlockSpec((4 * rows, width), lambda i: (tile_group(i, dims), 0))],
        out_specs=whole_block((rows, width)),
        out_shape=jax.ShapeDtypeStruct((rows, width), f32),
        scratch_shapes=scatter_scratch(dims, rows, width),
        compiler_params=pltpu.CompilerParams(collective_id=cid, has_side_effects=True, vmem_limit_bytes=60 * MB),
    )(p)


def layout(first, order, group_rows, block):
    places = jnp.arange(group_rows, dtype=jnp.int32)
    anchor = jnp.repeat(order, block, axis=1) * block + places % block
    doc = (anchor >= first).astype(jnp.int32)
    return (anchor, anchor - doc * first)


def rotary_tables(place):
    half = LANES // 2
    freq = jnp.exp(jnp.arange(half, dtype=f32) * (-2.0 * math.log(10000.0) / LANES))
    angle = place.astype(f32)[:, None] * freq[None, :]
    cos, sin = jnp.cos(angle), jnp.sin(angle)
    return (jnp.concatenate([cos, cos], axis=1), jnp.concatenate([-sin, sin], axis=1))


def logit_grad(route, gates, difference, experts):
    moved = gates[:, 0:1] * gates[:, 1:2] * difference
    names = jnp.arange(experts, dtype=jnp.int32)[None, :]
    return jnp.where(route[:, 0:1] == names, moved, 0.0) - jnp.where(
        route[:, 1:2] == names, moved, 0.0
    )


def norm_back(grad_hidden, normed, inverse, gain):
    grad_normed = grad_hidden * gain
    gain_grad = jnp.sum(grad_hidden * normed, axis=0)
    mean_term = jnp.mean(grad_normed * normed, axis=1, keepdims=True)
    return (inverse * (grad_normed - normed * mean_term), gain_grad)


def body(
    dims,
    layer_input,
    out_grad,
    doc_lengths,
    block_order,
    attn_route,
    ffn_route,
    norm_gains,
    kv_master,
    router_master,
    query_master,
    output_master,
    gate_up_master,
    down_master,
):
    own_rows, width = layer_input.shape
    members, groups = lax.axis_size("exp"), lax.axis_size("grp")
    member, group = lax.axis_index("exp"), lax.axis_index("grp")
    experts = members
    capacity = 3 * own_rows // experts
    group_rows = own_rows * members
    total = group_rows * groups
    devices = groups * members
    cw = width // groups
    depth = kv_master.shape[0]
    scale = 1.0 / math.sqrt(LANES)
    me = member.reshape(1).astype(jnp.int32)
    both = ("grp", "exp")

    def gather_all(v, cid):
        if dims is None:
            return lax.all_gather(kept(v), both, axis=0, tiled=True)
        return gather_kernel(v, dims, cid)

    def scatter_all(v, cid):
        v = v.reshape(devices, own_rows, v.shape[-1])
        if dims is None:
            return lax.psum_scatter(v, both, scatter_dimension=0, tiled=False).astype(f32)
        return scatter_kernel(v, dims, cid)

    def summed(parts):
        return jnp.concatenate([scatter_all(v, 0) for v in parts], axis=1) if dims is None else parts[0]

    blocks = block_order.shape[1]
    start_row = member * own_rows
    own_attn_route = lax.dynamic_slice_in_dim(attn_route, start_row, own_rows)
    own_ffn_route = lax.dynamic_slice_in_dim(ffn_route, start_row, own_rows)
    tall = lambda v: jnp.pad(v.astype(bf16), ((0, own_rows - v.shape[0]), (0, 0)))
    first_doc = doc_lengths[:, 0]
    small = jnp.concatenate(
        [
            tall(norm_gains),
            tall(router_master),
            own_attn_route.astype(bf16),
            own_ffn_route.astype(bf16),
            tall(jnp.concatenate([first_doc // 16, first_doc % 16, block_order[0]])[:, None]),
        ],
        axis=1,
    )
    at_route = 2 + 2 * experts
    small = jnp.pad(small, ((0, 0), (0, LANES - small.shape[1])))

    query_low = query_master[0].astype(bf16)
    kv_low = kv_master.astype(bf16).reshape(depth * 2, groups, cw)
    query_rows = query_low.shape[0]
    pieces_out = jnp.concatenate([query_low.reshape(query_rows, groups, cw), kv_low], axis=0).transpose(1, 0, 2)
    if dims is None:
        tokens = gather_all(layer_input, 1).reshape(total, width)
        extra = gather_all(small, 2).reshape(total, LANES)
        pieces_in = lax.all_to_all(pieces_out, "grp", split_axis=0, concat_axis=0, tiled=True)
        kv_all = lax.all_gather(pieces_in[:, query_rows:], "exp", axis=1, tiled=False)
    else:
        sent = jnp.concatenate([layer_input, small], axis=1)
        tokens, pieces_in, kv_all = gather_kernel(sent, dims, 1, pieces_out, 2 * depth)
        tokens = tokens.reshape(total, width + LANES)
        tokens, late_grad = lax.optimization_barrier((tokens, out_grad))
        extra = tokens[:, width:]
        kv_all = kv_all.transpose(1, 0, 2, 3)
    query_weight = pieces_in[:, :query_rows].reshape(width, cw)
    kv_weight = kv_all.reshape(width, 2 * cw)

    output_weight = output_master[0].astype(bf16)

    tables = extra.reshape(devices, own_rows, LANES)[:, :depth, :at_route].reshape(width, at_route)
    gains = tables[:, :2].astype(f32)
    router = tables[:, 2:]
    router_float = router.astype(f32)
    wide = lambda v: jnp.pad(v, ((0, 0), (0, LANES - v.shape[1])))
    routes = extra[:, at_route : at_route + 4].astype(jnp.int32)
    column = extra.reshape(groups, group_rows, LANES)[:, : blocks + 2, at_route + 4].astype(jnp.int32)

    def where_rows_stand(column):
        anchor, place = layout(
            column[:, 0:1] * 16 + column[:, 1:2], column[:, 2:], group_rows, own_rows // 2
        )
        cos, sin = rotary_tables(place.reshape(total))
        meta = jnp.concatenate(
            [anchor.reshape(total, 1), (anchor - place).reshape(total, 1), routes, routes[:, :2]], axis=1
        )
        return cos, sin, meta, jnp.broadcast_to(anchor[:, None, :], (groups, 8, group_rows))

    cos, sin, meta, key_rows = where_rows_stand(column)
    gain_one, gain_two = gains[:, 0], gains[:, 1]
    w_all = jnp.concatenate([query_weight, kv_weight, wide(router[:, :experts])], axis=1)

    qkv, att, aux, wg, wu, wd, attn_sum = attn_forward(
        dims, 3, me, tokens, gain_one[None], w_all, output_weight, cos, sin, meta, key_rows,
        gate_up_master[0], down_master[0], groups, scale,
    )
    own = (group * members + member) * own_rows
    attn_gates = lax.dynamic_slice(aux, (own, 2), (own_rows, 2))
    inputs = layer_input.astype(f32)
    middle = inputs + summed([attn_sum])
    inverse_two = lax.rsqrt(jnp.mean(middle * middle, axis=1, keepdims=True) + epsilon)
    normed_two = middle * inverse_two
    hidden_two = (normed_two * gain_two).astype(bf16)
    if dims is None:
        late_grad, hidden_two = lax.optimization_barrier((out_grad, hidden_two))
    h2 = gather_all(hidden_two, 4).reshape(total, width)
    tops = lax.all_gather(late_grad, both, axis=0, tiled=True)

    named = (routes[:, 2] == member) | (routes[:, 3] == member)
    named = named.reshape(devices, own_rows)
    position = jnp.cumsum(named.astype(jnp.int32), axis=1) - 1
    position = jnp.where(named, position, -1)
    tile_blocks = 4
    position = position.reshape(devices // tile_blocks, tile_blocks, own_rows)
    produced, ffn_aux, act, dgate, dup, *dh2_parts = ffn(
        dims, 5, me, h2, tops, wide(router[:, experts:]), meta, position,
        wg, wu, wd, capacity,
    )
    if dims is None:
        gate_up_grad, down_grad = ffn_weights(
            dims, 0, h2, tops, ffn_aux, position, act, dgate, dup, None, None, None, None, capacity
        )
        gate_up_grad, dh2_parts, produced = lax.optimization_barrier((gate_up_grad, dh2_parts, produced))
        back = summed(dh2_parts)
        produced, back = lax.optimization_barrier((produced, back))
        ffn_sum = scatter_all(produced, 0)
        ffn_sum, back = lax.optimization_barrier((ffn_sum, back))
    else:
        back = summed(dh2_parts)
    ffn_gates = lax.dynamic_slice(ffn_aux, (own, 2), (own_rows, 2))
    top_grad = out_grad.astype(f32)
    ffn_logit_grad = logit_grad(own_ffn_route, ffn_gates, back[:, width : width + 1], experts)
    hidden_two_grad = back[:, :width] + jnp.einsum(
        "te,de->td", ffn_logit_grad, router_float[:, experts:], precision=highest
    )
    middle_part, gain_two_grad = norm_back(hidden_two_grad, normed_two, inverse_two, gain_two)
    middle_grad = top_grad + middle_part
    dmid = gather_all(middle_grad.astype(bf16), 6).reshape(total, width)

    if dims is None:
        again, dmid = lax.optimization_barrier((layer_input, dmid))
        tokens = gather_all(again, 9).reshape(total, width)
        column, dmid = lax.optimization_barrier((column, dmid))
        cos, sin, meta, key_rows = where_rows_stand(column)
    dw, do, *dh1_parts = attn_backward(
        dims, 8, dmid, tokens, gain_one[None], qkv, att, aux, cos, sin, meta, key_rows, w_all, output_weight, groups, scale
    )
    back = summed(dh1_parts)
    inverse_one = lax.rsqrt(jnp.mean(inputs * inputs, axis=1, keepdims=True) + epsilon)
    normed_one = inputs * inverse_one
    hidden_one = (normed_one * gain_one).astype(bf16)
    attn_logit_grad = logit_grad(own_attn_route, attn_gates, back[:, width : width + 1], experts)
    hidden_one_grad = back[:, :width] + jnp.einsum(
        "te,de->td", attn_logit_grad, router_float[:, :experts], precision=highest
    )
    input_part, gain_one_grad = norm_back(hidden_one_grad, normed_one, inverse_one, gain_one)
    input_grad = middle_grad + input_part
    route_grad = [
        jnp.einsum("td,te->de", a.astype(f32), b, precision=highest)
        for a, b in ((hidden_one, attn_logit_grad), (hidden_two, ffn_logit_grad))
    ]
    sums = jnp.concatenate(
        [gain_one_grad[:, None], gain_two_grad[:, None], route_grad[0], route_grad[1]], axis=1
    )

    if dims is None:
        sums = lax.psum_scatter(sums, both, scatter_dimension=0, tiled=True)
        kv_part = dw[cw:].reshape(2 * cw, groups, members, depth)
        kv_part = lax.psum_scatter(kv_part.astype(bf16), "exp", scatter_dimension=2, tiled=False)
        query_part = dw[:cw].astype(bf16).reshape(cw, groups, width // groups)
        pieces_out = jnp.concatenate(
            [query_part.transpose(1, 0, 2).reshape(groups, -1), kv_part.transpose(1, 0, 2).reshape(groups, -1)],
            axis=1,
        )
        pieces_in = lax.all_to_all(pieces_out, "grp", split_axis=0, concat_axis=0, tiled=True)
        cut = cw * (width // groups)
        query_part = pieces_in[:, :cut].reshape(width, width // groups)
        kv_part = pieces_in[:, cut:].reshape(groups, 2, cw, depth).transpose(1, 0, 2, 3)
    else:
        beside = jnp.pad(
            sums.astype(bf16).reshape(devices, depth, sums.shape[1]),
            ((0, 0), (0, own_rows - depth), (0, LANES - sums.shape[1])),
        ).reshape(total, LANES)
        low = dw.astype(bf16)
        query_part = low[:cw].reshape(cw, groups, width // groups).transpose(1, 0, 2)
        kv_part = low[cw:].reshape(2, cw, groups, members // 2, LANES).transpose(0, 3, 2, 1, 4)
        gate_up_grad, down_grad, ffn_sum, query_part, kv_own, kv_other = ffn_weights(
            dims, 7, h2, tops, ffn_aux, position, act, dgate, dup, beside, produced, query_part, kv_part, capacity
        )
        sums = ffn_sum[:depth, width : width + sums.shape[1]]
        ffn_sum = ffn_sum[:, :width]
        query_part = query_part.reshape(width, width // groups)
        core = member % 2
        kv_part = jnp.where(core == 0, jnp.stack([kv_own, kv_other]), jnp.stack([kv_other, kv_own]))
        kv_part = lax.dynamic_slice_in_dim(kv_part, core * depth, depth, axis=3)
    final = middle + ffn_sum
    query_grad = query_part.T.astype(f32)
    kv_grad = kv_part.reshape(2 * width, depth).T.astype(f32)
    return (
        final.astype(bf16),
        input_grad,
        sums[:, :2],
        kv_grad,
        sums[:, 2:],
        query_grad[None],
        do[None],
        gate_up_grad[None],
        down_grad[None],
    )


def solution(mesh):
    groups, members = mesh.shape["grp"], mesh.shape["exp"]
    dims = (groups // 2, 2, members // 2) if groups <= 8 and members == 4 else None
    in_specs = (
        P(("grp", "exp"), None),
        P(("grp", "exp"), None),
        P("grp", None),
        P("grp", None),
        P("grp", None),
        P("grp", None),
        P(("grp", "exp"), None),
        P(("grp", "exp"), None),
        P(("grp", "exp"), None),
        P("exp", "grp", None),
        P("exp", "grp", None),
        P("exp", "grp", None, None),
        P("exp", "grp", None),
    )
    out_specs = (
        P(("grp", "exp"), None),
        P(("grp", "exp"), None),
        P(("grp", "exp"), None),
        P(("grp", "exp"), None),
        P(("grp", "exp"), None),
        P("exp", "grp", None),
        P("exp", "grp", None),
        P("exp", "grp", None, None),
        P("exp", "grp", None),
    )
    return jax.shard_map(
        functools.partial(body, dims),
        mesh=mesh,
        in_specs=in_specs,
        out_specs=out_specs,
        check_vma=False,
    )
```

```python
import functools
import math

import jax
import jax.numpy as jnp
from jax import lax
from jax.experimental import pallas as pl
from jax.experimental.pallas import tpu as pltpu
from jax.sharding import PartitionSpec as P

HEADS = 16
LANES = 128
MESH = pl.DeviceIdType.MESH
MB = 1024 * 1024
UNROLL = 4

epsilon = 1e-05
negative = -1e30
highest = lax.Precision.HIGHEST
f32 = jnp.float32
bf16 = jnp.bfloat16


def nn(a, b):
    return jnp.dot(a, b, preferred_element_type=f32)


def nt(a, b):
    return lax.dot_general(a, b, (((1,), (1,)), ((), ())), preferred_element_type=f32)


def tn(a, b):
    return lax.dot_general(a, b, (((0,), (0,)), ((), ())), preferred_element_type=f32)


def loop(count, step):
    def run(i, carry):
        step(i)
        return carry

    lax.fori_loop(0, count, run, 0)


def rows_at(i, size):
    return pl.ds(pl.multiple_of(i * size, size), size)


def kept(v):
    def copy(src, dst):
        dst[...] = src[...]

    return pl.pallas_call(copy, out_shape=jax.ShapeDtypeStruct(v.shape, v.dtype))(v)


def turn(v, cos, sin):
    return v * cos + pltpu.roll(v, LANES // 2, 1) * sin


def gate_columns(logits, r0, r1, me):
    lane = lax.broadcasted_iota(jnp.int32, logits.shape, 1)
    l0 = jnp.sum(jnp.where(lane == r0, logits, 0.0), axis=1, keepdims=True)
    l1 = jnp.sum(jnp.where(lane == r1, logits, 0.0), axis=1, keepdims=True)
    top = jnp.maximum(l0, l1)
    e0, e1 = jnp.exp(l0 - top), jnp.exp(l1 - top)
    g0, g1 = e0 / (e0 + e1), e1 / (e0 + e1)
    weight = jnp.where(r0 == me, g0, 0.0) + jnp.where(r1 == me, g1, 0.0)
    sign = jnp.where(r0 == me, 1.0, 0.0) - jnp.where(r1 == me, 1.0, 0.0)
    return jnp.where(
        lane == 0,
        weight,
        jnp.where(lane == 1, sign, jnp.where(lane == 2, g0, jnp.where(lane == 3, g1, 0.0))),
    )


def attn_forward_kernel(
    cw, scale, me, tokens, gain, w_all, ow, cos, sin, meta, krow, qkv, att, aux, part, h1, inv
):
    count, width = h1.shape
    heads = cw // LANES
    step_rows = min(512, count)

    def normalise(i):
        at = rows_at(i, 64)
        v = tokens[at, :].astype(f32)
        inverse = lax.rsqrt(jnp.mean(v * v, axis=1, keepdims=True) + epsilon)
        inv[at, :] = jnp.broadcast_to(inverse, (64, LANES))
        h1[at, :] = (v * inverse * gain[...]).astype(bf16)

    loop(count // 64, normalise)

    def project(i):
        at = rows_at(i, step_rows)
        y = nn(h1[at, :], w_all[...])
        c, s = cos[at, :], sin[at, :]
        for h in range(2 * heads):
            qkv[at, h * LANES : (h + 1) * LANES] = turn(
                y[:, h * LANES : (h + 1) * LANES], c, s
            ).astype(bf16)
        qkv[at, 2 * cw : 3 * cw] = y[:, 2 * cw : 3 * cw].astype(bf16)
        found = gate_columns(y[:, 3 * cw : 3 * cw + LANES], meta[at, 2:3], meta[at, 3:4], me[0])
        lane = lax.broadcasted_iota(jnp.int32, found.shape, 1)
        aux[at, :] = jnp.where(lane == 4, inv[at, :], found)

    loop(count // step_rows, project)

    def attend(i):
        at = rows_at(i, LANES)
        ak = krow[0, 0:1, :]
        allowed = (ak <= meta[at, 0:1]) & (ak >= meta[at, 1:2])
        old = aux[at, :]
        lane = lax.broadcasted_iota(jnp.int32, old.shape, 1)
        for h in range(heads):
            q = qkv[at, h * LANES : (h + 1) * LANES]
            k = qkv[:, cw + h * LANES : cw + (h + 1) * LANES]
            v = qkv[:, 2 * cw + h * LANES : 2 * cw + (h + 1) * LANES]
            scores = jnp.where(allowed, nt(q, k) * scale, negative)
            top = jnp.max(scores, axis=1, keepdims=True)
            raised = jnp.exp(scores - top)
            total = jnp.sum(raised, axis=1, keepdims=True)
            probs = (raised * (1.0 / total)).astype(bf16)
            att[at, h * LANES : (h + 1) * LANES] = nn(probs, v).astype(bf16)
            old = jnp.where(lane == 8 + h, top + jnp.log(total), old)
        aux[at, :] = old

    lax.fori_loop(0, count // LANES, lambda i, c: (attend(i), c)[1], 0, unroll=UNROLL)

    def output(i):
        at = rows_at(i, step_rows)
        scaled = (aux[at, 0:1] * att[at, :].astype(f32)).astype(bf16)
        part[at, :] = nn(scaled, ow[...]).astype(bf16)

    loop(count // step_rows, output)


def attn_backward_kernel(
    cw, scale, dmid, tokens, gain, qkv, att, aux, cos, sin, meta, krow, w_all, ow,
    dh1, side, dw, do, h1, datt, watt, dqkv, dk_sum, dv_sum,
):
    count, width = h1.shape
    heads = cw // LANES
    step_rows = min(512, count)

    @pl.when(pl.program_id(0) == 0)
    def _():
        dw[...] = jnp.zeros_like(dw)
        do[...] = jnp.zeros_like(do)

    def normalise(i):
        at = rows_at(i, 64)
        h1[at, :] = (tokens[at, :].astype(f32) * aux[at, 4:5] * gain[...]).astype(bf16)

    loop(count // 64, normalise)

    def incoming(i):
        at = rows_at(i, step_rows)
        raw = nt(dmid[at, :], ow[...])
        a = att[at, :].astype(f32)
        weight, sign = aux[at, 0:1], aux[at, 1:2]
        share = sign * jnp.sum(raw * a, axis=1, keepdims=True)
        side[at, :] = jnp.broadcast_to(share, (step_rows, LANES)).astype(bf16)
        datt[at, :] = (weight * raw).astype(bf16)
        watt[at, :] = (weight * a).astype(bf16)

    loop(count // step_rows, incoming)

    def out_weight(i):
        at = rows_at(i, 512)
        do[:, at] += tn(watt[...], dmid[:, at])

    loop(width // 512, out_weight)

    dk_sum[...] = jnp.zeros_like(dk_sum)
    dv_sum[...] = jnp.zeros_like(dv_sum)

    def back(i):
        at = rows_at(i, LANES)
        ak = krow[0, 0:1, :]
        allowed = (ak <= meta[at, 0:1]) & (ak >= meta[at, 1:2])
        for h in range(heads):
            hs = slice(h * LANES, (h + 1) * LANES)
            q, k, v = qkv[at, hs], qkv[:, cw + h * LANES : cw + (h + 1) * LANES], qkv[:, 2 * cw + h * LANES : 2 * cw + (h + 1) * LANES]
            scores = jnp.where(allowed, nt(q, k) * scale, negative)
            probs = jnp.exp(scores - aux[at, 8 + h : 9 + h])
            grad = datt[at, hs]
            dprobs = nt(grad, v)
            inner = jnp.sum(probs * dprobs, axis=1, keepdims=True)
            dscores = (probs * (dprobs - inner)).astype(bf16)
            dqkv[at, hs] = turn(nn(dscores, k) * scale, cos[at, :], -sin[at, :]).astype(bf16)
            dk_sum[:, hs] += tn(dscores, q)
            dv_sum[:, hs] += tn(probs.astype(bf16), grad)

    lax.fori_loop(0, count // LANES, lambda i, c: (back(i), c)[1], 0, unroll=UNROLL)
    for h in range(heads):
        hs = slice(h * LANES, (h + 1) * LANES)
        dqkv[:, cw + h * LANES : cw + (h + 1) * LANES] = turn(dk_sum[:, hs] * scale, cos[...], -sin[...]).astype(bf16)
        dqkv[:, 2 * cw + h * LANES : 2 * cw + (h + 1) * LANES] = dv_sum[:, hs].astype(bf16)

    def to_hidden(i):
        at = rows_at(i, step_rows)
        dh1[at, :width] = nt(dqkv[at, :], w_all[:, : 3 * cw]).astype(bf16)

    loop(count // step_rows, to_hidden)

    def weights(i):
        at = rows_at(i, 512)
        dw[:, at] += tn(dqkv[...], h1[:, at])

    loop(width // 512, weights)


def whole_block(shape):
    return pl.BlockSpec(shape, lambda i: (0,) * len(shape))


def once(shape):
    return pl.BlockSpec(shape, lambda i: (0,) * len(shape), pipeline_mode=pl.Buffered(1))


def attn_forward_plain(cw, scale, me, tokens, gain, w_all, ow, cos, sin, meta, krow, gate_up, down, qkv, att, aux, wg, wu, wd, part, h1, inv, *more):
    i = pl.program_id(0)
    Masters(gate_up, down, wg, wu, wd, *more).step(i, 1, 4)
    attn_forward_kernel(cw, scale, me, tokens, gain, w_all, ow, cos, sin, meta, krow, qkv, att, aux, part, h1, inv)


def attn_forward_fused(dims, cw, scale, me, tokens, gain, w_all, ow, cos, sin, meta, krow, gate_up, down, qkv, att, aux, wg, wu, wd, out, h1, inv, stage, low, sems, out_sems, *refs):
    i = pl.program_id(0)
    place = Place(dims)
    sums = Scatter(dims, place, out, refs)
    Masters(gate_up, down, wg, wu, wd, stage, low, sems, out_sems).step(i, sums.tiles, 5)
    pl.when(i == 0)(place.greet)

    @pl.when(i < sums.tiles)
    def _():
        attn_forward_kernel(cw, scale, me, tokens, gain, w_all, ow, cos, sin, meta, krow, qkv, att, aux, sums.tile.at[i % 2], h1, inv)

    pl.when(i == 0)(place.greeted)
    sums.run(i)


def attn_forward(dims, cid, me, tokens, gain, w_all, ow, cos, sin, meta, krow, gate_up, down, groups, scale):
    total = tokens.shape[0]
    cw, width = ow.shape
    count = total // groups
    at = (lambda i: tile_group(i, dims)) if dims else (lambda i: i)
    row = lambda w: pl.BlockSpec((count, w), lambda i: (at(i), 0))
    hbm = pl.BlockSpec(memory_space=pl.ANY)
    shape = lambda w, t: jax.ShapeDtypeStruct((total, w), t)
    if dims:
        own = count // 4
        kernel = functools.partial(attn_forward_fused, dims, cw, scale)
        last_spec, last_shape = whole_block((own, width)), jax.ShapeDtypeStruct((own, width), f32)
        params, more = dict(collective_id=cid, has_side_effects=True), scatter_scratch(dims, own, width)
    else:
        kernel = functools.partial(attn_forward_plain, cw, scale)
        last_spec, last_shape, params, more = row(width), shape(width, bf16), {}, []
    return pl.pallas_call(
        kernel,
        grid=(groups + 2 + dims[0] if dims else groups,),
        in_specs=[
            pl.BlockSpec(memory_space=pltpu.SMEM), row(width), whole_block(gain.shape),
            once(w_all.shape), once(ow.shape), row(LANES), row(LANES), row(8),
            pl.BlockSpec((1, 8, count), lambda i: (at(i), 0, 0)), hbm, hbm,
        ],
        out_specs=[row(3 * cw), row(cw), row(LANES), hbm, hbm, hbm, last_spec],
        out_shape=[shape(3 * cw, bf16), shape(cw, bf16), shape(LANES, f32)] + [jax.ShapeDtypeStruct(down.shape, bf16)] * 3 + [last_shape],
        scratch_shapes=[pltpu.VMEM((count, width), bf16), pltpu.VMEM((count, LANES), f32)] + masters_scratch(down.shape[0], width) + more,
        compiler_params=pltpu.CompilerParams(vmem_limit_bytes=60 * MB, **params),
    )(me, tokens, gain, w_all, ow, cos, sin, meta, krow, gate_up, down)


def attn_backward_plain(cw, scale, dmid, tokens, gain, qkv, att, aux, cos, sin, meta, krow, w_all, ow, dw_hbm, do_hbm, dh1, side, dw, do, sems, *more):
    attn_backward_kernel(cw, scale, dmid, tokens, gain, qkv, att, aux, cos, sin, meta, krow, w_all, ow, dh1, side, dw, do, *more)
    pl.when(pl.program_id(0) == pl.num_programs(0) - 1)(lambda: attn_weights_out(dw, do, dw_hbm, do_hbm, sems))


def attn_weights_out(dw, do, dw_hbm, do_hbm, sems):
    copies = [pltpu.make_async_copy(a, b, sems.at[n]) for n, (a, b) in enumerate(((dw, dw_hbm), (do, do_hbm)))]
    for c in copies:
        c.start()
    for c in copies:
        c.wait()


def attn_backward_fused(dims, cw, scale, dmid, tokens, gain, qkv, att, aux, cos, sin, meta, krow, w_all, ow, dw_hbm, do_hbm, out, dw, do, sems, h1, datt, watt, dqkv, dk_sum, dv_sum, *refs):
    i = pl.program_id(0)
    place = Place(dims)
    sums = Scatter(dims, place, out, refs)
    pl.when(i == 0)(place.greet)

    @pl.when(i < sums.tiles)
    def _():
        tile, side = sums.tile.at[i % 2], sums.tile.at[i % 2, :, pl.ds(dmid.shape[1], LANES)]
        attn_backward_kernel(cw, scale, dmid, tokens, gain, qkv, att, aux, cos, sin, meta, krow, w_all, ow, tile, side, dw, do, h1, datt, watt, dqkv, dk_sum, dv_sum)

    pl.when(i == 0)(place.greeted)
    sums.run(i)
    pl.when(i == sums.tiles)(lambda: attn_weights_out(dw, do, dw_hbm, do_hbm, sems))


def attn_backward(dims, cid, dmid, tokens, gain, qkv, att, aux, cos, sin, meta, krow, w_all, ow, groups, scale):
    total, width = dmid.shape
    cw = ow.shape[0]
    count = total // groups
    at = (lambda i: tile_group(i, dims)) if dims else (lambda i: i)
    row = lambda w: pl.BlockSpec((count, w), lambda i: (at(i), 0))
    wide = width + LANES
    hbm = pl.BlockSpec(memory_space=pl.ANY)
    if dims:
        own = count // 4
        kernel = functools.partial(attn_backward_fused, dims, cw, scale)
        last_spec, last_shape = [whole_block((own, wide))], [jax.ShapeDtypeStruct((own, wide), f32)]
        params, more = dict(collective_id=cid, has_side_effects=True), scatter_scratch(dims, own, wide)
    else:
        kernel = functools.partial(attn_backward_plain, cw, scale)
        last_spec = [row(width), row(LANES)]
        last_shape = [jax.ShapeDtypeStruct((total, w), bf16) for w in (width, LANES)]
        params, more = {}, []
    return pl.pallas_call(
        kernel,
        grid=(groups + 2 + dims[0] if dims else groups,),
        in_specs=[
            row(width), row(width), whole_block(gain.shape), row(3 * cw), row(cw), row(LANES), row(LANES), row(LANES), row(8),
            pl.BlockSpec((1, 8, count), lambda i: (at(i), 0, 0)),
            once(w_all.shape), once(ow.shape),
        ],
        out_specs=[hbm, hbm] + last_spec,
        out_shape=[jax.ShapeDtypeStruct((3 * cw, width), f32), jax.ShapeDtypeStruct((cw, width), f32)] + last_shape,
        scratch_shapes=[
            pltpu.VMEM((3 * cw, width), f32), pltpu.VMEM((cw, width), f32), pltpu.SemaphoreType.DMA((2,)),
            pltpu.VMEM((count, width), bf16), pltpu.VMEM((count, cw), bf16), pltpu.VMEM((count, cw), bf16), pltpu.VMEM((count, 3 * cw), bf16),
            pltpu.VMEM((count, cw), f32), pltpu.VMEM((count, cw), f32),
        ] + more,
        compiler_params=pltpu.CompilerParams(vmem_limit_bytes=62 * MB, **params),
    )(dmid, tokens, gain, qkv, att, aux, cos, sin, meta, krow, w_all, ow)


def pieces(total, size):
    return [(at, min(size, total - at)) for at in range(0, total, size)]


def chosen(posrow, i, cap):
    slot = lax.broadcasted_iota(jnp.int32, (cap, LANES), 0)
    return (slot == posrow[0, pl.ds(i, 1), :]).astype(bf16)


def is_dense(cap):
    return 2 * cap > LANES


def chosen_scratch(cap, few, width):
    return [pltpu.VMEM((16 if is_dense(cap) else few, width), bf16), pltpu.VMEM((few, width), bf16)]


def gated(top, weight, at, cs):
    return (weight * top[at, cs].astype(f32)).astype(bf16)


def compact(cap, h2, top, posrow, weight, xc, gc):
    def block(i):
        at, to = rows_at(i, LANES), rows_at(i, cap)
        w = weight(at)
        choose = None if is_dense(cap) else chosen(posrow, i, cap)
        for start, size in pieces(h2.shape[1], 512):
            cs = slice(start, start + size)
            if is_dense(cap):
                gc[at, cs] = gated(top, w, at, cs)
            else:
                xc[to, cs] = nn(choose, h2[at, cs]).astype(bf16)
                gc[to, cs] = nn(choose, gated(top, w, at, cs)).astype(bf16)

    loop(h2.shape[0] // LANES, block)


def stage_rows(hidden):
    return max(r for r in range(16, 177, 16) if hidden % r == 0)


class Masters:
    def __init__(self, gate_up, down, wg, wu, wd, stage, low, sems, out_sems):
        part = stage.shape[1]
        self.jobs = [
            (src.at[pl.ds(n * part, part)], dst.at[pl.ds(n * part, part)])
            for n in range(down.shape[0] // part)
            for src, dst in ((gate_up.at[:, 0, :], wg), (gate_up.at[:, 1, :], wu), (down, wd))
        ]
        self.stage, self.low, self.sems, self.out_sems = stage, low, sems, out_sems

    def load(self, n):
        return pltpu.make_async_copy(self.jobs[n][0], self.stage.at[n % 2], self.sems.at[n % 2])

    def store(self, n):
        return pltpu.make_async_copy(self.low.at[n % 2], self.jobs[n][1], self.out_sems.at[n % 2])

    def run(self, first, last):
        for n in range(first, last):
            self.load(n).wait()
            if n >= 2:
                self.store(n - 2).wait()

            def cast(r, n=n):
                at = rows_at(r, 16)
                self.low[n % 2, at, :] = self.stage[n % 2, at, :].astype(bf16)

            loop(self.low.shape[1] // 16, cast)
            self.store(n).start()
            if n + 2 < len(self.jobs):
                self.load(n + 2).start()

    def finish(self):
        for n in range(max(len(self.jobs) - 2, 0), len(self.jobs)):
            self.store(n).wait()

    def step(self, i, first_step, steps):
        count = len(self.jobs)

        @pl.when(i == first_step - 1)
        def _():
            for n in range(min(2, count)):
                self.load(n).start()

        for k in range(steps):
            pl.when(i == first_step + k)(
                lambda k=k: self.run(count * k // steps, count * (k + 1) // steps)
            )
        pl.when(i == first_step + steps - 1)(self.finish)


def masters_scratch(hidden, width):
    part = stage_rows(hidden)
    D = pltpu.SemaphoreType.DMA
    return [pltpu.VMEM((2, part, width), f32), pltpu.VMEM((2, part, width), bf16), D((2,)), D((2,))]


def ffn_compute(cap, me, h2, top, router, meta, posrow, produced, dh2, side, aux, act, dgate, dup, wg, wu, wd, xc, gc):
    rows, width = h2.shape
    hidden = wd.shape[0]
    blocks = rows // LANES

    aux[...] = gate_columns(nn(h2[...], router[...]), meta[:, 4:5], meta[:, 5:6], me[0])
    compact(cap, h2, top, posrow, lambda at: aux[at, 0:1], xc, gc)
    xs = h2 if is_dense(cap) else xc

    for start, size in pieces(hidden, 256):
        fs = slice(start, start + size)
        gate, up, dact = nt(xs[...], wg[fs, :]), nt(xs[...], wu[fs, :]), nt(gc[...], wd[fs, :])
        sigmoid = 1.0 / (1.0 + jnp.exp(-gate))
        silu = gate * sigmoid
        act[:, fs] = (silu * up).astype(bf16)
        dgate[:, fs] = (dact * up * sigmoid * (1.0 + gate * (1.0 - sigmoid))).astype(bf16)
        dup[:, fs] = (dact * silu).astype(bf16)

    if is_dense(cap):
        shares = jnp.zeros((rows, 1), f32)
        for start, size in pieces(width, 512):
            cs = slice(start, start + size)
            y = nn(act[...], wd[:, cs])
            shares = shares + jnp.sum(y * top[:, cs].astype(f32), axis=1, keepdims=True)
            produced[:, cs] = (aux[:, 0:1] * y).astype(bf16)
            dh2[:, cs] = (nn(dgate[...], wg[:, cs]) + nn(dup[...], wu[:, cs])).astype(bf16)
        side[...] = jnp.broadcast_to(aux[:, 1:2] * shares, (rows, LANES)).astype(bf16)
        return

    yc, bc = gc, xc

    def results(i):
        at = rows_at(i, 512)
        yc[:, at] = nn(act[...], wd[:, at]).astype(bf16)
        bc[:, at] = (nn(dgate[...], wg[:, at]) + nn(dup[...], wu[:, at])).astype(bf16)

    loop(width // 512, results)

    def scatter(i):
        at, of = rows_at(i, LANES), rows_at(i, cap)
        choose = chosen(posrow, i, cap)
        found = aux[at, :]
        share = jnp.zeros((LANES, 1), f32)
        for start, size in pieces(width, 512):
            cs = slice(start, start + size)
            y = tn(choose, yc[of, cs])
            share = share + jnp.sum(y * top[at, cs].astype(f32), axis=1, keepdims=True)
            produced[at, cs] = (found[:, 0:1] * y).astype(bf16)
            dh2[at, cs] = tn(choose, bc[of, cs]).astype(bf16)
        side[at, :] = jnp.broadcast_to(found[:, 1:2] * share, (LANES, LANES)).astype(bf16)

    loop(blocks, scatter)


def ffn_kernel(cap, me, h2, top, router, meta, posrow, wg, wu, wd, produced, aux, act, dgate, dup, dh2, side, xc, gc):
    ffn_compute(cap, me, h2, top, router, meta, posrow, produced, dh2, side, aux, act, dgate, dup, wg, wu, wd, xc, gc)


def ffn_fused_kernel(dims, cap, me, h2, top, router, meta, posrow, wg, wu, wd, produced, aux, act, dgate, dup, out, xc, gc, *refs):
    i = pl.program_id(0)
    place = Place(dims)
    sums = Scatter(dims, place, out, refs)

    pl.when(i == 0)(place.greet)

    @pl.when(i < sums.tiles)
    def _():
        tile, side = sums.tile.at[i % 2], sums.tile.at[i % 2, :, pl.ds(h2.shape[1], LANES)]
        ffn_compute(cap, me, h2, top, router, meta, posrow, produced, tile, side, aux, act, dgate, dup, wg, wu, wd, xc, gc)

    pl.when(i == 0)(place.greeted)
    sums.run(i)


def ffn(dims, cid, me, h2, top, router, meta, posrow, wg, wu, wd, cap):
    total, width = h2.shape
    hidden = wd.shape[0]
    tile = posrow.shape[1] * LANES
    few = tile if is_dense(cap) else tile // LANES * cap
    tiles = total // tile
    at = (lambda i: tile_group(i, dims)) if dims else (lambda i: i)
    row = lambda w: pl.BlockSpec((tile, w), lambda i: (at(i), 0))
    some = pl.BlockSpec((few, hidden), lambda i: (at(i), 0))
    own = total // (dims[0] * dims[1] * dims[2] * 2) if dims else 0
    wide = width + LANES
    if dims:
        kernel = functools.partial(ffn_fused_kernel, dims, cap)
        last_spec, last_shape = [whole_block((own, wide))], [jax.ShapeDtypeStruct((own, wide), f32)]
        params = dict(collective_id=cid, has_side_effects=True)
    else:
        kernel = functools.partial(ffn_kernel, cap)
        last_spec = [row(width), row(LANES)]
        last_shape = [jax.ShapeDtypeStruct((total, w), bf16) for w in (width, LANES)]
        params = {}
    return pl.pallas_call(
        kernel,
        grid=(tiles + 2 + dims[0] if dims else tiles,),
        in_specs=[
            pl.BlockSpec(memory_space=pltpu.SMEM), row(width), row(width), whole_block(router.shape), row(8),
            pl.BlockSpec((1,) + posrow.shape[1:], lambda i: (at(i), 0, 0)), once(wg.shape), once(wu.shape), once(wd.shape),
        ],
        out_specs=[row(width), row(LANES), some, some, some] + last_spec,
        out_shape=[
            jax.ShapeDtypeStruct((total, width), bf16),
            jax.ShapeDtypeStruct((total, LANES), f32),
        ] + [jax.ShapeDtypeStruct((tiles * few, hidden), bf16)] * 3 + last_shape,
        scratch_shapes=chosen_scratch(cap, few, width)
        + (scatter_scratch(dims, own, wide) if dims else []),
        compiler_params=pltpu.CompilerParams(vmem_limit_bytes=63 * MB, **params),
    )(me, h2, top, router, meta, posrow, wg, wu, wd)


def ffn_weights_compute(cap, first, h2, top, aux, posrow, act, dgate, dup, sg, su, sd, xc, gc):
    width = h2.shape[1]
    hidden = sd.shape[0]

    @pl.when(first)
    def _():
        for s in (sg, su, sd):

            def clear(i, s=s):
                s[rows_at(i, 32), :] = jnp.zeros((32, width), f32)

            loop(hidden // 32, clear)

    compact(cap, h2, top, posrow, lambda at: aux[at, 0:1], xc, gc)
    xs = h2 if is_dense(cap) else xc
    for start, size in pieces(hidden, 256):
        fs = slice(start, start + size)

        def grads(i, fs=fs):
            at = rows_at(i, 512)
            sd[fs, at] += tn(act[:, fs], gc[:, at])
            sg[fs, at] += tn(dgate[:, fs], xs[:, at])
            su[fs, at] += tn(dup[:, fs], xs[:, at])

        loop(width // 512, grads)


def ffn_weights_out(gate_up_grad, down_grad, sg, su, sd, sems):
    pairs = [(sg, gate_up_grad.at[:, 0, :]), (su, gate_up_grad.at[:, 1, :]), (sd, down_grad)]
    return [pltpu.make_async_copy(a, b, sems.at[i]) for i, (a, b) in enumerate(pairs)]


def ffn_weights_kernel(cap, h2, top, aux, posrow, act, dgate, dup, gate_up_grad, down_grad, sg, su, sd, xc, gc, sems):
    i = pl.program_id(0)
    ffn_weights_compute(cap, i == 0, h2, top, aux, posrow, act, dgate, dup, sg, su, sd, xc, gc)

    @pl.when(i == pl.num_programs(0) - 1)
    def _():
        copies = ffn_weights_out(gate_up_grad, down_grad, sg, su, sd, sems)
        for c in copies:
            c.start()
        for c in copies:
            c.wait()


class GradExchange:
    def __init__(self, dims, place, q_src, kv_src, q_out, kv_out, other_out, own, landed, along, refs):
        groups = dims[0] * dims[1]
        qs, qr, ql, ks, kr, kl, self.ls, self.ss, self.sr = refs
        self.place, self.kv_src, self.kv_out, self.other_out = place, kv_src, kv_out, other_out
        self.own, self.landed, self.along = own, landed, along
        self.query = Exchange(groups, q_src, q_out, qs, qr, ql)
        self.kv = Exchange(groups, own.at[place.y], kv_out, ks, kr, kl)

    def load(self):
        return pltpu.make_async_copy(self.kv_src.at[self.place.c], self.own, self.ls)

    def c_core(self):
        p = self.place
        return remote(self.kv_src.at[1 - p.c], self.landed, self.ss.at[0], self.sr.at[0], p.core())

    def c_y(self):
        p = self.place
        return remote(self.own.at[1 - p.y], self.along, self.ss.at[1], self.sr.at[1], p.along_y())

    def c_last(self):
        return remote(self.kv_out, self.other_out, self.ss.at[2], self.sr.at[2], self.place.core())

    def add(self, into, other):
        groups, rows, _ = into.shape

        def step(n):
            at = rows_at(n % (rows // 64), 64)
            g = n // (rows // 64)
            into[g, at, :] = (into[g, at, :].astype(f32) + other[g, at, :].astype(f32)).astype(bf16)

        loop(groups * (rows // 64), step)

    def step(self, i, last):
        @pl.when(i == 0)
        def _():
            self.c_core().start()
            self.load().start()
            self.query.start()

        @pl.when(i == 1)
        def _():
            self.load().wait()
            self.c_core().wait_recv()
            for n in range(2):
                self.add(self.own.at[n], self.landed.at[n])
            self.c_y().start()

        @pl.when(i == 3)
        def _():
            self.c_y().wait_recv()
            self.add(self.own.at[self.place.y], self.along)
            self.kv.start()

        @pl.when(i == 7)
        def _():
            self.kv.wait_came()
            self.c_last().start()

        @pl.when(i == last)
        def _():
            self.query.wait_came()
            self.c_last().wait_recv()
            for c in (self.c_core(), self.c_y(), self.c_last()):
                c.wait_send()
            self.query.wait_sent()
            self.kv.wait_sent()


def grad_exchange_scratch(groups, cw):
    D = pltpu.SemaphoreType.DMA
    V = lambda *s: pltpu.VMEM(s + (groups, cw, LANES), bf16)
    return [V(2), V(2), V()], exchange_scratch(groups) * 2 + [D, D((3,)), D((3,))]


def ffn_weights_fused(dims, cap, h2, top, aux, posrow, act, dgate, dup, extra, produced, q_src, kv_src, gate_up_grad, down_grad, out, q_out, kv_out, other_out, sg, su, sd, xc, gc, sems, load, own, landed, along, *refs):
    i = pl.program_id(0)
    place = Place(dims)
    sums = Scatter(dims, place, out, refs[:SCATTER_REFS])
    grads = GradExchange(dims, place, q_src, kv_src, q_out, kv_out, other_out, own, landed, along, refs[SCATTER_REFS:])
    rows, width = h2.shape
    copies = ffn_weights_out(gate_up_grad, down_grad, sg, su, sd, sems)

    @pl.when(i == 0)
    def _():
        place.greet_plane()
        place.greeted_plane()

    grads.step(i, sums.steps - 1)

    @pl.when(i < sums.tiles)
    def _():
        tile = sums.tile.at[i % 2]
        fetch = pltpu.make_async_copy(produced.at[rows_at(tile_group(i, dims), rows)], tile.at[:, pl.ds(0, width)], load)
        fetch.start()
        tile[:, width:] = extra[...]
        ffn_weights_compute(cap, i == 0, h2, top, aux, posrow, act, dgate, dup, sg, su, sd, xc, gc)
        fetch.wait()

    @pl.when(i == sums.tiles)
    def _():
        for c in copies:
            c.start()

    sums.run(i)

    @pl.when(i == sums.steps - 1)
    def _():
        for c in copies:
            c.wait()


def ffn_weights(dims, cid, h2, top, aux, posrow, act, dgate, dup, extra, produced, q_src, kv_src, cap):
    total, width = h2.shape
    hidden = act.shape[1]
    tile = posrow.shape[1] * LANES
    few = tile if is_dense(cap) else tile // LANES * cap
    tiles = total // tile
    at = (lambda i: tile_group(i, dims)) if dims else (lambda i: i)
    row = lambda w: pl.BlockSpec((tile, w), lambda i: (at(i), 0))
    some = pl.BlockSpec((few, hidden), lambda i: (at(i), 0))
    hbm = pl.BlockSpec(memory_space=pl.ANY)
    V = pltpu.VMEM
    scratch = [V((hidden, width), f32)] * 3 + chosen_scratch(cap, few, width) + [pltpu.SemaphoreType.DMA((3,))]
    out_specs = [hbm, hbm]
    out_shape = [jax.ShapeDtypeStruct((hidden, 2, width), f32), jax.ShapeDtypeStruct((hidden, width), f32)]
    in_specs = [
        row(width), row(width), row(LANES), pl.BlockSpec((1,) + posrow.shape[1:], lambda i: (at(i), 0, 0)), some, some, some,
    ]
    operands = [h2, top, aux, posrow, act, dgate, dup]
    if dims:
        own = tile // 4
        kernel = functools.partial(ffn_weights_fused, dims, cap)
        wide = width + LANES
        operands, in_specs = operands + [extra, produced, q_src, kv_src], in_specs + [row(LANES), hbm, hbm, hbm]
        groups, cw = q_src.shape[:2]
        out_specs = out_specs + [once((own, wide)), hbm, hbm, hbm]
        out_shape = out_shape + [jax.ShapeDtypeStruct((own, wide), f32), jax.ShapeDtypeStruct(q_src.shape, bf16)]
        out_shape = out_shape + [jax.ShapeDtypeStruct((groups, cw, LANES), bf16)] * 2
        buffers, marks = grad_exchange_scratch(groups, cw)
        scratch = scratch + [pltpu.SemaphoreType.DMA] + buffers + scatter_scratch(dims, own, wide) + marks
        params = dict(collective_id=cid, has_side_effects=True)
    else:
        kernel, params = functools.partial(ffn_weights_kernel, cap), {}
    return pl.pallas_call(
        kernel,
        grid=(tiles + 2 + dims[0] if dims else tiles,),
        in_specs=in_specs,
        out_specs=out_specs,
        out_shape=out_shape,
        scratch_shapes=scratch,
        compiler_params=pltpu.CompilerParams(vmem_limit_bytes=63 * MB, **params),
    )(*operands)


class Exchange:
    def __init__(self, groups, src, dst, sent, came, local):
        self.groups, self.src, self.dst, self.sent, self.came, self.local = groups, src, dst, sent, came, local
        self.gi, self.ei = lax.axis_index("grp"), lax.axis_index("exp")

    def peers(self):
        return [((self.gi + r) % self.groups, self.ei) for r in range(1, self.groups)]

    def copy(self, r, arriving=False):
        to, of = (self.gi + r) % self.groups, (self.gi + self.groups - r) % self.groups
        return pltpu.make_async_remote_copy(
            src_ref=self.src.at[to], dst_ref=self.dst.at[of if arriving else self.gi],
            send_sem=self.sent.at[r], recv_sem=self.came.at[r], device_id=(to, self.ei), device_id_type=MESH,
        )

    def own(self):
        return pltpu.make_async_copy(self.src.at[self.gi], self.dst.at[self.gi], self.local)

    def start(self):
        self.own().start()
        for r in range(1, self.groups):
            self.copy(r).start()

    def wait_came(self):
        self.own().wait()
        for r in range(1, self.groups):
            self.copy(r, True).wait_recv()

    def wait_sent(self):
        for r in range(1, self.groups):
            self.copy(r).wait_send()


def exchange_scratch(groups):
    D = pltpu.SemaphoreType.DMA
    return [D((groups,)), D((groups,)), D]


def ag_kernel(dims, halves, shared_rows, *refs):
    if shared_rows:
        src, ex_src, out, ex_out, shared, local_sem, zs, zr, xs, xr, ys, yr, cs, cr, exs, exr, exl, shs, shr, shl = refs
        ex = Exchange(dims[0] * dims[1], ex_src, ex_out, exs, exr, exl)
    else:
        src, out, local_sem, zs, zr, xs, xr, ys, yr, cs, cr = refs
        ex = None
    nz, nx, ny = dims
    gi = lax.axis_index("grp"); ei = lax.axis_index("exp")
    z, x = gi // nx, gi % nx
    y, c = ei // 2, ei % 2
    ne = ny * 2
    rows = src.shape[0]
    part = rows // halves
    def dev(z_, x_, y_, c_):
        return (z_ * nx + x_, y_ * 2 + c_)
    def slot(z_, x_, y_, c_):
        return (z_ * nx + x_) * ne + y_ * 2 + c_
    barrier = pltpu.get_barrier_semaphore()
    def sig(d):
        pl.semaphore_signal(barrier, inc=1, device_id=d, device_id_type=MESH)
    sig(dev(z, x, 1 - y, c))
    sig(dev(z, x, y, 1 - c))
    if ex is None:
        sig(dev(z, 1 - x, y, c))
        pl.when(z > 0)(lambda: sig(dev(z - 1, x, y, c)))
        pl.when(z < nz - 1)(lambda: sig(dev(z + 1, x, y, c)))
        pl.semaphore_wait(barrier, 3 + (z > 0).astype(jnp.int32) + (z < nz - 1).astype(jnp.int32))
    else:
        for peer in ex.peers():
            sig(peer)
        pl.semaphore_wait(barrier, 2 + len(ex.peers()))
    own = pltpu.make_async_copy(src, out.at[slot(z, x, y, c)], local_sem)
    own.start()
    span = 2 * nz - 1
    def piece(sl, h):
        return out.at[sl, pl.ds(h * part, part)]
    def copy(sl, h, is_own, ssem, rsem, d):
        s = src.at[pl.ds(h * part, part)] if is_own else piece(sl, h)
        return pltpu.make_async_remote_copy(src_ref=s, dst_ref=piece(sl, h), send_sem=ssem, recv_sem=rsem, device_id=d, device_id_type=MESH)
    def zcopy(h, delta, direction, arriving):
        zz = z - delta * direction
        k = (h * 2 + (0 if direction > 0 else 1)) * nz
        if arriving:
            return copy(slot(zz, x, y, c), h, False, zs.at[k + delta], zr.at[k + delta], dev(z, x, y, c) if False else dev(z, x, y, 1 - c))
        return copy(slot(zz, x, y, c), h, delta == 0, zs.at[k + delta + 1], zr.at[k + delta + 1], dev(z + direction, x, y, c))
    def valid(delta):
        zz = z + delta
        return (zz >= 0) & (zz < nz)
    def when(cond, f):
        pl.when(cond)(f)
    sends = []
    def order(h):
        return ("x", "y") if h % 2 == 0 else ("y", "x")
    def first(h, delta):
        a = order(h)[0]
        sems = (xs, xr) if a == "x" else (ys, yr)
        k = h * 2 * span + delta + nz - 1
        d = dev(z, 1 - x, y, c) if a == "x" else dev(z, x, 1 - y, c)
        return copy(slot(z + delta, x, y, c), h, delta == 0, sems[0].at[k], sems[1].at[k], d), (
            lambda: copy(slot(z + delta, 1 - x if a == "x" else x, 1 - y if a == "y" else y, c), h, False, sems[0].at[k], sems[1].at[k], d))
    def second(h, delta, rel):
        a0, a = order(h)
        sems = (xs, xr) if a == "x" else (ys, yr)
        k = h * 2 * span + (rel * span) + delta + nz - 1
        d = dev(z, 1 - x, y, c) if a == "x" else dev(z, x, 1 - y, c)
        x0 = (1 - x if rel else x) if a0 == "x" else x
        y0 = (1 - y if rel else y) if a0 == "y" else y
        snd = copy(slot(z + delta, x0, y0, c), h, delta == 0 and rel == 0, sems[0].at[k], sems[1].at[k], d)
        x1 = 1 - x if a == "x" else x0
        y1 = 1 - y if a == "y" else y0
        rcv = copy(slot(z + delta, x1, y1, c), h, False, sems[0].at[k], sems[1].at[k], d)
        return snd, rcv
    def core(h, delta, rx, ry):
        k = h * 4 * span + (rx * 2 + ry) * span + delta + nz - 1
        d = dev(z, x, y, 1 - c)
        xx = 1 - x if rx else x
        yy = 1 - y if ry else y
        return (copy(slot(z + delta, xx, yy, c), h, delta == 0 and not rx and not ry, cs.at[k], cr.at[k], d),
                copy(slot(z + delta, xx, yy, 1 - c), h, False, cs.at[k], cr.at[k], d))
    hs = range(halves)
    def have_z(delta):
        for h in hs:
            if delta <= 0:
                when(z < nz - 1, lambda h=h: zcopy(h, -delta, 1, False).start())
            if delta >= 0:
                when(z > 0, lambda h=h: zcopy(h, delta, -1, False).start())
            first(h, delta)[0].start()
            second(h, delta, 0)[0].start()
            core(h, delta, 0, 0)[0].start()
    have_z(0)
    def share(n):
        part = ex_out.at[:, pl.ds(ex_out.shape[1] - shared_rows, shared_rows)]
        number = (1 - y if n == 2 else y) * 2 + c
        return pltpu.make_async_remote_copy(
            src_ref=shared.at[:, number] if n == 2 else part, dst_ref=shared.at[:, number],
            send_sem=shs.at[n], recv_sem=shr.at[n],
            device_id=dev(z, x, 1 - y, c) if n == 0 else dev(z, x, y, 1 - c), device_id_type=MESH,
        )
    def share_own():
        part = ex_out.at[:, pl.ds(ex_out.shape[1] - shared_rows, shared_rows)]
        return pltpu.make_async_copy(part, shared.at[:, y * 2 + c], shl)
    def shared_came(n):
        number = ((1 - y) * 2 + c, y * 2 + 1 - c, (1 - y) * 2 + 1 - c)[n]
        return pltpu.make_async_remote_copy(
            src_ref=shared.at[:, number], dst_ref=shared.at[:, number], send_sem=shs.at[n], recv_sem=shr.at[n],
            device_id=dev(z, x, y, 1 - c), device_id_type=MESH,
        )
    if ex is not None:
        ex.start()
    def get_z(delta):
        def f():
            for h in hs:
                zcopy(h, abs(delta), -1 if delta > 0 else 1, True).wait_recv()
            have_z(delta)
        when(valid(delta), f)
    def get_first(delta):
        def f():
            for h in hs:
                first(h, delta)[1]().wait_recv()
                second(h, delta, 1)[0].start()
                rx = 1 if order(h)[0] == "x" else 0
                core(h, delta, rx, 1 - rx)[0].start()
        when(valid(delta), f)
    def get_second(delta):
        def f():
            for h in hs:
                for rel in range(2):
                    second(h, delta, rel)[1].wait_recv()
                    a0, a = order(h)
                    rx = 1 if a == "x" else (rel if a0 == "x" else 0)
                    ry = 1 if a == "y" else (rel if a0 == "y" else 0)
                    core(h, delta, rx, ry)[0].start()
        when(valid(delta), f)
    for step in range(nz + 2):
        for dist, fn in ((step, get_z), (step - 1, get_first), (step - 2, get_second)):
            if 0 <= dist < nz:
                if dist == 0:
                    if fn is not get_z: fn(0)
                else:
                    fn(-dist); fn(dist)
        if ex is not None and step == nz - 1:
            ex.wait_came()
            share_own().start()
            share(0).start()
            share(1).start()
        if ex is not None and step == nz + 1:
            shared_came(0).wait_recv()
            share(2).start()
    own.wait()
    if ex is not None:
        shared_came(1).wait_recv()
        shared_came(2).wait_recv()
        share_own().wait()
        for n in range(3):
            share(n).wait_send()
        ex.wait_sent()
    for delta in range(-(nz - 1), nz):
        def f(delta=delta):
            for h in hs:
                for rx in range(2):
                    for ry in range(2):
                        a, b = core(h, delta, rx, ry)
                        b.wait_recv(); a.wait_send()
                first(h, delta)[0].wait_send()
                for rel in range(2):
                    second(h, delta, rel)[0].wait_send()
                if delta <= 0:
                    when(z < nz - 1, lambda h=h: zcopy(h, -delta, 1, False).wait_send())
                if delta >= 0:
                    when(z > 0, lambda h=h: zcopy(h, delta, -1, False).wait_send())
        when(valid(delta), f)

def gather_kernel(v, dims, cid, exchanged=None, shared_rows=0, halves=2):
    nz, nx, ny = dims
    n = nz * nx * ny * 2
    span = 2 * nz - 1
    D = pltpu.SemaphoreType.DMA
    hbm = pl.BlockSpec(memory_space=pl.ANY)
    operands, out_shape, more = [v], [jax.ShapeDtypeStruct((n,) + v.shape, v.dtype)], []
    if shared_rows:
        e = exchanged
        operands += [e]
        out_shape += [jax.ShapeDtypeStruct(e.shape, e.dtype), jax.ShapeDtypeStruct((e.shape[0], ny * 2, shared_rows, e.shape[2]), e.dtype)]
        more = exchange_scratch(nz * nx) + [D((3,)), D((3,)), D]
    out = pl.pallas_call(
        functools.partial(ag_kernel, dims, halves, shared_rows),
        out_shape=out_shape,
        in_specs=[hbm] * len(operands),
        out_specs=[hbm] * len(out_shape),
        scratch_shapes=[D] + [D((halves * 2 * (nz + 1),))] * 2 + [D((halves * 2 * span,))] * 4 + [D((halves * 4 * span,))] * 2 + more,
        compiler_params=pltpu.CompilerParams(collective_id=cid, has_side_effects=True),
    )(*operands)
    return out if shared_rows else out[0]


def target_order(nz):
    low, high, order = 0, nz - 1, []
    while low <= high:
        order += [low] if low == high else [low, high]
        low, high = low + 1, high - 1
    return order


def tile_group(i, dims):
    nz, nx, _ = dims
    i = jnp.minimum(i, nz * nx - 1)
    j = i // nx
    t = jnp.where(j % 2 == 0, j // 2, nz - 1 - j // 2)
    return t * nx + i % nx


class Place:
    def __init__(self, dims):
        self.nz, self.nx, self.ny = dims
        gi, ei = lax.axis_index("grp"), lax.axis_index("exp")
        self.z, self.x = gi // self.nx, gi % self.nx
        self.y, self.c = ei // 2, ei % 2

    def device(self, z, x, y, c):
        return (z * self.nx + x, y * 2 + c)

    def core(self):
        return self.device(self.z, self.x, self.y, 1 - self.c)

    def along_x(self):
        return self.device(self.z, 1 - self.x, self.y, self.c)

    def along_y(self):
        return self.device(self.z, self.x, 1 - self.y, self.c)

    def along_z(self, by):
        return self.device(self.z + by, self.x, self.y, self.c)

    def greet(self):
        barrier = pltpu.get_barrier_semaphore()

        def signal(device):
            pl.semaphore_signal(barrier, inc=1, device_id=device, device_id_type=MESH)

        signal(self.along_x())
        signal(self.along_y())
        signal(self.core())
        pl.when(self.z > 0)(lambda: signal(self.along_z(-1)))
        pl.when(self.z < self.nz - 1)(lambda: signal(self.along_z(1)))

    def greet_plane(self):
        barrier = pltpu.get_barrier_semaphore()
        groups = self.nz * self.nx
        gi, ei = lax.axis_index("grp"), lax.axis_index("exp")
        peers = [((gi + r) % groups, ei) for r in range(1, groups)] + [self.along_y(), self.core()]
        for device in peers:
            pl.semaphore_signal(barrier, inc=1, device_id=device, device_id_type=MESH)

    def greeted_plane(self):
        pl.semaphore_wait(pltpu.get_barrier_semaphore(), self.nz * self.nx + 1)

    def greeted(self):
        inner = (self.z > 0).astype(jnp.int32) + (self.z < self.nz - 1).astype(jnp.int32)
        pl.semaphore_wait(pltpu.get_barrier_semaphore(), 3 + inner)


def remote(src, dst, sent, came, device):
    return pltpu.make_async_remote_copy(
        src_ref=src, dst_ref=dst, send_sem=sent, recv_sem=came, device_id=device, device_id_type=MESH
    )


def scatter_scratch(dims, rows, width):
    nz, nx, _ = dims
    tiles, half = nz * nx, rows // 2
    D, V = pltpu.SemaphoreType.DMA, lambda *s: pltpu.VMEM(s, bf16)
    return [
        V(2, 4 * rows, width),
        V(2, 2, rows, width),
        V(tiles, 2, rows, width),
        V(tiles, half, width), V(nz, 2, half, width),
        V(nz, half, width), V(nz, half, width),
        V(nz + 1, rows, width),
        D((tiles * 2,)), D((tiles * 2,)), D((tiles,)), D((tiles,)), D((nz * 2,)), D((nz * 2,)),
        D((nz,)), D((nz,)), D((nz,)), D((nz,)), D((nz * 2,)), D((nz * 2 + 2,)),
    ]


SCATTER_REFS = 20


class Scatter:
    def __init__(self, dims, place, out, refs):
        self.dims, self.place, self.out = dims, place, out
        (self.tile, self.crv, self.acc, self.ya, self.xb, self.xa, self.yb, self.zv,
         self.cs, self.cr, self.yas, self.yar, self.xbs, self.xbr,
         self.xas, self.xar, self.ybs, self.ybr, self.zs, self.zr) = refs
        self.rows = out.shape[0]
        self.half = self.rows // 2
        self.order = target_order(dims[0])
        self.tiles = dims[0] * dims[1]
        self.steps = self.tiles + 2 + dims[0]

    def add(self, into, *others):
        def step(r, _):
            at = rows_at(r, 16)
            total = others[0][at, :].astype(f32)
            for o in others[1:]:
                total = total + o[at, :].astype(f32)
            into[at, :] = total.astype(into.dtype)
            return 0

        lax.fori_loop(0, into.shape[0] // 16, step, 0)

    def low(self, k, q):
        return self.acc.at[k, q, pl.ds(0, self.half)]

    def high(self, k, q):
        return self.acc.at[k, q, pl.ds(self.half, self.half)]

    def shard(self, k, q, c):
        return self.tile.at[k % 2, rows_at(q * 2 + c, self.rows)]

    def c_core(self, k, q):
        p, s = self.place, k * 2 + q
        return remote(self.shard(k, q, 1 - p.c), self.crv.at[k % 2, q], self.cs.at[s], self.cr.at[s], p.core())

    def c_ya(self, k):
        p = self.place
        return remote(self.low(k, 1 - p.y), self.ya.at[k], self.yas.at[k], self.yar.at[k], p.along_y())

    def c_xb(self, k, q):
        p, j = self.place, k // 2
        s = j * 2 + q
        return remote(self.high(k, q), self.xb.at[j, q], self.xbs.at[s], self.xbr.at[s], p.along_x())

    def c_xa(self, k):
        p, j = self.place, k // 2
        return remote(self.low(k, p.y), self.xa.at[j], self.xas.at[j], self.xar.at[j], p.along_x())

    def c_yb(self, k):
        p, j = self.place, k // 2
        return remote(self.high(k, 1 - p.y), self.yb.at[j], self.ybs.at[j], self.ybr.at[j], p.along_y())

    def own_half(self, k, h):
        return self.acc.at[k, self.place.y, pl.ds(h * self.half, self.half)]

    def z_half(self, slot, h):
        return self.zv.at[slot, pl.ds(h * self.half, self.half)]

    def c_z(self, k, way, h):
        p, t = self.place, self.order[k // 2]
        slot = t if way > 0 else jnp.where(p.z - 1 == t, self.dims[0], t)
        return remote(self.own_half(k, h), self.z_half(slot, h), self.zs.at[t * 2 + h], self.zr.at[slot * 2 + h], p.along_z(way))

    def z_wait(self, k, slot, h):
        remote(self.own_half(k, h), self.z_half(slot, h), self.zs.at[h], self.zr.at[slot * 2 + h], self.place.core()).wait_recv()

    def phase_s(self, k):
        for q in range(2):
            self.c_core(k, q).start()

    def phase_b(self, k):
        p = self.place
        away = p.x != k % 2
        for q in (1 - p.y, p.y):
            self.c_core(k, q).wait_recv()
            self.add(self.acc.at[k, q], self.shard(k, q, p.c), self.crv.at[k % 2, q])
            if q is not p.y:
                self.c_ya(k).start()
            pl.when(away)(lambda q=q: self.c_xb(k, q).start())
        for q in range(2):
            self.c_core(k, q).wait_send()

    def phase_c(self, k):
        p, j = self.place, k // 2

        def give():
            self.c_ya(k).wait_recv()
            self.add(self.low(k, p.y), self.low(k, p.y), self.ya.at[k])
            self.c_xa(k).start()

        def keep():
            self.c_xb(k, 1 - p.y).wait_recv()
            self.add(self.high(k, 1 - p.y), self.high(k, 1 - p.y), self.xb.at[j, 1 - p.y])
            self.c_yb(k).start()

        pl.when(p.x != k % 2)(give)
        pl.when(p.x == k % 2)(keep)

    def phase_d(self, k):
        p, j, t, nz = self.place, k // 2, self.order[k // 2], self.dims[0]

        def ends(h):
            if t > 0:
                pl.when(p.z == 0)(lambda: self.c_z(k, 1, h).start())
            if t < nz - 1:
                pl.when(p.z == nz - 1)(lambda: self.c_z(k, -1, h).start())

        def keep():
            self.c_ya(k).wait_recv()
            self.c_xa(k).wait_recv()
            self.add(self.low(k, p.y), self.low(k, p.y), self.ya.at[k], self.xa.at[j])
            ends(0)
            self.c_xb(k, p.y).wait_recv()
            self.c_yb(k).wait_recv()
            self.add(self.high(k, p.y), self.high(k, p.y), self.xb.at[j, p.y], self.yb.at[j])
            ends(1)

        pl.when(p.x == k % 2)(keep)

    def phase_e(self, k, hop):
        p, t, nz = self.place, self.order[k // 2], self.dims[0]
        mine = p.x == k % 2

        def pass_on(way):
            def run():
                for h in range(2):
                    self.z_wait(k, t, h)
                    self.add(self.own_half(k, h), self.own_half(k, h), self.z_half(t, h))
                    self.c_z(k, way, h).start()

            return run

        if hop < t:
            pl.when(mine & (p.z == hop))(pass_on(1))
        if nz - 1 - hop > t:
            pl.when(mine & (p.z == nz - 1 - hop))(pass_on(-1))
        if hop == max(t, nz - 1 - t):

            def last():
                for h in range(2):
                    others = [self.own_half(k, h)]
                    for there, slot in ((t > 0, t), (t < nz - 1, nz)):
                        if there:
                            self.z_wait(k, slot, h)
                            others.append(self.z_half(slot, h))
                    self.add(self.out.at[pl.ds(h * self.half, self.half)], *others)

            pl.when(mine & (p.z == t))(last)

    def drain(self):
        p = self.place
        for k in range(self.tiles):
            self.c_ya(k).wait_send()

            def give(k=k):
                self.c_xa(k).wait_send()
                for q in range(2):
                    self.c_xb(k, q).wait_send()

            def keep(k=k):
                self.c_yb(k).wait_send()

                def along(k=k):
                    for h in range(2):
                        self.c_z(k, 1, h).wait_send()

                pl.when(p.z != self.order[k // 2])(along)

            pl.when(p.x != k % 2)(give)
            pl.when(p.x == k % 2)(keep)

    def run(self, i):
        for step in range(self.steps):

            def phases(step=step):
                for lag, phase in ((1, self.phase_b), (0, self.phase_s), (2, self.phase_c), (3, self.phase_d)):
                    if 0 <= step - lag < self.tiles:
                        phase(step - lag)
                for h in range(1, self.dims[0]):
                    if 0 <= step - 3 - h < self.tiles:
                        self.phase_e(step - 3 - h, h)
                if step == self.steps - 1:
                    self.drain()

            pl.when(i == step)(phases)


def scatter_kernel_body(dims, src, out, *refs):
    i = pl.program_id(0)
    place = Place(dims)
    s = Scatter(dims, place, out, refs)

    @pl.when(i == 0)
    def _():
        place.greet()
        place.greeted()

    @pl.when(i < s.tiles)
    def _():
        def copy(r):
            at = rows_at(r, 64)
            s.tile[i % 2, at, :] = src[at, :]
        loop(src.shape[0] // 64, copy)

    s.run(i)


def scatter_kernel(p, dims, cid):
    nz, nx, ny = dims
    n, rows, width = p.shape
    groups = nz * nx
    p = p.reshape(n * rows, width)
    return pl.pallas_call(
        functools.partial(scatter_kernel_body, dims),
        grid=(groups + 2 + nz,),
        in_specs=[pl.BlockSpec((4 * rows, width), lambda i: (tile_group(i, dims), 0))],
        out_specs=whole_block((rows, width)),
        out_shape=jax.ShapeDtypeStruct((rows, width), f32),
        scratch_shapes=scatter_scratch(dims, rows, width),
        compiler_params=pltpu.CompilerParams(collective_id=cid, has_side_effects=True, vmem_limit_bytes=60 * MB),
    )(p)


def layout(first, order, block):
    groups, blocks = order.shape
    rows = groups * blocks * block
    step = jnp.arange(block, dtype=jnp.int32)
    anchor = order[:, :, None] * block + step
    late = anchor >= first[:, :, None]
    place = anchor - jnp.where(late, first[:, :, None], 0)
    half = LANES // 2
    freq = jnp.exp(jnp.arange(half, dtype=f32) * (-2.0 * math.log(10000.0) / LANES))
    freq = jnp.concatenate([freq, freq])
    sign = jnp.where(jnp.arange(LANES) < half, -1.0, 1.0)
    inner = step.astype(f32)[:, None] * freq
    start = (order * block).astype(f32)[:, :, None, None] * freq
    moved = (order * block - first).astype(f32)[:, :, None, None] * freq
    chosen_cos = jnp.where(late[..., None], jnp.cos(moved), jnp.cos(start))
    chosen_sin = jnp.where(late[..., None], jnp.sin(moved), jnp.sin(start))
    cos = jnp.cos(inner) * chosen_cos - jnp.sin(inner) * chosen_sin
    sin = (jnp.sin(inner) * chosen_cos + jnp.cos(inner) * chosen_sin) * sign
    flat = lambda v: v.reshape(groups, blocks * block)
    return (flat(anchor), flat(place), cos.reshape(rows, LANES), sin.reshape(rows, LANES))


def logit_grad(route, gates, difference, experts):
    moved = gates[:, 0:1] * gates[:, 1:2] * difference
    names = jnp.arange(experts, dtype=jnp.int32)[None, :]
    return jnp.where(route[:, 0:1] == names, moved, 0.0) - jnp.where(
        route[:, 1:2] == names, moved, 0.0
    )


def norm_back(grad_hidden, normed, inverse, gain):
    grad_normed = grad_hidden * gain
    gain_grad = jnp.sum(grad_hidden * normed, axis=0)
    mean_term = jnp.mean(grad_normed * normed, axis=1, keepdims=True)
    return (inverse * (grad_normed - normed * mean_term), gain_grad)


def body(
    dims,
    layer_input,
    out_grad,
    doc_lengths,
    block_order,
    attn_route,
    ffn_route,
    norm_gains,
    kv_master,
    router_master,
    query_master,
    output_master,
    gate_up_master,
    down_master,
):
    own_rows, width = layer_input.shape
    members, groups = lax.axis_size("exp"), lax.axis_size("grp")
    member, group = lax.axis_index("exp"), lax.axis_index("grp")
    experts = members
    capacity = 3 * own_rows // experts
    group_rows = own_rows * members
    total = group_rows * groups
    devices = groups * members
    cw = width // groups
    depth = kv_master.shape[0]
    scale = 1.0 / math.sqrt(LANES)
    me = member.reshape(1).astype(jnp.int32)
    both = ("grp", "exp")

    def gather_all(v, cid):
        if dims is None:
            return lax.all_gather(kept(v), both, axis=0, tiled=True)
        return gather_kernel(v, dims, cid)

    def scatter_all(v, cid):
        v = v.reshape(devices, own_rows, v.shape[-1])
        if dims is None:
            return lax.psum_scatter(v, both, scatter_dimension=0, tiled=False).astype(f32)
        return scatter_kernel(v, dims, cid)

    def summed(parts):
        return jnp.concatenate([scatter_all(v, 0) for v in parts], axis=1) if dims is None else parts[0]

    blocks = block_order.shape[1]
    start_row = member * own_rows
    own_attn_route = lax.dynamic_slice_in_dim(attn_route, start_row, own_rows)
    own_ffn_route = lax.dynamic_slice_in_dim(ffn_route, start_row, own_rows)
    tall = lambda v: jnp.pad(v.astype(bf16), ((0, own_rows - v.shape[0]), (0, 0)))
    first_doc = doc_lengths[:, 0]
    small = jnp.concatenate(
        [
            tall(norm_gains),
            tall(router_master),
            own_attn_route.astype(bf16),
            own_ffn_route.astype(bf16),
            tall(jnp.concatenate([first_doc // 16, first_doc % 16, block_order[0]])[:, None]),
        ],
        axis=1,
    )
    at_route = 2 + 2 * experts
    small = jnp.pad(small, ((0, 0), (0, LANES - small.shape[1])))

    query_low = query_master[0].astype(bf16)
    kv_low = kv_master.astype(bf16).reshape(depth, 2, groups, cw).transpose(1, 0, 2, 3).reshape(2 * depth, groups, cw)
    query_rows = query_low.shape[0]
    pieces_out = jnp.concatenate([query_low.reshape(query_rows, groups, cw), kv_low], axis=0).transpose(1, 0, 2)
    if dims is None:
        tokens = gather_all(layer_input, 1).reshape(total, width)
        extra = gather_all(small, 2).reshape(total, LANES)
        pieces_in = lax.all_to_all(pieces_out, "grp", split_axis=0, concat_axis=0, tiled=True)
        kv_all = lax.all_gather(pieces_in[:, query_rows:], "exp", axis=1, tiled=False)
    else:
        sent = jnp.concatenate([layer_input, small], axis=1)
        tokens, pieces_in, kv_all = gather_kernel(sent, dims, 1, pieces_out, 2 * depth)
        tokens = tokens.reshape(total, width + LANES)
        tokens, late_grad = lax.optimization_barrier((tokens, out_grad))
        extra = tokens[:, width:]
    query_weight = pieces_in[:, :query_rows].reshape(width, cw)
    key_weight, value_weight = (kv_all[:, :, at : at + depth].reshape(width, cw) for at in (0, depth))

    output_weight = output_master[0].astype(bf16)

    tables = extra.reshape(devices, own_rows, LANES)[:, :depth, :at_route].reshape(width, at_route)
    gains = tables[:, :2].astype(f32)
    router = tables[:, 2:]
    router_float = router.astype(f32)
    wide = lambda v: jnp.pad(v, ((0, 0), (0, LANES - v.shape[1])))
    routes = extra[:, at_route : at_route + 4].astype(jnp.int32)
    column = extra.reshape(groups, group_rows, LANES)[:, : blocks + 2, at_route + 4].astype(jnp.int32)

    def where_rows_stand(column):
        first = column[:, 0:1] * 16 + column[:, 1:2]
        anchor, place, cos, sin = layout(first, column[:, 2:], own_rows // 2)
        meta = jnp.concatenate(
            [anchor.reshape(total, 1), (anchor - place).reshape(total, 1), routes, routes[:, :2]], axis=1
        )
        return cos, sin, meta, jnp.broadcast_to(anchor[:, None, :], (groups, 8, group_rows))

    cos, sin, meta, key_rows = where_rows_stand(column)
    gain_one, gain_two = gains[:, 0], gains[:, 1]
    w_all = jnp.concatenate([query_weight, key_weight, value_weight, wide(router[:, :experts])], axis=1)

    qkv, att, aux, wg, wu, wd, attn_sum = attn_forward(
        dims, 3, me, tokens, gain_one[None], w_all, output_weight, cos, sin, meta, key_rows,
        gate_up_master[0], down_master[0], groups, scale,
    )
    own = (group * members + member) * own_rows
    attn_gates = lax.dynamic_slice(aux, (own, 2), (own_rows, 2))
    inputs = layer_input.astype(f32)
    middle = inputs + summed([attn_sum])
    inverse_two = lax.rsqrt(jnp.mean(middle * middle, axis=1, keepdims=True) + epsilon)
    normed_two = middle * inverse_two
    hidden_two = (normed_two * gain_two).astype(bf16)
    if dims is None:
        late_grad, hidden_two = lax.optimization_barrier((out_grad, hidden_two))
    h2 = gather_all(hidden_two, 4).reshape(total, width)
    tops = lax.all_gather(late_grad, both, axis=0, tiled=True)

    if is_dense(capacity):
        position = jnp.zeros((devices, own_rows), jnp.int32)
    else:
        named = ((routes[:, 2] == member) | (routes[:, 3] == member)).reshape(devices, own_rows)
        position = jnp.where(named, jnp.cumsum(named.astype(jnp.int32), axis=1) - 1, -1)
    tile_blocks = 4
    position = position.reshape(devices // tile_blocks, tile_blocks, own_rows)
    produced, ffn_aux, act, dgate, dup, *dh2_parts = ffn(
        dims, 5, me, h2, tops, wide(router[:, experts:]), meta, position,
        wg, wu, wd, capacity,
    )
    if dims is None:
        gate_up_grad, down_grad = ffn_weights(
            dims, 0, h2, tops, ffn_aux, position, act, dgate, dup, None, None, None, None, capacity
        )
        gate_up_grad, dh2_parts, produced = lax.optimization_barrier((gate_up_grad, dh2_parts, produced))
        back = summed(dh2_parts)
        produced, back = lax.optimization_barrier((produced, back))
        ffn_sum = scatter_all(produced, 0)
        ffn_sum, back = lax.optimization_barrier((ffn_sum, back))
    else:
        back = summed(dh2_parts)
    ffn_gates = lax.dynamic_slice(ffn_aux, (own, 2), (own_rows, 2))
    top_grad = out_grad.astype(f32)
    ffn_logit_grad = logit_grad(own_ffn_route, ffn_gates, back[:, width : width + 1], experts)
    hidden_two_grad = back[:, :width] + jnp.einsum(
        "te,de->td", ffn_logit_grad, router_float[:, experts:], precision=highest
    )
    middle_part, gain_two_grad = norm_back(hidden_two_grad, normed_two, inverse_two, gain_two)
    middle_grad = top_grad + middle_part
    dmid = gather_all(middle_grad.astype(bf16), 6).reshape(total, width)

    if dims is None:
        again, dmid = lax.optimization_barrier((layer_input, dmid))
        tokens = gather_all(again, 9).reshape(total, width)
        column, dmid = lax.optimization_barrier((column, dmid))
        cos, sin, meta, key_rows = where_rows_stand(column)
    dw, do, *dh1_parts = attn_backward(
        dims, 8, dmid, tokens, gain_one[None], qkv, att, aux, cos, sin, meta, key_rows, w_all, output_weight, groups, scale
    )
    back = summed(dh1_parts)
    inverse_one = lax.rsqrt(jnp.mean(inputs * inputs, axis=1, keepdims=True) + epsilon)
    normed_one = inputs * inverse_one
    hidden_one = (normed_one * gain_one).astype(bf16)
    attn_logit_grad = logit_grad(own_attn_route, attn_gates, back[:, width : width + 1], experts)
    hidden_one_grad = back[:, :width] + jnp.einsum(
        "te,de->td", attn_logit_grad, router_float[:, :experts], precision=highest
    )
    input_part, gain_one_grad = norm_back(hidden_one_grad, normed_one, inverse_one, gain_one)
    input_grad = middle_grad + input_part
    route_grad = [
        jnp.einsum("td,te->de", a.astype(f32), b, precision=highest)
        for a, b in ((hidden_one, attn_logit_grad), (hidden_two, ffn_logit_grad))
    ]
    sums = jnp.concatenate(
        [gain_one_grad[:, None], gain_two_grad[:, None], route_grad[0], route_grad[1]], axis=1
    )

    if dims is None:
        sums = lax.psum_scatter(sums, both, scatter_dimension=0, tiled=True)
        kv_part = dw[cw:].reshape(2 * cw, groups, members, depth)
        kv_part = lax.psum_scatter(kv_part.astype(bf16), "exp", scatter_dimension=2, tiled=False)
        query_part = dw[:cw].astype(bf16).reshape(cw, groups, width // groups)
        pieces_out = jnp.concatenate(
            [query_part.transpose(1, 0, 2).reshape(groups, -1), kv_part.transpose(1, 0, 2).reshape(groups, -1)],
            axis=1,
        )
        pieces_in = lax.all_to_all(pieces_out, "grp", split_axis=0, concat_axis=0, tiled=True)
        cut = cw * (width // groups)
        query_part = pieces_in[:, :cut].reshape(width, width // groups)
        kv_part = pieces_in[:, cut:].reshape(groups, 2, cw, depth).transpose(1, 0, 2, 3)
    else:
        beside = jnp.pad(
            sums.astype(bf16).reshape(devices, depth, sums.shape[1]),
            ((0, 0), (0, own_rows - depth), (0, LANES - sums.shape[1])),
        ).reshape(total, LANES)
        low = dw.astype(bf16)
        query_part = low[:cw].reshape(cw, groups, width // groups).transpose(1, 0, 2)
        kv_part = low[cw:].reshape(2, cw, groups, members // 2, LANES).transpose(0, 3, 2, 1, 4)
        gate_up_grad, down_grad, ffn_sum, query_part, kv_own, kv_other = ffn_weights(
            dims, 7, h2, tops, ffn_aux, position, act, dgate, dup, beside, produced, query_part, kv_part, capacity
        )
        sums = ffn_sum[:depth, width : width + sums.shape[1]]
        ffn_sum = ffn_sum[:, :width]
        query_part = query_part.reshape(width, width // groups)
        core = member % 2
        kv_part = jnp.where(core == 0, jnp.stack([kv_own, kv_other]), jnp.stack([kv_other, kv_own]))
        kv_part = lax.dynamic_slice_in_dim(kv_part, core * depth, depth, axis=3)
    final = middle + ffn_sum
    query_grad = query_part.T.astype(f32)
    kv_grad = kv_part.reshape(2 * width, depth).T.astype(f32)
    return (
        final.astype(bf16),
        input_grad,
        sums[:, :2],
        kv_grad,
        sums[:, 2:],
        query_grad[None],
        do[None],
        gate_up_grad[None],
        down_grad[None],
    )


def solution(mesh):
    groups, members = mesh.shape["grp"], mesh.shape["exp"]
    dims = (groups // 2, 2, members // 2) if groups <= 8 and members == 4 else None
    in_specs = (
        P(("grp", "exp"), None),
        P(("grp", "exp"), None),
        P("grp", None),
        P("grp", None),
        P("grp", None),
        P("grp", None),
        P(("grp", "exp"), None),
        P(("grp", "exp"), None),
        P(("grp", "exp"), None),
        P("exp", "grp", None),
        P("exp", "grp", None),
        P("exp", "grp", None, None),
        P("exp", "grp", None),
    )
    out_specs = (
        P(("grp", "exp"), None),
        P(("grp", "exp"), None),
        P(("grp", "exp"), None),
        P(("grp", "exp"), None),
        P(("grp", "exp"), None),
        P("exp", "grp", None),
        P("exp", "grp", None),
        P("exp", "grp", None, None),
        P("exp", "grp", None),
    )
    return jax.shard_map(
        functools.partial(body, dims),
        mesh=mesh,
        in_specs=in_specs,
        out_specs=out_specs,
        check_vma=False,
    )
```

```python
import functools
import math

import jax
import jax.numpy as jnp
from jax import lax
from jax.experimental import pallas as pl
from jax.experimental.pallas import tpu as pltpu
from jax.sharding import PartitionSpec as P

HEADS = 16
LANES = 128
MESH = pl.DeviceIdType.MESH
MB = 1024 * 1024
UNROLL = 4

epsilon = 1e-05
negative = -1e30
highest = lax.Precision.HIGHEST
f32 = jnp.float32
bf16 = jnp.bfloat16


def nn(a, b):
    return jnp.dot(a, b, preferred_element_type=f32)


def nt(a, b):
    return lax.dot_general(a, b, (((1,), (1,)), ((), ())), preferred_element_type=f32)


def tn(a, b):
    return lax.dot_general(a, b, (((0,), (0,)), ((), ())), preferred_element_type=f32)


def loop(count, step):
    def run(i, carry):
        step(i)
        return carry

    lax.fori_loop(0, count, run, 0)


def rows_at(i, size):
    return pl.ds(pl.multiple_of(i * size, size), size)


def kept(v):
    def copy(src, dst):
        dst[...] = src[...]

    return pl.pallas_call(copy, out_shape=jax.ShapeDtypeStruct(v.shape, v.dtype))(v)


def turn(v, cos, sin):
    return v * cos + pltpu.roll(v, LANES // 2, 1) * sin


def gate_columns(logits, r0, r1, me):
    lane = lax.broadcasted_iota(jnp.int32, logits.shape, 1)
    l0 = jnp.sum(jnp.where(lane == r0, logits, 0.0), axis=1, keepdims=True)
    l1 = jnp.sum(jnp.where(lane == r1, logits, 0.0), axis=1, keepdims=True)
    top = jnp.maximum(l0, l1)
    e0, e1 = jnp.exp(l0 - top), jnp.exp(l1 - top)
    g0, g1 = e0 / (e0 + e1), e1 / (e0 + e1)
    weight = jnp.where(r0 == me, g0, 0.0) + jnp.where(r1 == me, g1, 0.0)
    sign = jnp.where(r0 == me, 1.0, 0.0) - jnp.where(r1 == me, 1.0, 0.0)
    return jnp.where(
        lane == 0,
        weight,
        jnp.where(lane == 1, sign, jnp.where(lane == 2, g0, jnp.where(lane == 3, g1, 0.0))),
    )


def attn_forward_kernel(
    cw, scale, me, tokens, gain, w_all, ow, cos, sin, meta, krow, qkv, att, aux, part, h1, inv
):
    count, width = h1.shape
    heads = cw // LANES
    step_rows = min(512, count)

    def normalise(i):
        at = rows_at(i, 64)
        v = tokens[at, :].astype(f32)
        inverse = lax.rsqrt(jnp.mean(v * v, axis=1, keepdims=True) + epsilon)
        inv[at, :] = jnp.broadcast_to(inverse, (64, LANES))
        h1[at, :] = (v * inverse * gain[...]).astype(bf16)

    loop(count // 64, normalise)

    def project(i):
        at = rows_at(i, step_rows)
        y = nn(h1[at, :], w_all[...])
        c, s = cos[at, :], sin[at, :]
        for h in range(2 * heads):
            qkv[at, h * LANES : (h + 1) * LANES] = turn(
                y[:, h * LANES : (h + 1) * LANES], c, s
            ).astype(bf16)
        qkv[at, 2 * cw : 3 * cw] = y[:, 2 * cw : 3 * cw].astype(bf16)
        found = gate_columns(y[:, 3 * cw : 3 * cw + LANES], meta[at, 2:3], meta[at, 3:4], me[0])
        lane = lax.broadcasted_iota(jnp.int32, found.shape, 1)
        aux[at, :] = jnp.where(lane == 4, inv[at, :], found)

    loop(count // step_rows, project)

    def attend(i):
        at = rows_at(i, LANES)
        ak = krow[0, 0:1, :]
        allowed = (ak <= meta[at, 0:1]) & (ak >= meta[at, 1:2])
        old = aux[at, :]
        lane = lax.broadcasted_iota(jnp.int32, old.shape, 1)
        for h in range(heads):
            q = qkv[at, h * LANES : (h + 1) * LANES]
            k = qkv[:, cw + h * LANES : cw + (h + 1) * LANES]
            v = qkv[:, 2 * cw + h * LANES : 2 * cw + (h + 1) * LANES]
            scores = jnp.where(allowed, nt(q, k) * scale, negative)
            top = jnp.max(scores, axis=1, keepdims=True)
            raised = jnp.exp(scores - top)
            total = jnp.sum(raised, axis=1, keepdims=True)
            probs = (raised * (1.0 / total)).astype(bf16)
            att[at, h * LANES : (h + 1) * LANES] = nn(probs, v).astype(bf16)
            old = jnp.where(lane == 8 + h, top + jnp.log(total), old)
        aux[at, :] = old

    lax.fori_loop(0, count // LANES, lambda i, c: (attend(i), c)[1], 0, unroll=UNROLL)

    def output(i):
        at = rows_at(i, step_rows)
        scaled = (aux[at, 0:1] * att[at, :].astype(f32)).astype(bf16)
        part[at, :] = nn(scaled, ow[...]).astype(bf16)

    loop(count // step_rows, output)


def attn_backward_kernel(
    cw, scale, dmid, tokens, gain, qkv, att, aux, cos, sin, meta, krow, w_all, ow,
    dh1, side, dw, do, h1, datt, watt, dqkv, dk_sum, dv_sum,
):
    count, width = h1.shape
    heads = cw // LANES
    step_rows = min(512, count)

    @pl.when(pl.program_id(0) == 0)
    def _():
        dw[...] = jnp.zeros_like(dw)
        do[...] = jnp.zeros_like(do)

    def normalise(i):
        at = rows_at(i, 64)
        h1[at, :] = (tokens[at, :].astype(f32) * aux[at, 4:5] * gain[...]).astype(bf16)

    loop(count // 64, normalise)

    def incoming(i):
        at = rows_at(i, step_rows)
        raw = nt(dmid[at, :], ow[...])
        a = att[at, :].astype(f32)
        weight, sign = aux[at, 0:1], aux[at, 1:2]
        share = sign * jnp.sum(raw * a, axis=1, keepdims=True)
        side[at, :] = jnp.broadcast_to(share, (step_rows, LANES)).astype(bf16)
        datt[at, :] = (weight * raw).astype(bf16)
        watt[at, :] = (weight * a).astype(bf16)

    loop(count // step_rows, incoming)

    def out_weight(i):
        at = rows_at(i, 512)
        do[:, at] += tn(watt[...], dmid[:, at])

    loop(width // 512, out_weight)

    dk_sum[...] = jnp.zeros_like(dk_sum)
    dv_sum[...] = jnp.zeros_like(dv_sum)

    def back(i):
        at = rows_at(i, LANES)
        ak = krow[0, 0:1, :]
        allowed = (ak <= meta[at, 0:1]) & (ak >= meta[at, 1:2])
        for h in range(heads):
            hs = slice(h * LANES, (h + 1) * LANES)
            q, k, v = qkv[at, hs], qkv[:, cw + h * LANES : cw + (h + 1) * LANES], qkv[:, 2 * cw + h * LANES : 2 * cw + (h + 1) * LANES]
            scores = jnp.where(allowed, nt(q, k) * scale, negative)
            probs = jnp.exp(scores - aux[at, 8 + h : 9 + h])
            grad = datt[at, hs]
            dprobs = nt(grad, v)
            inner = jnp.sum(probs * dprobs, axis=1, keepdims=True)
            dscores = (probs * (dprobs - inner)).astype(bf16)
            dqkv[at, hs] = turn(nn(dscores, k) * scale, cos[at, :], -sin[at, :]).astype(bf16)
            dk_sum[:, hs] += tn(dscores, q)
            dv_sum[:, hs] += tn(probs.astype(bf16), grad)

    lax.fori_loop(0, count // LANES, lambda i, c: (back(i), c)[1], 0, unroll=UNROLL)
    for h in range(heads):
        hs = slice(h * LANES, (h + 1) * LANES)
        dqkv[:, cw + h * LANES : cw + (h + 1) * LANES] = turn(dk_sum[:, hs] * scale, cos[...], -sin[...]).astype(bf16)
        dqkv[:, 2 * cw + h * LANES : 2 * cw + (h + 1) * LANES] = dv_sum[:, hs].astype(bf16)

    def to_hidden(i):
        at = rows_at(i, step_rows)
        dh1[at, :width] = nt(dqkv[at, :], w_all[:, : 3 * cw]).astype(bf16)

    loop(count // step_rows, to_hidden)

    def weights(i):
        at = rows_at(i, 512)
        dw[:, at] += tn(dqkv[...], h1[:, at])

    loop(width // 512, weights)


def whole_block(shape):
    return pl.BlockSpec(shape, lambda i: (0,) * len(shape))


def once(shape):
    return pl.BlockSpec(shape, lambda i: (0,) * len(shape), pipeline_mode=pl.Buffered(1))


def attn_forward_plain(cw, scale, me, tokens, gain, w_all, ow, cos, sin, meta, krow, gate_up, down, qkv, att, aux, wg, wu, wd, part, h1, inv, *more):
    i = pl.program_id(0)
    Masters(gate_up, down, wg, wu, wd, *more).step(i, 1, 4)
    attn_forward_kernel(cw, scale, me, tokens, gain, w_all, ow, cos, sin, meta, krow, qkv, att, aux, part, h1, inv)


def attn_forward_fused(dims, cw, scale, me, tokens, gain, w_all, ow, cos, sin, meta, krow, gate_up, down, qkv, att, aux, wg, wu, wd, out, h1, inv, stage, low, sems, out_sems, *refs):
    i = pl.program_id(0)
    place = Place(dims)
    sums = Scatter(dims, place, out, refs)
    Masters(gate_up, down, wg, wu, wd, stage, low, sems, out_sems).step(i, sums.tiles, 5)
    pl.when(i == 0)(place.greet)

    @pl.when(i < sums.tiles)
    def _():
        attn_forward_kernel(cw, scale, me, tokens, gain, w_all, ow, cos, sin, meta, krow, qkv, att, aux, sums.tile.at[i % 2], h1, inv)

    pl.when(i == 0)(place.greeted)
    sums.run(i)


def attn_forward(dims, cid, me, tokens, gain, w_all, ow, cos, sin, meta, krow, gate_up, down, groups, scale):
    total = tokens.shape[0]
    cw, width = ow.shape
    count = total // groups
    at = (lambda i: tile_group(i, dims)) if dims else (lambda i: i)
    row = lambda w: pl.BlockSpec((count, w), lambda i: (at(i), 0))
    hbm = pl.BlockSpec(memory_space=pl.ANY)
    shape = lambda w, t: jax.ShapeDtypeStruct((total, w), t)
    if dims:
        own = count // 4
        kernel = functools.partial(attn_forward_fused, dims, cw, scale)
        last_spec, last_shape = whole_block((own, width)), jax.ShapeDtypeStruct((own, width), f32)
        params, more = dict(collective_id=cid, has_side_effects=True), scatter_scratch(dims, own, width)
    else:
        kernel = functools.partial(attn_forward_plain, cw, scale)
        last_spec, last_shape, params, more = row(width), shape(width, bf16), {}, []
    return pl.pallas_call(
        kernel,
        grid=(groups + 2 + dims[0] if dims else groups,),
        in_specs=[
            pl.BlockSpec(memory_space=pltpu.SMEM), row(width), whole_block(gain.shape),
            once(w_all.shape), once(ow.shape), row(LANES), row(LANES), row(8),
            pl.BlockSpec((1, 8, count), lambda i: (at(i), 0, 0)), hbm, hbm,
        ],
        out_specs=[row(3 * cw), row(cw), row(LANES), hbm, hbm, hbm, last_spec],
        out_shape=[shape(3 * cw, bf16), shape(cw, bf16), shape(LANES, f32)] + [jax.ShapeDtypeStruct(down.shape, bf16)] * 3 + [last_shape],
        scratch_shapes=[pltpu.VMEM((count, width), bf16), pltpu.VMEM((count, LANES), f32)] + masters_scratch(down.shape[0], width) + more,
        compiler_params=pltpu.CompilerParams(vmem_limit_bytes=60 * MB, **params),
    )(me, tokens, gain, w_all, ow, cos, sin, meta, krow, gate_up, down)


def attn_backward_plain(cw, scale, dmid, tokens, gain, qkv, att, aux, cos, sin, meta, krow, w_all, ow, dw_hbm, do_hbm, dh1, side, dw, do, sems, *more):
    attn_backward_kernel(cw, scale, dmid, tokens, gain, qkv, att, aux, cos, sin, meta, krow, w_all, ow, dh1, side, dw, do, *more)
    pl.when(pl.program_id(0) == pl.num_programs(0) - 1)(lambda: attn_weights_out(dw, do, dw_hbm, do_hbm, sems))


def attn_weights_out(dw, do, dw_hbm, do_hbm, sems):
    copies = [pltpu.make_async_copy(a, b, sems.at[n]) for n, (a, b) in enumerate(((dw, dw_hbm), (do, do_hbm)))]
    for c in copies:
        c.start()
    for c in copies:
        c.wait()


def attn_backward_fused(dims, cw, scale, dmid, tokens, gain, qkv, att, aux, cos, sin, meta, krow, w_all, ow, dw_hbm, do_hbm, out, dw, do, sems, h1, datt, watt, dqkv, dk_sum, dv_sum, *refs):
    i = pl.program_id(0)
    place = Place(dims)
    sums = Scatter(dims, place, out, refs)
    pl.when(i == 0)(place.greet)

    @pl.when(i < sums.tiles)
    def _():
        tile, side = sums.tile.at[i % 2], sums.tile.at[i % 2, :, pl.ds(dmid.shape[1], LANES)]
        attn_backward_kernel(cw, scale, dmid, tokens, gain, qkv, att, aux, cos, sin, meta, krow, w_all, ow, tile, side, dw, do, h1, datt, watt, dqkv, dk_sum, dv_sum)

    pl.when(i == 0)(place.greeted)
    sums.run(i)
    pl.when(i == sums.tiles)(lambda: attn_weights_out(dw, do, dw_hbm, do_hbm, sems))


def attn_backward(dims, cid, dmid, tokens, gain, qkv, att, aux, cos, sin, meta, krow, w_all, ow, groups, scale):
    total, width = dmid.shape
    cw = ow.shape[0]
    count = total // groups
    at = (lambda i: tile_group(i, dims)) if dims else (lambda i: i)
    row = lambda w: pl.BlockSpec((count, w), lambda i: (at(i), 0))
    wide = width + LANES
    hbm = pl.BlockSpec(memory_space=pl.ANY)
    if dims:
        own = count // 4
        kernel = functools.partial(attn_backward_fused, dims, cw, scale)
        last_spec, last_shape = [whole_block((own, wide))], [jax.ShapeDtypeStruct((own, wide), f32)]
        params, more = dict(collective_id=cid, has_side_effects=True), scatter_scratch(dims, own, wide)
    else:
        kernel = functools.partial(attn_backward_plain, cw, scale)
        last_spec = [row(width), row(LANES)]
        last_shape = [jax.ShapeDtypeStruct((total, w), bf16) for w in (width, LANES)]
        params, more = {}, []
    return pl.pallas_call(
        kernel,
        grid=(groups + 2 + dims[0] if dims else groups,),
        in_specs=[
            row(width), row(width), whole_block(gain.shape), row(3 * cw), row(cw), row(LANES), row(LANES), row(LANES), row(8),
            pl.BlockSpec((1, 8, count), lambda i: (at(i), 0, 0)),
            once(w_all.shape), once(ow.shape),
        ],
        out_specs=[hbm, hbm] + last_spec,
        out_shape=[jax.ShapeDtypeStruct((3 * cw, width), f32), jax.ShapeDtypeStruct((cw, width), f32)] + last_shape,
        scratch_shapes=[
            pltpu.VMEM((3 * cw, width), f32), pltpu.VMEM((cw, width), f32), pltpu.SemaphoreType.DMA((2,)),
            pltpu.VMEM((count, width), bf16), pltpu.VMEM((count, cw), bf16), pltpu.VMEM((count, cw), bf16), pltpu.VMEM((count, 3 * cw), bf16),
            pltpu.VMEM((count, cw), f32), pltpu.VMEM((count, cw), f32),
        ] + more,
        compiler_params=pltpu.CompilerParams(vmem_limit_bytes=62 * MB, **params),
    )(dmid, tokens, gain, qkv, att, aux, cos, sin, meta, krow, w_all, ow)


def pieces(total, size):
    return [(at, min(size, total - at)) for at in range(0, total, size)]


def chosen(posrow, i, cap):
    slot = lax.broadcasted_iota(jnp.int32, (cap, LANES), 0)
    return (slot == posrow[0, pl.ds(i, 1), :]).astype(bf16)


def is_dense(cap):
    return 2 * cap > LANES


def chosen_scratch(cap, few, width):
    return [pltpu.VMEM((16 if is_dense(cap) else few, width), bf16), pltpu.VMEM((few, width), bf16)]


def gated(top, weight, at, cs):
    return (weight * top[at, cs].astype(f32)).astype(bf16)


def compact(cap, h2, top, posrow, weight, xc, gc):
    def block(i):
        at, to = rows_at(i, LANES), rows_at(i, cap)
        w = weight(at)
        choose = None if is_dense(cap) else chosen(posrow, i, cap)
        for start, size in pieces(h2.shape[1], 512):
            cs = slice(start, start + size)
            if is_dense(cap):
                gc[at, cs] = gated(top, w, at, cs)
            else:
                xc[to, cs] = nn(choose, h2[at, cs]).astype(bf16)
                gc[to, cs] = nn(choose, gated(top, w, at, cs)).astype(bf16)

    loop(h2.shape[0] // LANES, block)


def stage_rows(hidden):
    return max(r for r in range(16, 177, 16) if hidden % r == 0)


class Masters:
    def __init__(self, gate_up, down, wg, wu, wd, stage, low, sems, out_sems):
        part = stage.shape[1]
        self.jobs = [
            (src.at[pl.ds(n * part, part)], dst.at[pl.ds(n * part, part)])
            for n in range(down.shape[0] // part)
            for src, dst in ((gate_up.at[:, 0, :], wg), (gate_up.at[:, 1, :], wu), (down, wd))
        ]
        self.stage, self.low, self.sems, self.out_sems = stage, low, sems, out_sems

    def load(self, n):
        return pltpu.make_async_copy(self.jobs[n][0], self.stage.at[n % 2], self.sems.at[n % 2])

    def store(self, n):
        return pltpu.make_async_copy(self.low.at[n % 2], self.jobs[n][1], self.out_sems.at[n % 2])

    def run(self, first, last):
        for n in range(first, last):
            self.load(n).wait()
            if n >= 2:
                self.store(n - 2).wait()

            def cast(r, n=n):
                at = rows_at(r, 16)
                self.low[n % 2, at, :] = self.stage[n % 2, at, :].astype(bf16)

            loop(self.low.shape[1] // 16, cast)
            self.store(n).start()
            if n + 2 < len(self.jobs):
                self.load(n + 2).start()

    def finish(self):
        for n in range(max(len(self.jobs) - 2, 0), len(self.jobs)):
            self.store(n).wait()

    def step(self, i, first_step, steps):
        count = len(self.jobs)

        @pl.when(i == first_step - 1)
        def _():
            for n in range(min(2, count)):
                self.load(n).start()

        for k in range(steps):
            pl.when(i == first_step + k)(
                lambda k=k: self.run(count * k // steps, count * (k + 1) // steps)
            )
        pl.when(i == first_step + steps - 1)(self.finish)


def masters_scratch(hidden, width):
    part = stage_rows(hidden)
    D = pltpu.SemaphoreType.DMA
    return [pltpu.VMEM((2, part, width), f32), pltpu.VMEM((2, part, width), bf16), D((2,)), D((2,))]


def ffn_compute(cap, me, h2, top, router, meta, posrow, produced, dh2, side, aux, act, dgate, dup, wg, wu, wd, xc, gc):
    rows, width = h2.shape
    hidden = wd.shape[0]
    blocks = rows // LANES

    aux[...] = gate_columns(nn(h2[...], router[...]), meta[:, 4:5], meta[:, 5:6], me[0])
    compact(cap, h2, top, posrow, lambda at: aux[at, 0:1], xc, gc)
    xs = h2 if is_dense(cap) else xc

    for start, size in pieces(hidden, 256):
        fs = slice(start, start + size)
        gate, up, dact = nt(xs[...], wg[fs, :]), nt(xs[...], wu[fs, :]), nt(gc[...], wd[fs, :])
        sigmoid = 1.0 / (1.0 + jnp.exp(-gate))
        silu = gate * sigmoid
        act[:, fs] = (silu * up).astype(bf16)
        dgate[:, fs] = (dact * up * sigmoid * (1.0 + gate * (1.0 - sigmoid))).astype(bf16)
        dup[:, fs] = (dact * silu).astype(bf16)

    if is_dense(cap):
        shares = jnp.zeros((rows, 1), f32)
        for start, size in pieces(width, 512):
            cs = slice(start, start + size)
            y = nn(act[...], wd[:, cs])
            shares = shares + jnp.sum(y * top[:, cs].astype(f32), axis=1, keepdims=True)
            produced[:, cs] = (aux[:, 0:1] * y).astype(bf16)
            dh2[:, cs] = (nn(dgate[...], wg[:, cs]) + nn(dup[...], wu[:, cs])).astype(bf16)
        side[...] = jnp.broadcast_to(aux[:, 1:2] * shares, (rows, LANES)).astype(bf16)
        return

    yc, bc = gc, xc

    def results(i):
        at = rows_at(i, 512)
        yc[:, at] = nn(act[...], wd[:, at]).astype(bf16)
        bc[:, at] = (nn(dgate[...], wg[:, at]) + nn(dup[...], wu[:, at])).astype(bf16)

    loop(width // 512, results)

    def scatter(i):
        at, of = rows_at(i, LANES), rows_at(i, cap)
        choose = chosen(posrow, i, cap)
        found = aux[at, :]
        share = jnp.zeros((LANES, 1), f32)
        for start, size in pieces(width, 512):
            cs = slice(start, start + size)
            y = tn(choose, yc[of, cs])
            share = share + jnp.sum(y * top[at, cs].astype(f32), axis=1, keepdims=True)
            produced[at, cs] = (found[:, 0:1] * y).astype(bf16)
            dh2[at, cs] = tn(choose, bc[of, cs]).astype(bf16)
        side[at, :] = jnp.broadcast_to(found[:, 1:2] * share, (LANES, LANES)).astype(bf16)

    loop(blocks, scatter)


def ffn_kernel(cap, me, h2, top, router, meta, posrow, wg, wu, wd, produced, aux, act, dgate, dup, dh2, side, xc, gc):
    ffn_compute(cap, me, h2, top, router, meta, posrow, produced, dh2, side, aux, act, dgate, dup, wg, wu, wd, xc, gc)


def ffn_fused_kernel(dims, cap, me, h2, top, router, meta, posrow, wg, wu, wd, produced, aux, act, dgate, dup, out, xc, gc, *refs):
    i = pl.program_id(0)
    place = Place(dims)
    sums = Scatter(dims, place, out, refs)

    pl.when(i == 0)(place.greet)

    @pl.when(i < sums.tiles)
    def _():
        tile, side = sums.tile.at[i % 2], sums.tile.at[i % 2, :, pl.ds(h2.shape[1], LANES)]
        ffn_compute(cap, me, h2, top, router, meta, posrow, produced, tile, side, aux, act, dgate, dup, wg, wu, wd, xc, gc)

    pl.when(i == 0)(place.greeted)
    sums.run(i)


def ffn(dims, cid, me, h2, top, router, meta, posrow, wg, wu, wd, cap):
    total, width = h2.shape
    hidden = wd.shape[0]
    tile = posrow.shape[1] * LANES
    few = tile if is_dense(cap) else tile // LANES * cap
    tiles = total // tile
    at = (lambda i: tile_group(i, dims)) if dims else (lambda i: i)
    row = lambda w: pl.BlockSpec((tile, w), lambda i: (at(i), 0))
    some = pl.BlockSpec((few, hidden), lambda i: (at(i), 0))
    own = total // (dims[0] * dims[1] * dims[2] * 2) if dims else 0
    wide = width + LANES
    if dims:
        kernel = functools.partial(ffn_fused_kernel, dims, cap)
        last_spec, last_shape = [whole_block((own, wide))], [jax.ShapeDtypeStruct((own, wide), f32)]
        params = dict(collective_id=cid, has_side_effects=True)
    else:
        kernel = functools.partial(ffn_kernel, cap)
        last_spec = [row(width), row(LANES)]
        last_shape = [jax.ShapeDtypeStruct((total, w), bf16) for w in (width, LANES)]
        params = {}
    return pl.pallas_call(
        kernel,
        grid=(tiles + 2 + dims[0] if dims else tiles,),
        in_specs=[
            pl.BlockSpec(memory_space=pltpu.SMEM), row(width), row(width), whole_block(router.shape), row(8),
            pl.BlockSpec((1,) + posrow.shape[1:], lambda i: (at(i), 0, 0)), once(wg.shape), once(wu.shape), once(wd.shape),
        ],
        out_specs=[row(width), row(LANES), some, some, some] + last_spec,
        out_shape=[
            jax.ShapeDtypeStruct((total, width), bf16),
            jax.ShapeDtypeStruct((total, LANES), f32),
        ] + [jax.ShapeDtypeStruct((tiles * few, hidden), bf16)] * 3 + last_shape,
        scratch_shapes=chosen_scratch(cap, few, width)
        + (scatter_scratch(dims, own, wide) if dims else []),
        compiler_params=pltpu.CompilerParams(vmem_limit_bytes=63 * MB, **params),
    )(me, h2, top, router, meta, posrow, wg, wu, wd)


def ffn_weights_compute(cap, first, h2, top, aux, posrow, act, dgate, dup, sg, su, sd, xc, gc):
    width = h2.shape[1]
    hidden = sd.shape[0]

    @pl.when(first)
    def _():
        for s in (sg, su, sd):

            def clear(i, s=s):
                s[rows_at(i, 32), :] = jnp.zeros((32, width), f32)

            loop(hidden // 32, clear)

    compact(cap, h2, top, posrow, lambda at: aux[at, 0:1], xc, gc)
    xs = h2 if is_dense(cap) else xc
    for start, size in pieces(hidden, 256):
        fs = slice(start, start + size)

        def grads(i, fs=fs):
            at = rows_at(i, 1024)
            sd[fs, at] += tn(act[:, fs], gc[:, at])
            sg[fs, at] += tn(dgate[:, fs], xs[:, at])
            su[fs, at] += tn(dup[:, fs], xs[:, at])

        loop(width // 1024, grads)


def ffn_weights_out(gate_up_grad, down_grad, sg, su, sd, sems):
    pairs = [(sg, gate_up_grad.at[:, 0, :]), (su, gate_up_grad.at[:, 1, :]), (sd, down_grad)]
    return [pltpu.make_async_copy(a, b, sems.at[i]) for i, (a, b) in enumerate(pairs)]


def ffn_weights_kernel(cap, h2, top, aux, posrow, act, dgate, dup, gate_up_grad, down_grad, sg, su, sd, xc, gc, sems):
    i = pl.program_id(0)
    ffn_weights_compute(cap, i == 0, h2, top, aux, posrow, act, dgate, dup, sg, su, sd, xc, gc)

    @pl.when(i == pl.num_programs(0) - 1)
    def _():
        copies = ffn_weights_out(gate_up_grad, down_grad, sg, su, sd, sems)
        for c in copies:
            c.start()
        for c in copies:
            c.wait()


class GradExchange:
    def __init__(self, dims, place, q_src, kv_src, q_out, kv_out, other_out, own, landed, along, refs):
        groups = dims[0] * dims[1]
        qs, qr, ql, ks, kr, kl, self.ls, self.ss, self.sr = refs
        self.place, self.kv_src, self.kv_out, self.other_out = place, kv_src, kv_out, other_out
        self.own, self.landed, self.along = own, landed, along
        self.query = Exchange(groups, q_src, q_out, qs, qr, ql)
        self.kv = Exchange(groups, own.at[place.y], kv_out, ks, kr, kl)

    def load(self):
        return pltpu.make_async_copy(self.kv_src.at[self.place.c], self.own, self.ls)

    def c_core(self):
        p = self.place
        return remote(self.kv_src.at[1 - p.c], self.landed, self.ss.at[0], self.sr.at[0], p.core())

    def c_y(self):
        p = self.place
        return remote(self.own.at[1 - p.y], self.along, self.ss.at[1], self.sr.at[1], p.along_y())

    def c_last(self):
        return remote(self.kv_out, self.other_out, self.ss.at[2], self.sr.at[2], self.place.core())

    def add(self, into, other):
        groups, rows, _ = into.shape

        def step(n):
            at = rows_at(n % (rows // 64), 64)
            g = n // (rows // 64)
            into[g, at, :] = (into[g, at, :].astype(f32) + other[g, at, :].astype(f32)).astype(bf16)

        loop(groups * (rows // 64), step)

    def step(self, i, last):
        @pl.when(i == 0)
        def _():
            self.c_core().start()
            self.load().start()
            self.query.start()

        @pl.when(i == 1)
        def _():
            self.load().wait()
            self.c_core().wait_recv()
            for n in range(2):
                self.add(self.own.at[n], self.landed.at[n])
            self.c_y().start()

        @pl.when(i == 3)
        def _():
            self.c_y().wait_recv()
            self.add(self.own.at[self.place.y], self.along)
            self.kv.start()

        @pl.when(i == 7)
        def _():
            self.kv.wait_came()
            self.c_last().start()

        @pl.when(i == last)
        def _():
            self.query.wait_came()
            self.c_last().wait_recv()
            for c in (self.c_core(), self.c_y(), self.c_last()):
                c.wait_send()
            self.query.wait_sent()
            self.kv.wait_sent()


def grad_exchange_scratch(groups, cw):
    D = pltpu.SemaphoreType.DMA
    V = lambda *s: pltpu.VMEM(s + (groups, cw, LANES), bf16)
    return [V(2), V(2), V()], exchange_scratch(groups) * 2 + [D, D((3,)), D((3,))]


def ffn_weights_fused(dims, cap, h2, top, aux, posrow, act, dgate, dup, extra, produced, q_src, kv_src, gate_up_grad, down_grad, out, q_out, kv_out, other_out, sg, su, sd, xc, gc, sems, load, own, landed, along, *refs):
    i = pl.program_id(0)
    place = Place(dims)
    sums = Scatter(dims, place, out, refs[:SCATTER_REFS])
    grads = GradExchange(dims, place, q_src, kv_src, q_out, kv_out, other_out, own, landed, along, refs[SCATTER_REFS:])
    rows, width = h2.shape
    copies = ffn_weights_out(gate_up_grad, down_grad, sg, su, sd, sems)

    @pl.when(i == 0)
    def _():
        place.greet_plane()
        place.greeted_plane()

    grads.step(i, sums.steps - 1)

    @pl.when(i < sums.tiles)
    def _():
        tile = sums.tile.at[i % 2]
        fetch = pltpu.make_async_copy(produced.at[rows_at(tile_group(i, dims), rows)], tile.at[:, pl.ds(0, width)], load)
        fetch.start()
        tile[:, width:] = extra[...]
        ffn_weights_compute(cap, i == 0, h2, top, aux, posrow, act, dgate, dup, sg, su, sd, xc, gc)
        fetch.wait()

    @pl.when(i == sums.tiles)
    def _():
        for c in copies:
            c.start()

    sums.run(i)

    @pl.when(i == sums.steps - 1)
    def _():
        for c in copies:
            c.wait()


def ffn_weights(dims, cid, h2, top, aux, posrow, act, dgate, dup, extra, produced, q_src, kv_src, cap):
    total, width = h2.shape
    hidden = act.shape[1]
    tile = posrow.shape[1] * LANES
    few = tile if is_dense(cap) else tile // LANES * cap
    tiles = total // tile
    at = (lambda i: tile_group(i, dims)) if dims else (lambda i: i)
    row = lambda w: pl.BlockSpec((tile, w), lambda i: (at(i), 0))
    some = pl.BlockSpec((few, hidden), lambda i: (at(i), 0))
    hbm = pl.BlockSpec(memory_space=pl.ANY)
    V = pltpu.VMEM
    scratch = [V((hidden, width), f32)] * 3 + chosen_scratch(cap, few, width) + [pltpu.SemaphoreType.DMA((3,))]
    out_specs = [hbm, hbm]
    out_shape = [jax.ShapeDtypeStruct((hidden, 2, width), f32), jax.ShapeDtypeStruct((hidden, width), f32)]
    in_specs = [
        row(width), row(width), row(LANES), pl.BlockSpec((1,) + posrow.shape[1:], lambda i: (at(i), 0, 0)), some, some, some,
    ]
    operands = [h2, top, aux, posrow, act, dgate, dup]
    if dims:
        own = tile // 4
        kernel = functools.partial(ffn_weights_fused, dims, cap)
        wide = width + LANES
        operands, in_specs = operands + [extra, produced, q_src, kv_src], in_specs + [row(LANES), hbm, hbm, hbm]
        groups, cw = q_src.shape[:2]
        out_specs = out_specs + [once((own, wide)), hbm, hbm, hbm]
        out_shape = out_shape + [jax.ShapeDtypeStruct((own, wide), f32), jax.ShapeDtypeStruct(q_src.shape, bf16)]
        out_shape = out_shape + [jax.ShapeDtypeStruct((groups, cw, LANES), bf16)] * 2
        buffers, marks = grad_exchange_scratch(groups, cw)
        scratch = scratch + [pltpu.SemaphoreType.DMA] + buffers + scatter_scratch(dims, own, wide) + marks
        params = dict(collective_id=cid, has_side_effects=True)
    else:
        kernel, params = functools.partial(ffn_weights_kernel, cap), {}
    return pl.pallas_call(
        kernel,
        grid=(tiles + 2 + dims[0] if dims else tiles,),
        in_specs=in_specs,
        out_specs=out_specs,
        out_shape=out_shape,
        scratch_shapes=scratch,
        compiler_params=pltpu.CompilerParams(vmem_limit_bytes=63 * MB, **params),
    )(*operands)


class Exchange:
    def __init__(self, groups, src, dst, sent, came, local):
        self.groups, self.src, self.dst, self.sent, self.came, self.local = groups, src, dst, sent, came, local
        self.gi, self.ei = lax.axis_index("grp"), lax.axis_index("exp")

    def peers(self):
        return [((self.gi + r) % self.groups, self.ei) for r in range(1, self.groups)]

    def copy(self, r, arriving=False):
        to, of = (self.gi + r) % self.groups, (self.gi + self.groups - r) % self.groups
        return pltpu.make_async_remote_copy(
            src_ref=self.src.at[to], dst_ref=self.dst.at[of if arriving else self.gi],
            send_sem=self.sent.at[r], recv_sem=self.came.at[r], device_id=(to, self.ei), device_id_type=MESH,
        )

    def own(self):
        return pltpu.make_async_copy(self.src.at[self.gi], self.dst.at[self.gi], self.local)

    def start(self):
        self.own().start()
        for r in range(1, self.groups):
            self.copy(r).start()

    def wait_came(self):
        self.own().wait()
        for r in range(1, self.groups):
            self.copy(r, True).wait_recv()

    def wait_sent(self):
        for r in range(1, self.groups):
            self.copy(r).wait_send()


def exchange_scratch(groups):
    D = pltpu.SemaphoreType.DMA
    return [D((groups,)), D((groups,)), D]


def ag_kernel(dims, halves, shared_rows, *refs):
    if shared_rows:
        src, ex_src, out, ex_out, shared, local_sem, zs, zr, xs, xr, ys, yr, cs, cr, exs, exr, exl, shs, shr, shl = refs
        ex = Exchange(dims[0] * dims[1], ex_src, ex_out, exs, exr, exl)
    else:
        src, out, local_sem, zs, zr, xs, xr, ys, yr, cs, cr = refs
        ex = None
    nz, nx, ny = dims
    gi = lax.axis_index("grp"); ei = lax.axis_index("exp")
    z, x = gi // nx, gi % nx
    y, c = ei // 2, ei % 2
    ne = ny * 2
    rows = src.shape[0]
    part = rows // halves
    def dev(z_, x_, y_, c_):
        return (z_ * nx + x_, y_ * 2 + c_)
    def slot(z_, x_, y_, c_):
        return (z_ * nx + x_) * ne + y_ * 2 + c_
    barrier = pltpu.get_barrier_semaphore()
    def sig(d):
        pl.semaphore_signal(barrier, inc=1, device_id=d, device_id_type=MESH)
    sig(dev(z, x, 1 - y, c))
    sig(dev(z, x, y, 1 - c))
    if ex is None:
        sig(dev(z, 1 - x, y, c))
        pl.when(z > 0)(lambda: sig(dev(z - 1, x, y, c)))
        pl.when(z < nz - 1)(lambda: sig(dev(z + 1, x, y, c)))
        pl.semaphore_wait(barrier, 3 + (z > 0).astype(jnp.int32) + (z < nz - 1).astype(jnp.int32))
    else:
        for peer in ex.peers():
            sig(peer)
        pl.semaphore_wait(barrier, 2 + len(ex.peers()))
    own = pltpu.make_async_copy(src, out.at[slot(z, x, y, c)], local_sem)
    own.start()
    span = 2 * nz - 1
    def piece(sl, h):
        return out.at[sl, pl.ds(h * part, part)]
    def copy(sl, h, is_own, ssem, rsem, d):
        s = src.at[pl.ds(h * part, part)] if is_own else piece(sl, h)
        return pltpu.make_async_remote_copy(src_ref=s, dst_ref=piece(sl, h), send_sem=ssem, recv_sem=rsem, device_id=d, device_id_type=MESH)
    def zcopy(h, delta, direction, arriving):
        zz = z - delta * direction
        k = (h * 2 + (0 if direction > 0 else 1)) * nz
        if arriving:
            return copy(slot(zz, x, y, c), h, False, zs.at[k + delta], zr.at[k + delta], dev(z, x, y, c) if False else dev(z, x, y, 1 - c))
        return copy(slot(zz, x, y, c), h, delta == 0, zs.at[k + delta + 1], zr.at[k + delta + 1], dev(z + direction, x, y, c))
    def valid(delta):
        zz = z + delta
        return (zz >= 0) & (zz < nz)
    def when(cond, f):
        pl.when(cond)(f)
    sends = []
    def order(h):
        return ("x", "y") if h % 2 == 0 else ("y", "x")
    def first(h, delta):
        a = order(h)[0]
        sems = (xs, xr) if a == "x" else (ys, yr)
        k = h * 2 * span + delta + nz - 1
        d = dev(z, 1 - x, y, c) if a == "x" else dev(z, x, 1 - y, c)
        return copy(slot(z + delta, x, y, c), h, delta == 0, sems[0].at[k], sems[1].at[k], d), (
            lambda: copy(slot(z + delta, 1 - x if a == "x" else x, 1 - y if a == "y" else y, c), h, False, sems[0].at[k], sems[1].at[k], d))
    def second(h, delta, rel):
        a0, a = order(h)
        sems = (xs, xr) if a == "x" else (ys, yr)
        k = h * 2 * span + (rel * span) + delta + nz - 1
        d = dev(z, 1 - x, y, c) if a == "x" else dev(z, x, 1 - y, c)
        x0 = (1 - x if rel else x) if a0 == "x" else x
        y0 = (1 - y if rel else y) if a0 == "y" else y
        snd = copy(slot(z + delta, x0, y0, c), h, delta == 0 and rel == 0, sems[0].at[k], sems[1].at[k], d)
        x1 = 1 - x if a == "x" else x0
        y1 = 1 - y if a == "y" else y0
        rcv = copy(slot(z + delta, x1, y1, c), h, False, sems[0].at[k], sems[1].at[k], d)
        return snd, rcv
    def core(h, delta, rx, ry):
        k = h * 4 * span + (rx * 2 + ry) * span + delta + nz - 1
        d = dev(z, x, y, 1 - c)
        xx = 1 - x if rx else x
        yy = 1 - y if ry else y
        return (copy(slot(z + delta, xx, yy, c), h, delta == 0 and not rx and not ry, cs.at[k], cr.at[k], d),
                copy(slot(z + delta, xx, yy, 1 - c), h, False, cs.at[k], cr.at[k], d))
    hs = range(halves)
    def have_z(delta):
        for h in hs:
            if delta <= 0:
                when(z < nz - 1, lambda h=h: zcopy(h, -delta, 1, False).start())
            if delta >= 0:
                when(z > 0, lambda h=h: zcopy(h, delta, -1, False).start())
            first(h, delta)[0].start()
            second(h, delta, 0)[0].start()
            core(h, delta, 0, 0)[0].start()
    have_z(0)
    def share(n):
        part = ex_out.at[:, pl.ds(ex_out.shape[1] - shared_rows, shared_rows)]
        number = (1 - y if n == 2 else y) * 2 + c
        return pltpu.make_async_remote_copy(
            src_ref=shared.at[:, number] if n == 2 else part, dst_ref=shared.at[:, number],
            send_sem=shs.at[n], recv_sem=shr.at[n],
            device_id=dev(z, x, 1 - y, c) if n == 0 else dev(z, x, y, 1 - c), device_id_type=MESH,
        )
    def share_own():
        part = ex_out.at[:, pl.ds(ex_out.shape[1] - shared_rows, shared_rows)]
        return pltpu.make_async_copy(part, shared.at[:, y * 2 + c], shl)
    def shared_came(n):
        number = ((1 - y) * 2 + c, y * 2 + 1 - c, (1 - y) * 2 + 1 - c)[n]
        return pltpu.make_async_remote_copy(
            src_ref=shared.at[:, number], dst_ref=shared.at[:, number], send_sem=shs.at[n], recv_sem=shr.at[n],
            device_id=dev(z, x, y, 1 - c), device_id_type=MESH,
        )
    if ex is not None:
        ex.start()
    def get_z(delta):
        def f():
            for h in hs:
                zcopy(h, abs(delta), -1 if delta > 0 else 1, True).wait_recv()
            have_z(delta)
        when(valid(delta), f)
    def get_first(delta):
        def f():
            for h in hs:
                first(h, delta)[1]().wait_recv()
                second(h, delta, 1)[0].start()
                rx = 1 if order(h)[0] == "x" else 0
                core(h, delta, rx, 1 - rx)[0].start()
        when(valid(delta), f)
    def get_second(delta):
        def f():
            for h in hs:
                for rel in range(2):
                    second(h, delta, rel)[1].wait_recv()
                    a0, a = order(h)
                    rx = 1 if a == "x" else (rel if a0 == "x" else 0)
                    ry = 1 if a == "y" else (rel if a0 == "y" else 0)
                    core(h, delta, rx, ry)[0].start()
        when(valid(delta), f)
    for step in range(nz + 2):
        for dist, fn in ((step, get_z), (step - 1, get_first), (step - 2, get_second)):
            if 0 <= dist < nz:
                if dist == 0:
                    if fn is not get_z: fn(0)
                else:
                    fn(-dist); fn(dist)
        if ex is not None and step == nz - 1:
            ex.wait_came()
            share_own().start()
            share(0).start()
            share(1).start()
        if ex is not None and step == nz + 1:
            shared_came(0).wait_recv()
            share(2).start()
    own.wait()
    if ex is not None:
        shared_came(1).wait_recv()
        shared_came(2).wait_recv()
        share_own().wait()
        for n in range(3):
            share(n).wait_send()
        ex.wait_sent()
    for delta in range(-(nz - 1), nz):
        def f(delta=delta):
            for h in hs:
                for rx in range(2):
                    for ry in range(2):
                        a, b = core(h, delta, rx, ry)
                        b.wait_recv(); a.wait_send()
                first(h, delta)[0].wait_send()
                for rel in range(2):
                    second(h, delta, rel)[0].wait_send()
                if delta <= 0:
                    when(z < nz - 1, lambda h=h: zcopy(h, -delta, 1, False).wait_send())
                if delta >= 0:
                    when(z > 0, lambda h=h: zcopy(h, delta, -1, False).wait_send())
        when(valid(delta), f)

def gather_kernel(v, dims, cid, exchanged=None, shared_rows=0, halves=2):
    nz, nx, ny = dims
    n = nz * nx * ny * 2
    span = 2 * nz - 1
    D = pltpu.SemaphoreType.DMA
    hbm = pl.BlockSpec(memory_space=pl.ANY)
    operands, out_shape, more = [v], [jax.ShapeDtypeStruct((n,) + v.shape, v.dtype)], []
    if shared_rows:
        e = exchanged
        operands += [e]
        out_shape += [jax.ShapeDtypeStruct(e.shape, e.dtype), jax.ShapeDtypeStruct((e.shape[0], ny * 2, shared_rows, e.shape[2]), e.dtype)]
        more = exchange_scratch(nz * nx) + [D((3,)), D((3,)), D]
    out = pl.pallas_call(
        functools.partial(ag_kernel, dims, halves, shared_rows),
        out_shape=out_shape,
        in_specs=[hbm] * len(operands),
        out_specs=[hbm] * len(out_shape),
        scratch_shapes=[D] + [D((halves * 2 * (nz + 1),))] * 2 + [D((halves * 2 * span,))] * 4 + [D((halves * 4 * span,))] * 2 + more,
        compiler_params=pltpu.CompilerParams(collective_id=cid, has_side_effects=True),
    )(*operands)
    return out if shared_rows else out[0]


def target_order(nz):
    low, high, order = 0, nz - 1, []
    while low <= high:
        order += [low] if low == high else [low, high]
        low, high = low + 1, high - 1
    return order


def tile_group(i, dims):
    nz, nx, _ = dims
    i = jnp.minimum(i, nz * nx - 1)
    j = i // nx
    t = jnp.where(j % 2 == 0, j // 2, nz - 1 - j // 2)
    return t * nx + i % nx


class Place:
    def __init__(self, dims):
        self.nz, self.nx, self.ny = dims
        gi, ei = lax.axis_index("grp"), lax.axis_index("exp")
        self.z, self.x = gi // self.nx, gi % self.nx
        self.y, self.c = ei // 2, ei % 2

    def device(self, z, x, y, c):
        return (z * self.nx + x, y * 2 + c)

    def core(self):
        return self.device(self.z, self.x, self.y, 1 - self.c)

    def along_x(self):
        return self.device(self.z, 1 - self.x, self.y, self.c)

    def along_y(self):
        return self.device(self.z, self.x, 1 - self.y, self.c)

    def along_z(self, by):
        return self.device(self.z + by, self.x, self.y, self.c)

    def greet(self):
        barrier = pltpu.get_barrier_semaphore()

        def signal(device):
            pl.semaphore_signal(barrier, inc=1, device_id=device, device_id_type=MESH)

        signal(self.along_x())
        signal(self.along_y())
        signal(self.core())
        pl.when(self.z > 0)(lambda: signal(self.along_z(-1)))
        pl.when(self.z < self.nz - 1)(lambda: signal(self.along_z(1)))

    def greet_plane(self):
        barrier = pltpu.get_barrier_semaphore()
        groups = self.nz * self.nx
        gi, ei = lax.axis_index("grp"), lax.axis_index("exp")
        peers = [((gi + r) % groups, ei) for r in range(1, groups)] + [self.along_y(), self.core()]
        for device in peers:
            pl.semaphore_signal(barrier, inc=1, device_id=device, device_id_type=MESH)

    def greeted_plane(self):
        pl.semaphore_wait(pltpu.get_barrier_semaphore(), self.nz * self.nx + 1)

    def greeted(self):
        inner = (self.z > 0).astype(jnp.int32) + (self.z < self.nz - 1).astype(jnp.int32)
        pl.semaphore_wait(pltpu.get_barrier_semaphore(), 3 + inner)


def remote(src, dst, sent, came, device):
    return pltpu.make_async_remote_copy(
        src_ref=src, dst_ref=dst, send_sem=sent, recv_sem=came, device_id=device, device_id_type=MESH
    )


def scatter_scratch(dims, rows, width):
    nz, nx, _ = dims
    tiles, half = nz * nx, rows // 2
    D, V = pltpu.SemaphoreType.DMA, lambda *s: pltpu.VMEM(s, bf16)
    return [
        V(2, 4 * rows, width),
        V(2, 2, rows, width),
        V(tiles, 2, rows, width),
        V(tiles, half, width), V(nz, 2, half, width),
        V(nz, half, width), V(nz, half, width),
        V(nz + 1, rows, width),
        D((tiles * 2,)), D((tiles * 2,)), D((tiles,)), D((tiles,)), D((nz * 2,)), D((nz * 2,)),
        D((nz,)), D((nz,)), D((nz,)), D((nz,)), D((nz * 2,)), D((nz * 2 + 2,)),
    ]


SCATTER_REFS = 20


class Scatter:
    def __init__(self, dims, place, out, refs):
        self.dims, self.place, self.out = dims, place, out
        (self.tile, self.crv, self.acc, self.ya, self.xb, self.xa, self.yb, self.zv,
         self.cs, self.cr, self.yas, self.yar, self.xbs, self.xbr,
         self.xas, self.xar, self.ybs, self.ybr, self.zs, self.zr) = refs
        self.rows = out.shape[0]
        self.half = self.rows // 2
        self.order = target_order(dims[0])
        self.tiles = dims[0] * dims[1]
        self.steps = self.tiles + 2 + dims[0]

    def add(self, into, *others):
        def step(r, _):
            at = rows_at(r, 16)
            total = others[0][at, :].astype(f32)
            for o in others[1:]:
                total = total + o[at, :].astype(f32)
            into[at, :] = total.astype(into.dtype)
            return 0

        lax.fori_loop(0, into.shape[0] // 16, step, 0)

    def low(self, k, q):
        return self.acc.at[k, q, pl.ds(0, self.half)]

    def high(self, k, q):
        return self.acc.at[k, q, pl.ds(self.half, self.half)]

    def shard(self, k, q, c):
        return self.tile.at[k % 2, rows_at(q * 2 + c, self.rows)]

    def c_core(self, k, q):
        p, s = self.place, k * 2 + q
        return remote(self.shard(k, q, 1 - p.c), self.crv.at[k % 2, q], self.cs.at[s], self.cr.at[s], p.core())

    def c_ya(self, k):
        p = self.place
        return remote(self.low(k, 1 - p.y), self.ya.at[k], self.yas.at[k], self.yar.at[k], p.along_y())

    def c_xb(self, k, q):
        p, j = self.place, k // 2
        s = j * 2 + q
        return remote(self.high(k, q), self.xb.at[j, q], self.xbs.at[s], self.xbr.at[s], p.along_x())

    def c_xa(self, k):
        p, j = self.place, k // 2
        return remote(self.low(k, p.y), self.xa.at[j], self.xas.at[j], self.xar.at[j], p.along_x())

    def c_yb(self, k):
        p, j = self.place, k // 2
        return remote(self.high(k, 1 - p.y), self.yb.at[j], self.ybs.at[j], self.ybr.at[j], p.along_y())

    def own_half(self, k, h):
        return self.acc.at[k, self.place.y, pl.ds(h * self.half, self.half)]

    def z_half(self, slot, h):
        return self.zv.at[slot, pl.ds(h * self.half, self.half)]

    def c_z(self, k, way, h):
        p, t = self.place, self.order[k // 2]
        slot = t if way > 0 else jnp.where(p.z - 1 == t, self.dims[0], t)
        return remote(self.own_half(k, h), self.z_half(slot, h), self.zs.at[t * 2 + h], self.zr.at[slot * 2 + h], p.along_z(way))

    def z_wait(self, k, slot, h):
        remote(self.own_half(k, h), self.z_half(slot, h), self.zs.at[h], self.zr.at[slot * 2 + h], self.place.core()).wait_recv()

    def phase_s(self, k):
        for q in range(2):
            self.c_core(k, q).start()

    def phase_b(self, k):
        p = self.place
        away = p.x != k % 2
        for q in (1 - p.y, p.y):
            self.c_core(k, q).wait_recv()
            self.add(self.acc.at[k, q], self.shard(k, q, p.c), self.crv.at[k % 2, q])
            if q is not p.y:
                self.c_ya(k).start()
            pl.when(away)(lambda q=q: self.c_xb(k, q).start())
        for q in range(2):
            self.c_core(k, q).wait_send()

    def phase_c(self, k):
        p, j = self.place, k // 2

        def give():
            self.c_ya(k).wait_recv()
            self.add(self.low(k, p.y), self.low(k, p.y), self.ya.at[k])
            self.c_xa(k).start()

        def keep():
            self.c_xb(k, 1 - p.y).wait_recv()
            self.add(self.high(k, 1 - p.y), self.high(k, 1 - p.y), self.xb.at[j, 1 - p.y])
            self.c_yb(k).start()

        pl.when(p.x != k % 2)(give)
        pl.when(p.x == k % 2)(keep)

    def phase_d(self, k):
        p, j, t, nz = self.place, k // 2, self.order[k // 2], self.dims[0]

        def ends(h):
            if t > 0:
                pl.when(p.z == 0)(lambda: self.c_z(k, 1, h).start())
            if t < nz - 1:
                pl.when(p.z == nz - 1)(lambda: self.c_z(k, -1, h).start())

        def keep():
            self.c_ya(k).wait_recv()
            self.c_xa(k).wait_recv()
            self.add(self.low(k, p.y), self.low(k, p.y), self.ya.at[k], self.xa.at[j])
            ends(0)
            self.c_xb(k, p.y).wait_recv()
            self.c_yb(k).wait_recv()
            self.add(self.high(k, p.y), self.high(k, p.y), self.xb.at[j, p.y], self.yb.at[j])
            ends(1)

        pl.when(p.x == k % 2)(keep)

    def phase_e(self, k, hop):
        p, t, nz = self.place, self.order[k // 2], self.dims[0]
        mine = p.x == k % 2

        def pass_on(way):
            def run():
                for h in range(2):
                    self.z_wait(k, t, h)
                    self.add(self.own_half(k, h), self.own_half(k, h), self.z_half(t, h))
                    self.c_z(k, way, h).start()

            return run

        if hop < t:
            pl.when(mine & (p.z == hop))(pass_on(1))
        if nz - 1 - hop > t:
            pl.when(mine & (p.z == nz - 1 - hop))(pass_on(-1))
        if hop == max(t, nz - 1 - t):

            def last():
                for h in range(2):
                    others = [self.own_half(k, h)]
                    for there, slot in ((t > 0, t), (t < nz - 1, nz)):
                        if there:
                            self.z_wait(k, slot, h)
                            others.append(self.z_half(slot, h))
                    self.add(self.out.at[pl.ds(h * self.half, self.half)], *others)

            pl.when(mine & (p.z == t))(last)

    def drain(self):
        p = self.place
        for k in range(self.tiles):
            self.c_ya(k).wait_send()

            def give(k=k):
                self.c_xa(k).wait_send()
                for q in range(2):
                    self.c_xb(k, q).wait_send()

            def keep(k=k):
                self.c_yb(k).wait_send()

                def along(k=k):
                    for h in range(2):
                        self.c_z(k, 1, h).wait_send()

                pl.when(p.z != self.order[k // 2])(along)

            pl.when(p.x != k % 2)(give)
            pl.when(p.x == k % 2)(keep)

    def run(self, i):
        for step in range(self.steps):

            def phases(step=step):
                for lag, phase in ((1, self.phase_b), (0, self.phase_s), (2, self.phase_c), (3, self.phase_d)):
                    if 0 <= step - lag < self.tiles:
                        phase(step - lag)
                for h in range(1, self.dims[0]):
                    if 0 <= step - 3 - h < self.tiles:
                        self.phase_e(step - 3 - h, h)
                if step == self.steps - 1:
                    self.drain()

            pl.when(i == step)(phases)


def scatter_kernel_body(dims, src, out, *refs):
    i = pl.program_id(0)
    place = Place(dims)
    s = Scatter(dims, place, out, refs)

    @pl.when(i == 0)
    def _():
        place.greet()
        place.greeted()

    @pl.when(i < s.tiles)
    def _():
        def copy(r):
            at = rows_at(r, 64)
            s.tile[i % 2, at, :] = src[at, :]
        loop(src.shape[0] // 64, copy)

    s.run(i)


def scatter_kernel(p, dims, cid):
    nz, nx, ny = dims
    n, rows, width = p.shape
    groups = nz * nx
    p = p.reshape(n * rows, width)
    return pl.pallas_call(
        functools.partial(scatter_kernel_body, dims),
        grid=(groups + 2 + nz,),
        in_specs=[pl.BlockSpec((4 * rows, width), lambda i: (tile_group(i, dims), 0))],
        out_specs=whole_block((rows, width)),
        out_shape=jax.ShapeDtypeStruct((rows, width), f32),
        scratch_shapes=scatter_scratch(dims, rows, width),
        compiler_params=pltpu.CompilerParams(collective_id=cid, has_side_effects=True, vmem_limit_bytes=60 * MB),
    )(p)


def layout(first, order, block):
    groups, blocks = order.shape
    rows = groups * blocks * block
    step = jnp.arange(block, dtype=jnp.int32)
    anchor = order[:, :, None] * block + step
    late = anchor >= first[:, :, None]
    place = anchor - jnp.where(late, first[:, :, None], 0)
    half = LANES // 2
    freq = jnp.exp(jnp.arange(half, dtype=f32) * (-2.0 * math.log(10000.0) / LANES))
    freq = jnp.concatenate([freq, freq])
    sign = jnp.where(jnp.arange(LANES) < half, -1.0, 1.0)
    inner = step.astype(f32)[:, None] * freq
    start = (order * block).astype(f32)[:, :, None, None] * freq
    moved = (order * block - first).astype(f32)[:, :, None, None] * freq
    chosen_cos = jnp.where(late[..., None], jnp.cos(moved), jnp.cos(start))
    chosen_sin = jnp.where(late[..., None], jnp.sin(moved), jnp.sin(start))
    cos = jnp.cos(inner) * chosen_cos - jnp.sin(inner) * chosen_sin
    sin = (jnp.sin(inner) * chosen_cos + jnp.cos(inner) * chosen_sin) * sign
    flat = lambda v: v.reshape(groups, blocks * block)
    return (flat(anchor), flat(place), cos.reshape(rows, LANES), sin.reshape(rows, LANES))


def logit_grad(route, gates, difference, experts):
    moved = gates[:, 0:1] * gates[:, 1:2] * difference
    names = jnp.arange(experts, dtype=jnp.int32)[None, :]
    return jnp.where(route[:, 0:1] == names, moved, 0.0) - jnp.where(
        route[:, 1:2] == names, moved, 0.0
    )


def norm_back(grad_hidden, normed, inverse, gain):
    grad_normed = grad_hidden * gain
    gain_grad = jnp.sum(grad_hidden * normed, axis=0)
    mean_term = jnp.mean(grad_normed * normed, axis=1, keepdims=True)
    return (inverse * (grad_normed - normed * mean_term), gain_grad)


def body(
    dims,
    layer_input,
    out_grad,
    doc_lengths,
    block_order,
    attn_route,
    ffn_route,
    norm_gains,
    kv_master,
    router_master,
    query_master,
    output_master,
    gate_up_master,
    down_master,
):
    own_rows, width = layer_input.shape
    members, groups = lax.axis_size("exp"), lax.axis_size("grp")
    member, group = lax.axis_index("exp"), lax.axis_index("grp")
    experts = members
    capacity = 3 * own_rows // experts
    group_rows = own_rows * members
    total = group_rows * groups
    devices = groups * members
    cw = width // groups
    depth = kv_master.shape[0]
    scale = 1.0 / math.sqrt(LANES)
    me = member.reshape(1).astype(jnp.int32)
    both = ("grp", "exp")

    def gather_all(v, cid):
        if dims is None:
            return lax.all_gather(kept(v), both, axis=0, tiled=True)
        return gather_kernel(v, dims, cid)

    def scatter_all(v, cid):
        v = v.reshape(devices, own_rows, v.shape[-1])
        if dims is None:
            return lax.psum_scatter(v, both, scatter_dimension=0, tiled=False).astype(f32)
        return scatter_kernel(v, dims, cid)

    def summed(parts):
        return jnp.concatenate([scatter_all(v, 0) for v in parts], axis=1) if dims is None else parts[0]

    blocks = block_order.shape[1]
    start_row = member * own_rows
    own_attn_route = lax.dynamic_slice_in_dim(attn_route, start_row, own_rows)
    own_ffn_route = lax.dynamic_slice_in_dim(ffn_route, start_row, own_rows)
    tall = lambda v: jnp.pad(v.astype(bf16), ((0, own_rows - v.shape[0]), (0, 0)))
    first_doc = doc_lengths[:, 0]
    small = jnp.concatenate(
        [
            tall(norm_gains),
            tall(router_master),
            own_attn_route.astype(bf16),
            own_ffn_route.astype(bf16),
            tall(jnp.concatenate([first_doc // 16, first_doc % 16, block_order[0]])[:, None]),
        ],
        axis=1,
    )
    at_route = 2 + 2 * experts
    small = jnp.pad(small, ((0, 0), (0, LANES - small.shape[1])))

    query_low = query_master[0].astype(bf16)
    kv_low = kv_master.astype(bf16).reshape(depth, 2, groups, cw).transpose(1, 0, 2, 3).reshape(2 * depth, groups, cw)
    query_rows = query_low.shape[0]
    pieces_out = jnp.concatenate([query_low.reshape(query_rows, groups, cw), kv_low], axis=0).transpose(1, 0, 2)
    if dims is None:
        tokens = gather_all(layer_input, 1).reshape(total, width)
        extra = gather_all(small, 2).reshape(total, LANES)
        pieces_in = lax.all_to_all(pieces_out, "grp", split_axis=0, concat_axis=0, tiled=True)
        kv_all = lax.all_gather(pieces_in[:, query_rows:], "exp", axis=1, tiled=False)
    else:
        sent = jnp.concatenate([layer_input, small], axis=1)
        tokens, pieces_in, kv_all = gather_kernel(sent, dims, 1, pieces_out, 2 * depth)
        tokens = tokens.reshape(total, width + LANES)
        tokens, late_grad = lax.optimization_barrier((tokens, out_grad))
        extra = tokens[:, width:]
    query_weight = pieces_in[:, :query_rows].reshape(width, cw)
    key_weight, value_weight = (kv_all[:, :, at : at + depth].reshape(width, cw) for at in (0, depth))

    output_weight = output_master[0].astype(bf16)

    tables = extra.reshape(devices, own_rows, LANES)[:, :depth, :at_route].reshape(width, at_route)
    gains = tables[:, :2].astype(f32)
    router = tables[:, 2:]
    router_float = router.astype(f32)
    wide = lambda v: jnp.pad(v, ((0, 0), (0, LANES - v.shape[1])))
    routes = extra[:, at_route : at_route + 4].astype(jnp.int32)
    column = extra.reshape(groups, group_rows, LANES)[:, : blocks + 2, at_route + 4].astype(jnp.int32)

    def where_rows_stand(column):
        first = column[:, 0:1] * 16 + column[:, 1:2]
        anchor, place, cos, sin = layout(first, column[:, 2:], own_rows // 2)
        meta = jnp.concatenate(
            [anchor.reshape(total, 1), (anchor - place).reshape(total, 1), routes, routes[:, :2]], axis=1
        )
        return cos, sin, meta, jnp.broadcast_to(anchor[:, None, :], (groups, 8, group_rows))

    cos, sin, meta, key_rows = where_rows_stand(column)
    gain_one, gain_two = gains[:, 0], gains[:, 1]
    w_all = jnp.concatenate([query_weight, key_weight, value_weight, wide(router[:, :experts])], axis=1)

    qkv, att, aux, wg, wu, wd, attn_sum = attn_forward(
        dims, 3, me, tokens, gain_one[None], w_all, output_weight, cos, sin, meta, key_rows,
        gate_up_master[0], down_master[0], groups, scale,
    )
    own = (group * members + member) * own_rows
    attn_gates = lax.dynamic_slice(aux, (own, 2), (own_rows, 2))
    inputs = layer_input.astype(f32)
    middle = inputs + summed([attn_sum])
    inverse_two = lax.rsqrt(jnp.mean(middle * middle, axis=1, keepdims=True) + epsilon)
    normed_two = middle * inverse_two
    hidden_two = (normed_two * gain_two).astype(bf16)
    if dims is None:
        late_grad, hidden_two = lax.optimization_barrier((out_grad, hidden_two))
    h2 = gather_all(hidden_two, 4).reshape(total, width)
    tops = lax.all_gather(late_grad, both, axis=0, tiled=True)

    if is_dense(capacity):
        position = jnp.zeros((devices, own_rows), jnp.int32)
    else:
        named = ((routes[:, 2] == member) | (routes[:, 3] == member)).reshape(devices, own_rows)
        position = jnp.where(named, jnp.cumsum(named.astype(jnp.int32), axis=1) - 1, -1)
    tile_blocks = 4
    position = position.reshape(devices // tile_blocks, tile_blocks, own_rows)
    produced, ffn_aux, act, dgate, dup, *dh2_parts = ffn(
        dims, 5, me, h2, tops, wide(router[:, experts:]), meta, position,
        wg, wu, wd, capacity,
    )
    if dims is None:
        gate_up_grad, down_grad = ffn_weights(
            dims, 0, h2, tops, ffn_aux, position, act, dgate, dup, None, None, None, None, capacity
        )
        gate_up_grad, dh2_parts, produced = lax.optimization_barrier((gate_up_grad, dh2_parts, produced))
        back = summed(dh2_parts)
        produced, back = lax.optimization_barrier((produced, back))
        ffn_sum = scatter_all(produced, 0)
        ffn_sum, back = lax.optimization_barrier((ffn_sum, back))
    else:
        back = summed(dh2_parts)
    ffn_gates = lax.dynamic_slice(ffn_aux, (own, 2), (own_rows, 2))
    top_grad = out_grad.astype(f32)
    ffn_logit_grad = logit_grad(own_ffn_route, ffn_gates, back[:, width : width + 1], experts)
    hidden_two_grad = back[:, :width] + jnp.einsum(
        "te,de->td", ffn_logit_grad, router_float[:, experts:], precision=highest
    )
    middle_part, gain_two_grad = norm_back(hidden_two_grad, normed_two, inverse_two, gain_two)
    middle_grad = top_grad + middle_part
    dmid = gather_all(middle_grad.astype(bf16), 6).reshape(total, width)

    if dims is None:
        again, dmid = lax.optimization_barrier((layer_input, dmid))
        tokens = gather_all(again, 9).reshape(total, width)
        column, dmid = lax.optimization_barrier((column, dmid))
        cos, sin, meta, key_rows = where_rows_stand(column)
    dw, do, *dh1_parts = attn_backward(
        dims, 8, dmid, tokens, gain_one[None], qkv, att, aux, cos, sin, meta, key_rows, w_all, output_weight, groups, scale
    )
    back = summed(dh1_parts)
    inverse_one = lax.rsqrt(jnp.mean(inputs * inputs, axis=1, keepdims=True) + epsilon)
    normed_one = inputs * inverse_one
    hidden_one = (normed_one * gain_one).astype(bf16)
    attn_logit_grad = logit_grad(own_attn_route, attn_gates, back[:, width : width + 1], experts)
    hidden_one_grad = back[:, :width] + jnp.einsum(
        "te,de->td", attn_logit_grad, router_float[:, :experts], precision=highest
    )
    input_part, gain_one_grad = norm_back(hidden_one_grad, normed_one, inverse_one, gain_one)
    input_grad = middle_grad + input_part
    route_grad = [
        jnp.einsum("td,te->de", a.astype(f32), b, precision=highest)
        for a, b in ((hidden_one, attn_logit_grad), (hidden_two, ffn_logit_grad))
    ]
    sums = jnp.concatenate(
        [gain_one_grad[:, None], gain_two_grad[:, None], route_grad[0], route_grad[1]], axis=1
    )

    if dims is None:
        sums = lax.psum_scatter(sums, both, scatter_dimension=0, tiled=True)
        kv_part = dw[cw:].reshape(2 * cw, groups, members, depth)
        kv_part = lax.psum_scatter(kv_part.astype(bf16), "exp", scatter_dimension=2, tiled=False)
        query_part = dw[:cw].astype(bf16).reshape(cw, groups, width // groups)
        pieces_out = jnp.concatenate(
            [query_part.transpose(1, 0, 2).reshape(groups, -1), kv_part.transpose(1, 0, 2).reshape(groups, -1)],
            axis=1,
        )
        pieces_in = lax.all_to_all(pieces_out, "grp", split_axis=0, concat_axis=0, tiled=True)
        cut = cw * (width // groups)
        query_part = pieces_in[:, :cut].reshape(width, width // groups)
        kv_part = pieces_in[:, cut:].reshape(groups, 2, cw, depth).transpose(1, 0, 2, 3)
    else:
        beside = jnp.pad(
            sums.astype(bf16).reshape(devices, depth, sums.shape[1]),
            ((0, 0), (0, own_rows - depth), (0, LANES - sums.shape[1])),
        ).reshape(total, LANES)
        low = dw.astype(bf16)
        query_part = low[:cw].reshape(cw, groups, width // groups).transpose(1, 0, 2)
        kv_part = low[cw:].reshape(2, cw, groups, members // 2, LANES).transpose(0, 3, 2, 1, 4)
        gate_up_grad, down_grad, ffn_sum, query_part, kv_own, kv_other = ffn_weights(
            dims, 7, h2, tops, ffn_aux, position, act, dgate, dup, beside, produced, query_part, kv_part, capacity
        )
        sums = ffn_sum[:depth, width : width + sums.shape[1]]
        ffn_sum = ffn_sum[:, :width]
        query_part = query_part.reshape(width, width // groups)
        core = member % 2
        kv_part = jnp.where(core == 0, jnp.stack([kv_own, kv_other]), jnp.stack([kv_other, kv_own]))
        kv_part = lax.dynamic_slice_in_dim(kv_part, core * depth, depth, axis=3)
    final = middle + ffn_sum
    query_grad = query_part.T.astype(f32)
    kv_grad = kv_part.reshape(2 * width, depth).T.astype(f32)
    return (
        final.astype(bf16),
        input_grad,
        sums[:, :2],
        kv_grad,
        sums[:, 2:],
        query_grad[None],
        do[None],
        gate_up_grad[None],
        down_grad[None],
    )


def solution(mesh):
    groups, members = mesh.shape["grp"], mesh.shape["exp"]
    dims = (groups // 2, 2, members // 2) if groups <= 8 and members == 4 else None
    in_specs = (
        P(("grp", "exp"), None),
        P(("grp", "exp"), None),
        P("grp", None),
        P("grp", None),
        P("grp", None),
        P("grp", None),
        P(("grp", "exp"), None),
        P(("grp", "exp"), None),
        P(("grp", "exp"), None),
        P("exp", "grp", None),
        P("exp", "grp", None),
        P("exp", "grp", None, None),
        P("exp", "grp", None),
    )
    out_specs = (
        P(("grp", "exp"), None),
        P(("grp", "exp"), None),
        P(("grp", "exp"), None),
        P(("grp", "exp"), None),
        P(("grp", "exp"), None),
        P("exp", "grp", None),
        P("exp", "grp", None),
        P("exp", "grp", None, None),
        P("exp", "grp", None),
    )
    return jax.shard_map(
        functools.partial(body, dims),
        mesh=mesh,
        in_specs=in_specs,
        out_specs=out_specs,
        check_vma=False,
    )
```
